32 devices in a mesh: dp: 8 (over y, x, core), tensor: 4 (over z).
Axes of the slice: x: 2, y: 2, z: 4, core: 2. Of those that a mesh axis runs over, the one named last changes fastest.
Arguments:
- activations: bfloat16 [6144, 8192], P('dp'), may hold values from -48 to 48
- cotangent: bfloat16 [6144, 1024], P('dp', 'tensor'), may hold values from -0.375 to 0.375
- sampled_rows: int32 [512], P('dp'), may hold values from 0 to 767
- block_owner: int32 [32], replicated, may hold values from 0 to 7, as said below
Outputs:
- natural_step: float32 [8192, 1024], P('dp', 'tensor')
- owner_block_inverses: float32 [32, 256, 256], P('dp')
The draws below stay inside these ranges and needn't reach their ends.
Inputs may be any that keep to these rules, and one draw needn't show every extreme that they name: `block_owner`: each index of dp owns either no block or exactly 4 blocks; block 0 is owned by index 4.
All inputs are finite; a program needn't handle non-finite values. Where the reference program divides by a largest or mean magnitude, that divisor is 1e-20 or more.
Results may differ from the reference program's by a relative error of at most 0.0003.
Values may be sent and summed in bfloat16 or wider, within the bound.
No kernel may reach another device: no remote copies, remote signals or barrier semaphores. Data moves between devices by JAX's collectives and lax.ppermute only.
A program may use at most 128 MiB of HBM per device.

```python
import math
import jax
import jax.numpy as jnp
from jax import lax

D = 8192
KVW = 1024
TOK_DEV = 768
S_DEV = 64
FACTOR_BLOCK = 256
ITERS = 10
TOKENS = 6144
SAMPLES = 512
NBLK = 32
GW = 256
CAP = 4
SLOT_TOTAL = 32
N_DP = 8
N_TENSOR = 4


def log_spread(key, count, low_end, high_end):
    uniform_unit = jax.random.uniform(key, (count,), jnp.float32)
    return low_end * jnp.exp(uniform_unit * math.log(high_end / low_end))


def scaled_field(key, row_total, column_total):
    subkeys = jax.random.split(key, 3)
    starting_values = jnp.clip(jax.random.normal(subkeys[0], (row_total, column_total), jnp.float32), -4.0, 4.0)
    row_scale = log_spread(subkeys[1], row_total, 0.3, 3.0)
    column_scale = log_spread(subkeys[2], column_total, 0.3, 3.0)
    return starting_values * row_scale[:, None] * column_scale[None, :]


def draw_activations(key, part):
    return scaled_field(jax.random.fold_in(key, 11), TOKENS, D).astype(jnp.bfloat16)


def draw_cotangent(key, part):
    return (scaled_field(jax.random.fold_in(key, 23), TOKENS, KVW) / 128.0).astype(jnp.bfloat16)


def draw_block_owner(key, part):
    key_blocks, key_devices = jax.random.split(jax.random.fold_in(key, 37))
    block_order = jax.random.permutation(key_blocks, NBLK)
    positions = jnp.argsort(block_order)
    mapping = jax.random.permutation(key_devices, N_DP).astype(jnp.int32)
    target = (positions[0] % N_DP).astype(jnp.int32)
    half_index = jnp.int32(N_DP // 2)
    current = jnp.take(mapping, target)
    device_ids = jnp.arange(N_DP, dtype=jnp.int32)
    swapped = jnp.where(mapping == half_index, current, mapping)
    swapped = jnp.where(device_ids == target, half_index, swapped)
    return jnp.take(swapped, positions % N_DP).astype(jnp.int32)


def plant(drawn, stream_key, smallest, largest):
    longest = drawn.shape.index(max(drawn.shape))
    spots = []
    for shift in (0, 1):
        where = [jax.random.randint(jax.random.fold_in(stream_key, axis), (), 0, length) for axis, length in enumerate(drawn.shape)]
        where[longest] = (where[longest] + shift) % drawn.shape[longest]
        spots.append(tuple(where))
    return drawn.at[spots[0]].set(smallest).at[spots[1]].set(largest)


def setup_inputs(seed: int = 0) -> dict:
    seeds = jax.random.split(jax.random.key(seed), 5)
    return {
        "activations": draw_activations(jax.random.fold_in(seeds[4], 71), 0),
        "cotangent": draw_cotangent(jax.random.fold_in(seeds[4], 71), 0),
        "sampled_rows": plant(jax.random.randint(seeds[2], (SAMPLES,), 0, TOK_DEV), jax.random.fold_in(seeds[2], 1), 0, TOK_DEV - 1).astype(jnp.int32),
        "block_owner": draw_block_owner(jax.random.fold_in(seeds[4], 71), 0),
    }


DAMPING = 0.05
precise_mode = lax.Precision.HIGHEST


def newton_inverse(matrix):
    extent = matrix.shape[-1]
    identity = jnp.eye(extent, dtype=jnp.float32)
    row_bound = jnp.max(jnp.sum(jnp.abs(matrix), axis=2), axis=1)
    initial = identity[None, :, :] / row_bound[:, None, None]

    def advance(turn_index, current):
        product = jnp.einsum("nij,njk->nik", matrix, current, precision=precise_mode)
        return jnp.einsum("nij,njk->nik", current, 2.0 * identity[None, :, :] - product, precision=precise_mode)

    return lax.fori_loop(0, ITERS, advance, initial)


def block_rank(block_owner):
    block_total = block_owner.shape[0]
    same_owner = block_owner[:, None] == block_owner[None, :]
    positions = jnp.arange(block_total, dtype=jnp.int32)
    before = positions[None, :] < positions[:, None]
    return jnp.sum((same_owner & before).astype(jnp.int32), axis=1)


def reference(activations, cotangent, sampled_rows, block_owner):
    grad = jnp.dot(activations.T, cotangent, preferred_element_type=jnp.float32)
    shard_base = (jnp.arange(SAMPLES, dtype=jnp.int32) // S_DEV) * TOK_DEV
    global_rows = (shard_base + sampled_rows).astype(jnp.int32)
    picked_acts = jnp.take(activations, global_rows, axis=0).astype(jnp.float32)
    picked_grads = jnp.take(cotangent, global_rows, axis=0).astype(jnp.float32)
    act_blocks = picked_acts.reshape(SAMPLES, NBLK, FACTOR_BLOCK)
    a_gram = jnp.einsum("snk,snl->nkl", act_blocks, act_blocks, precision=precise_mode)
    a_factor = a_gram / SAMPLES + DAMPING * jnp.eye(FACTOR_BLOCK, dtype=jnp.float32)[None, :, :]
    grad_groups = picked_grads.reshape(SAMPLES, N_TENSOR, GW)
    g_gram = jnp.einsum("snk,snl->nkl", grad_groups, grad_groups, precision=precise_mode)
    g_factor = g_gram * (TOKENS / SAMPLES) + DAMPING * jnp.eye(GW, dtype=jnp.float32)[None, :, :]
    input_factor_inverse = newton_inverse(a_factor)
    g_inverse = newton_inverse(g_factor)
    grad_four = grad.reshape(NBLK, FACTOR_BLOCK, N_TENSOR, GW)
    right_done = jnp.einsum("njtk,tkl->njtl", grad_four, g_inverse, precision=precise_mode)
    natural_step = jnp.einsum("nij,njtl->nitl", input_factor_inverse, right_done, precision=precise_mode).reshape(D, KVW)
    owner_slot_index = (block_owner * CAP + block_rank(block_owner)).astype(jnp.int32)
    owner_block_inverses = jnp.zeros((SLOT_TOTAL, FACTOR_BLOCK, FACTOR_BLOCK), jnp.float32).at[owner_slot_index].set(input_factor_inverse)
    return natural_step, owner_block_inverses
```

```python
import jax
import jax.numpy as jnp
from jax import lax
from jax.experimental import pallas as pl
from jax.experimental.pallas import tpu as pltpu
from jax.sharding import PartitionSpec as P

S_DEV = 64
FACTOR_BLOCK = 256
ITERS = 10


DAMPING = 0.05
precise_mode = lax.Precision.HIGHEST
f32 = jnp.float32
bf16 = jnp.bfloat16


def block_rank(block_owner):
    block_total = block_owner.shape[0]
    same_owner = block_owner[:, None] == block_owner[None, :]
    positions = jnp.arange(block_total, dtype=jnp.int32)
    before = positions[None, :] < positions[:, None]
    return jnp.sum((same_owner & before).astype(jnp.int32), axis=1)


def from_partner(block, axis, apart):
    count = lax.axis_size(axis)
    route = []
    for low in range(count):
        high = low | 1 << apart
        if high != low and high < count:
            route += [(low, high), (high, low)]
    return lax.ppermute(block, axis, route)


def newton_inverse(matrix):
    extent = matrix.shape[-1]
    identity = jnp.eye(extent, dtype=jnp.float32)
    row_bound = jnp.max(jnp.sum(jnp.abs(matrix), axis=2), axis=1)
    initial = identity[None, :, :] / row_bound[:, None, None]

    def advance(turn_index, current):
        product = jnp.einsum("nij,njk->nik", matrix, current, precision=precise_mode)
        return jnp.einsum(
            "nij,njk->nik", current, 2.0 * identity[None, :, :] - product, precision=precise_mode
        )

    return lax.fori_loop(0, ITERS, advance, initial)


def owner_grams(received):
    return jnp.einsum("pcsk,pcsl->ckl", received, received, preferred_element_type=jnp.float32)


def general_device(activations, cotangent, sampled_rows, block_owner):
    tok_local = activations.shape[0]
    model_width = activations.shape[1]
    group_w = cotangent.shape[1]
    dp_count = lax.axis_size("dp")
    my_dp = lax.axis_index("dp")
    block_total = model_width // FACTOR_BLOCK
    capacity = max(1, block_total // dp_count)
    row_share = model_width // dp_count
    samples_all = S_DEV * dp_count
    grad_rows = lax.psum_scatter(
        lax.dot_general(
            activations, cotangent, (((0,), (0,)), ((), ())), preferred_element_type=jnp.float32
        ),
        "dp",
        scatter_dimension=0,
        tiled=True,
    )
    picked_acts = jnp.take(activations, sampled_rows, axis=0)
    picked_grads = jnp.take(cotangent, sampled_rows, axis=0)
    g_partial = lax.dot_general(
        picked_grads, picked_grads, (((0,), (0,)), ((), ())), preferred_element_type=jnp.float32
    )
    g_total = lax.psum(g_partial, "dp")
    g_factor = g_total * (tok_local / S_DEV) + DAMPING * jnp.eye(group_w, dtype=jnp.float32)
    slot_of = block_owner * capacity + block_rank(block_owner)
    dest_ids = jnp.arange(dp_count * capacity, dtype=jnp.int32)
    chooser = (slot_of[None, :] == dest_ids[:, None]).astype(jnp.bfloat16)
    row_blocks = picked_acts.reshape(S_DEV, block_total, FACTOR_BLOCK)
    outgoing = lax.dot_general(
        chooser, row_blocks, (((1,), (1,)), ((), ())), preferred_element_type=jnp.float32
    )
    outgoing = outgoing.astype(jnp.bfloat16).reshape(dp_count, capacity, S_DEV, FACTOR_BLOCK)
    gram_slots = owner_grams(
        lax.all_to_all(outgoing, "dp", split_axis=0, concat_axis=0, tiled=True)
    )
    a_factor = (
        gram_slots / samples_all + DAMPING * jnp.eye(FACTOR_BLOCK, dtype=jnp.float32)[None, :, :]
    )
    input_factor_inverse = newton_inverse(a_factor)
    owned_count = jnp.sum((block_owner == my_dp).astype(jnp.int32))
    slot_used = jnp.arange(capacity, dtype=jnp.int32) < owned_count
    owned_out = jnp.where(slot_used[:, None, None], input_factor_inverse, 0.0)
    g_inverse = newton_inverse(g_factor[None, :, :])[0]
    per_dev = max(1, row_share // FACTOR_BLOCK)
    rows_each = min(row_share, FACTOR_BLOCK)
    first_block = my_dp * row_share // FACTOR_BLOCK
    need_ids = first_block + jnp.arange(per_dev, dtype=jnp.int32)
    need_slots = jnp.take(slot_of, need_ids)
    row_offset = my_dp * row_share % FACTOR_BLOCK
    shard_piece = lax.all_gather(owned_out, "dp", axis=0, tiled=True)
    rows_part = lax.dynamic_slice_in_dim(shard_piece, row_offset, rows_each, 1)
    slot_ids = jnp.arange(shard_piece.shape[0], dtype=jnp.int32)
    selector = (need_slots[:, None] == slot_ids[None, :]).astype(jnp.float32)
    inverse_rows = jnp.einsum("jm,mkl->jkl", selector, rows_part, precision=precise_mode)
    grad_right = jnp.dot(
        grad_rows, g_inverse, precision=precise_mode, preferred_element_type=jnp.float32
    )
    if row_share < FACTOR_BLOCK:
        partner = from_partner(grad_right, "dp", 0)
        is_lower = my_dp % 2 == 0
        joined = jnp.where(
            is_lower,
            jnp.concatenate([grad_right, partner], 0),
            jnp.concatenate([partner, grad_right], 0),
        )
        complete_rows = joined[None, :, :]
    else:
        complete_rows = grad_right.reshape(per_dev, FACTOR_BLOCK, group_w)
    natural_step = jnp.einsum("jrk,jkl->jrl", inverse_rows, complete_rows, precision=precise_mode)
    return (natural_step.reshape(row_share, group_w), owned_out)


VMEM_LIMIT = 48 * 1024 * 1024


def vmem(shape=None, index_map=None):
    if shape is None:
        return pl.BlockSpec(memory_space=pltpu.VMEM)
    return pl.BlockSpec(shape, index_map)


def pick_body(ids, rows_ref, cot_ref, act_ref, out_ref, held, sems):
    count = held.shape[0]
    dests = count // 2

    def copy(i):
        start = pl.multiple_of(ids[i] * FACTOR_BLOCK, FACTOR_BLOCK)
        return pltpu.make_async_copy(
            act_ref.at[:, pl.ds(start, FACTOR_BLOCK)], held.at[i], sems.at[i]
        )

    for i in range(count):
        copy(i).start()
    samples = rows_ref.shape[0]
    tokens = cot_ref.shape[0]
    places = lax.broadcasted_iota(jnp.int32, (samples, tokens), 1)
    chooser = (places == rows_ref[...]).astype(bf16)
    picked = jnp.dot(chooser, cot_ref[...], preferred_element_type=f32).astype(bf16)
    for d in range(dests):
        out_ref[d, :, 2 * FACTOR_BLOCK :] = picked
    for i in range(count):
        copy(i).wait()
        picked = jnp.dot(chooser, held[i], preferred_element_type=f32).astype(bf16)
        out_ref[i // 2, :, (i % 2) * FACTOR_BLOCK : (i % 2 + 1) * FACTOR_BLOCK] = picked


def pick_rows(ids, sampled_rows, cotangent, activations):
    count = ids.shape[0]
    samples = sampled_rows.shape[0]
    tokens, group_w = cotangent.shape
    return pl.pallas_call(
        pick_body,
        out_shape=jax.ShapeDtypeStruct(
            (count // 2, samples, 2 * FACTOR_BLOCK + group_w), bf16
        ),
        grid_spec=pltpu.PrefetchScalarGridSpec(
            num_scalar_prefetch=1,
            grid=(),
            in_specs=[vmem(), vmem(), pl.BlockSpec(memory_space=pl.ANY)],
            out_specs=vmem(),
            scratch_shapes=[
                pltpu.VMEM((count, tokens, FACTOR_BLOCK), bf16),
                pltpu.SemaphoreType.DMA((count,)),
            ],
        ),
        compiler_params=pltpu.CompilerParams(vmem_limit_bytes=VMEM_LIMIT),
        cost_estimate=pl.CostEstimate(
            flops=2 * samples * tokens * count * FACTOR_BLOCK,
            bytes_accessed=2 * tokens * count * FACTOR_BLOCK,
            transcendentals=0,
        ),
        name="pick_rows",
    )(ids, sampled_rows[:, None], cotangent, activations)


def grad_body(ids, cot_ref, act_ref, first_ref, second_ref, turned):
    half = pl.num_programs(0) // 2
    step = pl.program_id(0)

    @pl.when(step == 0)
    def _():
        turned[...] = cot_ref[...].astype(f32).T.astype(bf16)

    product = jnp.dot(turned[...], act_ref[...], preferred_element_type=f32)

    @pl.when(step < half)
    def _():
        first_ref[0] = product

    @pl.when(step >= half)
    def _():
        second_ref[0] = product


def partial_grads(ids, cotangent, activations, row_share):
    tokens, group_w = cotangent.shape
    steps = ids.shape[0]
    half = steps // 2
    one = jax.ShapeDtypeStruct((half, group_w, row_share), f32)
    return pl.pallas_call(
        grad_body,
        out_shape=(one, one),
        grid_spec=pltpu.PrefetchScalarGridSpec(
            num_scalar_prefetch=1,
            grid=(steps,),
            in_specs=[
                pl.BlockSpec((tokens, group_w), lambda i, ids: (0, 0)),
                pl.BlockSpec((tokens, row_share), lambda i, ids: (0, ids[i])),
            ],
            out_specs=[
                pl.BlockSpec((1, group_w, row_share), lambda i, ids: (jnp.minimum(i, half - 1), 0, 0)),
                pl.BlockSpec((1, group_w, row_share), lambda i, ids: (jnp.maximum(i - half, 0), 0, 0)),
            ],
            scratch_shapes=[pltpu.VMEM((group_w, tokens), bf16)],
        ),
        compiler_params=pltpu.CompilerParams(vmem_limit_bytes=VMEM_LIMIT),
        cost_estimate=pl.CostEstimate(
            flops=2 * tokens * group_w * row_share * steps,
            bytes_accessed=steps * row_share * (2 * tokens + 4 * group_w),
            transcendentals=0,
        ),
        name="partial_grads",
    )(ids, cotangent, activations)


def exact_dot(left, right, dims=(((1,), (0,)), ((), ()))):
    return lax.dot_general(left, right, dims, precision=precise_mode, preferred_element_type=f32)


def invert_body(scales, rows_ref, need_ref, own_ref, out_ref):
    width = FACTOR_BLOCK
    eye = (
        lax.broadcasted_iota(jnp.int32, (width, width), 0)
        == lax.broadcasted_iota(jnp.int32, (width, width), 1)
    ).astype(f32)
    states = []
    for m in range(3):
        rows = rows_ref[:, m * width : (m + 1) * width]
        gram = lax.dot_general(
            rows, rows, (((0,), (0,)), ((), ())), preferred_element_type=f32
        )
        matrix = gram * scales[m] + DAMPING * eye
        bound = jnp.max(jnp.sum(jnp.abs(matrix), axis=1, keepdims=True), axis=0, keepdims=True)
        inverse_bound = 1.0 / bound
        low = matrix * inverse_bound
        states.append((low, (2.0 * eye - low) * inverse_bound))
    lows = [2.0 * low - exact_dot(low, low) for low, _ in states]
    currents = [current for _, current in states]
    for turn in range(1, ITERS):
        if turn < ITERS - 1:
            both = [
                exact_dot(jnp.concatenate([current, low], axis=0), low)
                for current, low in zip(currents, lows)
            ]
            currents = [2.0 * current - b[:width] for current, b in zip(currents, both)]
            lows = [2.0 * low - b[width:] for low, b in zip(lows, both)]
        else:
            currents = [
                2.0 * current - exact_dot(current, low) for current, low in zip(currents, lows)
            ]
    need_ref[...] = currents[0]
    own_ref[...] = currents[1] * scales[3]
    out_ref[...] = currents[2]


def invert_factors(scales, rows):
    one = jax.ShapeDtypeStruct((FACTOR_BLOCK, FACTOR_BLOCK), f32)
    return pl.pallas_call(
        invert_body,
        out_shape=(one, one, one),
        in_specs=[pl.BlockSpec(memory_space=pltpu.SMEM), vmem()],
        out_specs=(vmem(), vmem(), vmem()),
        compiler_params=pltpu.CompilerParams(vmem_limit_bytes=VMEM_LIMIT),
        cost_estimate=pl.CostEstimate(
            flops=2 * 6 * 3 * 19 * FACTOR_BLOCK**3, bytes_accessed=2 << 20, transcendentals=0
        ),
        name="invert_factors",
    )(scales, rows)


def finish_body(order, *refs):
    (self_own, self_got, x_a, x_b, y_a, y_b, g_ref) = refs[:7]
    needs, owns = refs[7:11], refs[11:15]
    step_ref, owned_ref = refs[15:]
    half = x_a.shape[0]
    top = self_own[0, :half] + self_got[0, :half] + (x_a[...] + y_a[...])
    low = self_own[0, half:] + self_got[0, half:] + (x_b[...] + y_b[...])
    total = jnp.concatenate([top, low], axis=0)
    right = exact_dot(g_ref[...], total, (((0,), (0,)), ((), ())))
    tmp = right
    blocks = []
    for j in range(len(needs)):
        blocks.append(tmp[:, j * FACTOR_BLOCK : (j + 1) * FACTOR_BLOCK])
    for k in range(len(needs)):
        j = order[k]
        owned_ref[j] = owns[k][...]
        chosen = blocks[0]
        for other in range(1, len(needs)):
            chosen = jnp.where(j == other, blocks[other], chosen)
        start = pl.multiple_of(j * FACTOR_BLOCK, FACTOR_BLOCK)
        step_ref[pl.ds(start, FACTOR_BLOCK), :] = exact_dot(
            needs[k][...], chosen, (((1,), (1,)), ((), ()))
        )


def finish(order, pieces, needs, owns):
    group_w, row_share = pieces[0].shape[1:]
    count = len(needs)
    return pl.pallas_call(
        finish_body,
        out_shape=(
            jax.ShapeDtypeStruct((row_share, group_w), f32),
            jax.ShapeDtypeStruct((count, FACTOR_BLOCK, FACTOR_BLOCK), f32),
        ),
        in_specs=[pl.BlockSpec(memory_space=pltpu.SMEM)] + [vmem()] * (7 + 2 * count),
        out_specs=(vmem(), vmem()),
        compiler_params=pltpu.CompilerParams(vmem_limit_bytes=VMEM_LIMIT),
        cost_estimate=pl.CostEstimate(
            flops=2 * 6 * 2 * row_share * group_w * FACTOR_BLOCK,
            bytes_accessed=9 << 20,
            transcendentals=0,
        ),
        name="finish",
    )(order, *pieces, *needs, *owns)


def square_device(activations, cotangent, sampled_rows, block_owner):
    tok_local, model_width = activations.shape
    dp_count = lax.axis_size("dp")
    depth = lax.axis_size("tensor")
    me = lax.axis_index("dp")
    z = lax.axis_index("tensor")
    samples = sampled_rows.shape[0]
    row_share = model_width // dp_count
    block_total = block_owner.shape[0]
    capacity = block_total // dp_count

    def swap(block, bit):
        return lax.ppermute(block, "dp", [(i, i ^ bit) for i in range(dp_count)])

    def shift(block, by):
        return lax.ppermute(block, "tensor", [(i, (i + by) % depth) for i in range(depth)])

    core, across_x, across_y = 1, 2, 4

    slot_of = block_owner * capacity + block_rank(block_owner)
    dests = jnp.arange(dp_count, dtype=jnp.int32)
    my_slots = dests * capacity + z
    blocks = jnp.arange(block_total, dtype=jnp.int32)
    in_slot = slot_of[None, :] == my_slots[:, None]
    slot_block = jnp.sum(jnp.where(in_slot, blocks[None, :], 0), axis=1)
    ids = jnp.stack([my_slots, slot_block], axis=1).reshape(2 * dp_count)
    owned_count = jnp.sum((block_owner == me).astype(jnp.int32))
    used = (z < owned_count).astype(f32)
    scales = jnp.stack(
        [
            jnp.asarray(1.0 / (samples * dp_count), f32),
            jnp.asarray(1.0 / (samples * dp_count), f32),
            jnp.asarray(tok_local / samples, f32),
            used,
        ]
    )

    def grads(masks):
        to = [me ^ m ^ core for m in masks] + [me ^ m for m in masks]
        return partial_grads(jnp.stack(to).astype(jnp.int32), cotangent, activations, row_share)

    far_theirs, far_mine = grads([across_x | across_y])
    far_got = swap(far_theirs, core)
    picked = pick_rows(ids, sampled_rows, cotangent, activations)
    got = lax.all_to_all(picked, "dp", split_axis=0, concat_axis=0, tiled=True)
    half = cotangent.shape[1] // 2
    far_x = swap(far_mine[0, :half] + far_got[0, :half], across_x)
    far_y = swap(far_mine[0, half:] + far_got[0, half:], across_y)

    near_theirs, near_mine = grads([across_x, across_y])
    near_got = swap(near_theirs, core)
    self_theirs, self_mine = grads([0])
    self_got = swap(self_theirs, core)

    x_a = swap(near_mine[0, :half] + near_got[0, :half], across_x)
    y_b = swap(near_mine[1, half:] + near_got[1, half:], across_y)
    x_b = swap(near_mine[0, half:] + near_got[0, half:] + far_y, across_x)
    y_a = swap(near_mine[1, :half] + near_got[1, :half] + far_x, across_y)

    need, own, g_inverse = invert_factors(scales, got.reshape(-1, got.shape[-1]))
    needs = [need] + [shift(need, by) for by in range(1, depth)]
    owns = [own] + [shift(own, by) for by in range(1, depth)]
    order = jnp.stack([(z - by) % depth for by in range(depth)]).astype(jnp.int32)
    return finish(order, (self_mine, self_got, x_a, x_b, y_a, y_b, g_inverse), needs, owns)


def solution(mesh):
    def per_device(activations, cotangent, sampled_rows, block_owner):
        block_total = activations.shape[1] // FACTOR_BLOCK
        dp_count, depth = mesh.shape["dp"], mesh.shape["tensor"]
        fits = (
            dp_count == 8
            and block_total == dp_count * depth
            and cotangent.shape[1] == FACTOR_BLOCK
            and sampled_rows.shape[0] % 16 == 0
            and activations.shape[0] % 128 == 0
        )
        run = square_device if fits else general_device
        return run(activations, cotangent, sampled_rows, block_owner)

    return jax.shard_map(
        per_device,
        mesh=mesh,
        in_specs=(P("dp", None), P("dp", "tensor"), P("dp"), P()),
        out_specs=(P("dp", "tensor"), P("dp", None, None)),
        check_vma=False,
    )
```

```python
import functools

import jax
import jax.numpy as jnp
from jax import lax
from jax.experimental import pallas as pl
from jax.experimental.pallas import tpu as pltpu
from jax.sharding import PartitionSpec as P

S_DEV = 64
FACTOR_BLOCK = 256
ITERS = 10


DAMPING = 0.05
precise_mode = lax.Precision.HIGHEST
f32 = jnp.float32
bf16 = jnp.bfloat16


def block_rank(block_owner):
    block_total = block_owner.shape[0]
    same_owner = block_owner[:, None] == block_owner[None, :]
    positions = jnp.arange(block_total, dtype=jnp.int32)
    before = positions[None, :] < positions[:, None]
    return jnp.sum((same_owner & before).astype(jnp.int32), axis=1)


def from_partner(block, axis, apart):
    count = lax.axis_size(axis)
    route = []
    for low in range(count):
        high = low | 1 << apart
        if high != low and high < count:
            route += [(low, high), (high, low)]
    return lax.ppermute(block, axis, route)


def newton_inverse(matrix):
    extent = matrix.shape[-1]
    identity = jnp.eye(extent, dtype=jnp.float32)
    row_bound = jnp.max(jnp.sum(jnp.abs(matrix), axis=2), axis=1)
    initial = identity[None, :, :] / row_bound[:, None, None]

    def advance(turn_index, current):
        product = jnp.einsum("nij,njk->nik", matrix, current, precision=precise_mode)
        return jnp.einsum(
            "nij,njk->nik", current, 2.0 * identity[None, :, :] - product, precision=precise_mode
        )

    return lax.fori_loop(0, ITERS, advance, initial)


def owner_grams(received):
    return jnp.einsum("pcsk,pcsl->ckl", received, received, preferred_element_type=jnp.float32)


def general_device(activations, cotangent, sampled_rows, block_owner):
    tok_local = activations.shape[0]
    model_width = activations.shape[1]
    group_w = cotangent.shape[1]
    dp_count = lax.axis_size("dp")
    my_dp = lax.axis_index("dp")
    block_total = model_width // FACTOR_BLOCK
    capacity = max(1, block_total // dp_count)
    row_share = model_width // dp_count
    samples_all = S_DEV * dp_count
    grad_rows = lax.psum_scatter(
        lax.dot_general(
            activations, cotangent, (((0,), (0,)), ((), ())), preferred_element_type=jnp.float32
        ),
        "dp",
        scatter_dimension=0,
        tiled=True,
    )
    picked_acts = jnp.take(activations, sampled_rows, axis=0)
    picked_grads = jnp.take(cotangent, sampled_rows, axis=0)
    g_partial = lax.dot_general(
        picked_grads, picked_grads, (((0,), (0,)), ((), ())), preferred_element_type=jnp.float32
    )
    g_total = lax.psum(g_partial, "dp")
    g_factor = g_total * (tok_local / S_DEV) + DAMPING * jnp.eye(group_w, dtype=jnp.float32)
    slot_of = block_owner * capacity + block_rank(block_owner)
    dest_ids = jnp.arange(dp_count * capacity, dtype=jnp.int32)
    chooser = (slot_of[None, :] == dest_ids[:, None]).astype(jnp.bfloat16)
    row_blocks = picked_acts.reshape(S_DEV, block_total, FACTOR_BLOCK)
    outgoing = lax.dot_general(
        chooser, row_blocks, (((1,), (1,)), ((), ())), preferred_element_type=jnp.float32
    )
    outgoing = outgoing.astype(jnp.bfloat16).reshape(dp_count, capacity, S_DEV, FACTOR_BLOCK)
    gram_slots = owner_grams(
        lax.all_to_all(outgoing, "dp", split_axis=0, concat_axis=0, tiled=True)
    )
    a_factor = (
        gram_slots / samples_all + DAMPING * jnp.eye(FACTOR_BLOCK, dtype=jnp.float32)[None, :, :]
    )
    input_factor_inverse = newton_inverse(a_factor)
    owned_count = jnp.sum((block_owner == my_dp).astype(jnp.int32))
    slot_used = jnp.arange(capacity, dtype=jnp.int32) < owned_count
    owned_out = jnp.where(slot_used[:, None, None], input_factor_inverse, 0.0)
    g_inverse = newton_inverse(g_factor[None, :, :])[0]
    per_dev = max(1, row_share // FACTOR_BLOCK)
    rows_each = min(row_share, FACTOR_BLOCK)
    first_block = my_dp * row_share // FACTOR_BLOCK
    need_ids = first_block + jnp.arange(per_dev, dtype=jnp.int32)
    need_slots = jnp.take(slot_of, need_ids)
    row_offset = my_dp * row_share % FACTOR_BLOCK
    shard_piece = lax.all_gather(owned_out, "dp", axis=0, tiled=True)
    rows_part = lax.dynamic_slice_in_dim(shard_piece, row_offset, rows_each, 1)
    slot_ids = jnp.arange(shard_piece.shape[0], dtype=jnp.int32)
    selector = (need_slots[:, None] == slot_ids[None, :]).astype(jnp.float32)
    inverse_rows = jnp.einsum("jm,mkl->jkl", selector, rows_part, precision=precise_mode)
    grad_right = jnp.dot(
        grad_rows, g_inverse, precision=precise_mode, preferred_element_type=jnp.float32
    )
    if row_share < FACTOR_BLOCK:
        partner = from_partner(grad_right, "dp", 0)
        is_lower = my_dp % 2 == 0
        joined = jnp.where(
            is_lower,
            jnp.concatenate([grad_right, partner], 0),
            jnp.concatenate([partner, grad_right], 0),
        )
        complete_rows = joined[None, :, :]
    else:
        complete_rows = grad_right.reshape(per_dev, FACTOR_BLOCK, group_w)
    natural_step = jnp.einsum("jrk,jkl->jrl", inverse_rows, complete_rows, precision=precise_mode)
    return (natural_step.reshape(row_share, group_w), owned_out)


MIB = 1 << 20
VMEM_MIB = 63
AHEAD = 3
PREPARE_FLOPS = 20_000_000_000
ANY = pl.BlockSpec(memory_space=pl.ANY)
VMEM = pl.BlockSpec(memory_space=pltpu.VMEM)
SMEM = pl.BlockSpec(memory_space=pltpu.SMEM)
CORE, NEAR_X, NEAR_Y, FAR = 1, 2, 4, 6
MASKS = (FAR, NEAR_X, NEAR_Y, 0)


def shaped(shape, dtype=f32):
    return jax.ShapeDtypeStruct(shape, dtype)


def call(body, name, out_shape, in_specs, out_specs, scratch=(), flops=0, moved=0):
    return pl.pallas_call(
        body,
        out_shape=out_shape,
        in_specs=in_specs,
        out_specs=out_specs,
        scratch_shapes=scratch,
        compiler_params=pltpu.CompilerParams(vmem_limit_bytes=VMEM_MIB * MIB),
        cost_estimate=pl.CostEstimate(flops=flops, bytes_accessed=moved, transcendentals=0),
        name=name,
    )


def start_all(sources, targets, sems, first=0):
    copies = [
        pltpu.make_async_copy(source, target, sems.at[first + i])
        for i, (source, target) in enumerate(zip(sources, targets))
    ]
    for copy in copies:
        copy.start()
    return copies


def fold_rows(rows):
    return rows + rows // 2


def encode(x, into):
    rows = x.shape[0]
    high = x.astype(bf16)
    into[:rows] = high
    base = high.astype(f32)
    left = (x - base) * pl.reciprocal(base, approx=True) * 256.0
    left = jnp.where(jnp.abs(base) < 1e-30, 0.0, jnp.clip(left, -1.0, 1.0))
    digit = jnp.floor(left * 63.5 + 64.0)
    first, second = digit[: rows // 2], digit[rows // 2 :]
    negative = second >= 64.0
    power = jnp.exp2(jnp.where(negative, second - 96.0, second - 32.0))
    packed = (first + 128.0) * power
    into[rows:] = jnp.where(negative, -packed, packed).astype(bf16)


def decode(ref):
    rows = ref.shape[0] * 2 // 3
    packed = ref[rows:].astype(f32)
    size = jnp.abs(packed)
    power = jnp.floor(jnp.log2(size) + 1e-3)
    first = jnp.floor(size * jnp.exp2(7.0 - power) + 0.5) - 128.0
    second = power + jnp.where(packed < 0.0, 89.0, 25.0)
    digit = jnp.concatenate([first, second], axis=0)
    base = ref[:rows].astype(f32)
    return base + base * ((digit - 63.5) * (1.0 / (63.5 * 256.0)))


def project_body(
    owner, rows_ref, cot_ref, act_ref, theirs, own_theirs, out_ref,
    held, cot, rows, left, grads, picks, slots, sems, out_sems, small_sems,
):
    count, tokens, share = held.shape
    group_w = cot.shape[1]
    samples = rows.shape[1]
    per_tile = share // FACTOR_BLOCK
    me = lax.axis_index("dp")
    z = lax.axis_index("tensor")
    half = count // 2
    tiles = [me ^ m ^ CORE for m in MASKS] + [me ^ m for m in MASKS]
    targets = [theirs.at[i] for i in range(half - 1)] + [own_theirs.at[0]]

    small = start_all([cot_ref, rows_ref], [cot, rows], small_sems)
    starts = [pl.multiple_of(t * share, share) for t in tiles]
    loads = [
        pltpu.make_async_copy(act_ref.at[:, pl.ds(start, share)], held.at[i], sems.at[i])
        for i, start in enumerate(starts)
    ]
    for load in loads[:AHEAD]:
        load.start()

    for d in range(count):
        slots[0, d] = 0
        slots[1, d] = 0
    for b in range(owner.shape[0]):
        holder = owner[b]
        rank = slots[0, holder]
        slots[0, holder] = rank + 1
        slots[1, holder] = jnp.where(rank == z, b, slots[1, holder])

    for copy in small:
        copy.wait()
    left[:group_w] = cot[...].astype(f32).T.astype(bf16)
    places = lax.broadcasted_iota(jnp.int32, (tokens, samples), 0)
    left[group_w:] = (places == rows[...]).astype(f32).T.astype(bf16)

    stores = []
    for i in range(count):
        loads[i].wait()
        if i + AHEAD < count:
            loads[i + AHEAD].start()
        if i < half:
            product = jnp.dot(left[...], held[i], preferred_element_type=f32)
            grads[i] = product[:group_w]
            stores += start_all([grads.at[i]], [targets[i]], out_sems, i)
            picked = product[group_w:]
        else:
            picked = jnp.dot(left[group_w:], held[i], preferred_element_type=f32)
        for j in range(per_tile):
            picks[tiles[i] * per_tile + j] = picked[
                :, j * FACTOR_BLOCK : (j + 1) * FACTOR_BLOCK
            ].astype(bf16)
    picked_cot = jnp.dot(left[group_w:], cot[...], preferred_element_type=f32).astype(bf16)
    for d in range(count):
        first = d * per_tile + 2 * (z % 2)
        for j, block in enumerate((first, first + 1, slots[1, d])):
            out_ref[d, :, j * FACTOR_BLOCK : (j + 1) * FACTOR_BLOCK] = picks[block]
        out_ref[d, :, 3 * FACTOR_BLOCK :] = picked_cot
    for store in stores:
        store.wait()


def project(block_owner, sampled_rows, cotangent, activations, count):
    samples = sampled_rows.shape[0]
    tokens, group_w = cotangent.shape
    model_width = activations.shape[1]
    share = model_width // count
    one = shaped((1, group_w, share))
    rest = shaped((count // 2 - 1, group_w, share))
    return call(
        project_body,
        "project",
        (rest, one, shaped((count, samples, 3 * FACTOR_BLOCK + group_w), bf16)),
        [SMEM, ANY, ANY, ANY],
        (ANY, ANY, VMEM),
        [
            pltpu.VMEM((count, tokens, share), bf16),
            pltpu.VMEM((tokens, group_w), bf16),
            pltpu.VMEM((1, samples), jnp.int32),
            pltpu.VMEM((group_w + samples, tokens), bf16),
            pltpu.VMEM((count // 2, group_w, share), f32),
            pltpu.VMEM((model_width // FACTOR_BLOCK, samples, FACTOR_BLOCK), bf16),
            pltpu.SMEM((2, count), jnp.int32),
            pltpu.SemaphoreType.DMA((count,)),
            pltpu.SemaphoreType.DMA((count // 2,)),
            pltpu.SemaphoreType.DMA((2,)),
        ],
        flops=2 * tokens * (group_w + samples) * model_width,
        moved=2 * tokens * model_width + 2 * group_w * model_width,
    )(block_owner, sampled_rows[None, :], cotangent, activations)


def sum_body(cot_ref, act_ref, got_ref, x_ref, y_ref, x_b, y_a, cot, held, got, left, wire, plain, sems, got_sems, out_sems):
    share = held.shape[2]
    half = cot.shape[1] // 2
    me = lax.axis_index("dp")
    starts = [pl.multiple_of((me ^ m) * share, share) for m in MASKS[:3]]
    loads = start_all(
        [cot_ref] + [act_ref.at[:, pl.ds(start, share)] for start in starts],
        [cot] + [held.at[i] for i in range(3)],
        sems,
    )
    more = start_all([got_ref.at[i] for i in range(3)], [got.at[i] for i in range(3)], got_sems)
    loads[0].wait()
    left[...] = cot[...].astype(f32).T.astype(bf16)
    targets = [(x_ref.at[0], y_ref.at[0]), (x_ref.at[1], x_b), (y_a, y_ref.at[1])]
    stores = []
    for i in range(3):
        loads[i + 1].wait()
        product = jnp.dot(left[...], held[i], preferred_element_type=f32)
        more[i].wait()
        got[i] += product
        for k in range(2):
            part = got[i, k * half : (k + 1) * half]
            n = 2 * i + k
            if n in (3, 4):
                plain[n - 3] = part
                source = plain.at[n - 3]
            else:
                encode(part, wire.at[n])
                source = wire.at[n]
            stores += start_all([source], [targets[i][k]], out_sems, n)
    for store in stores:
        store.wait()


def hop_body(x_b, y_a, x_got, y_got, _, x_ref, y_ref, x_own, y_own, x_in, y_in, x_out, y_out, sems, out_sems):
    loads = start_all(
        [x_b, y_got.at[0], y_a, x_got.at[0]], [x_own, y_in, y_own, x_in], sems
    )
    stores = []
    for n, (own, come, out, ref) in enumerate(((x_own, y_in, x_out, x_ref), (y_own, x_in, y_out, y_ref))):
        loads[2 * n].wait()
        loads[2 * n + 1].wait()
        encode(own[...] + decode(come), out)
        stores += start_all([out], [ref], out_sems, n)
    for store in stores:
        store.wait()


def two(x):
    high = x.astype(bf16)
    return high, (x - high.astype(f32)).astype(bf16)


def wide_dot(left, right, dims=(((1,), (0,)), ((), ()))):
    left_high, left_low = two(left)
    right_high, right_low = two(right)

    def dot(a, b):
        return lax.dot_general(a, b, dims, preferred_element_type=f32)

    return dot(left_high, right_high) + (dot(left_high, right_low) + dot(left_low, right_high))


def places(extent):
    return (
        lax.broadcasted_iota(jnp.int32, (extent, extent), 0),
        lax.broadcasted_iota(jnp.int32, (extent, extent), 1),
    )


FOLD_ROWS = 8


def fold(matrix, into, at=()):
    half = matrix.shape[0] // 2
    row, column = places(half)
    low = matrix[half:, half:]
    into[(*at, slice(0, half), slice(0, half))] = jnp.where(row <= column, matrix[:half, :half], low)
    into[(*at, slice(0, half), slice(half, 2 * half))] = matrix[:half, half:]
    diagonal = jnp.sum(jnp.where(row == column, low, 0.0), axis=0, keepdims=True)
    wide = jnp.concatenate([diagonal, diagonal], axis=1)
    into[(*at, slice(half, half + FOLD_ROWS))] = jnp.broadcast_to(wide, (FOLD_ROWS, 2 * half))


def unfold(packed):
    half = packed.shape[1] // 2
    row, column = places(half)
    both, corner = packed[:half, :half], packed[:half, half:]
    turned = both.T
    top = jnp.where(row <= column, both, turned)
    low = jnp.where(row == column, packed[half : half + 1, :half], jnp.where(row > column, both, turned))
    return jnp.concatenate(
        [jnp.concatenate([top, corner], axis=1), jnp.concatenate([corner.T, low], axis=1)], axis=0
    )


def invert_body(scales, owner, rows_ref, _, __, all_ref, own_ref, out_ref):
    width = FACTOR_BLOCK
    me = lax.axis_index("dp")
    owned = jnp.int32(0)
    for b in range(owner.shape[0]):
        owned = owned + jnp.where(owner[b] == me, 1, 0)
    used = jnp.where(lax.axis_index("tensor") < owned, 1.0, 0.0).astype(f32)
    row, column = places(width)
    eye = (row == column).astype(f32)
    states = []
    for m in range(4):
        rows = rows_ref[:, m * width : (m + 1) * width]
        gram = lax.dot_general(
            rows, rows, (((0,), (0,)), ((), ())), preferred_element_type=f32
        )
        matrix = gram * scales[1 if m == 3 else 0] + DAMPING * eye
        bound = jnp.max(jnp.sum(jnp.abs(matrix), axis=1, keepdims=True), axis=0, keepdims=True)
        inverse_bound = 1.0 / bound
        low = matrix * inverse_bound
        states.append((low, (2.0 * eye - low) * inverse_bound))
    lows = [2.0 * low - wide_dot(low, low) for low, _ in states]
    currents = [current for _, current in states]
    for turn in range(1, ITERS):
        if turn < ITERS - 1:
            both = [
                wide_dot(jnp.concatenate([current, low], axis=0), low)
                for current, low in zip(currents, lows)
            ]
            currents = [2.0 * current - b[:width] for current, b in zip(currents, both)]
            lows = [2.0 * low - b[width:] for low, b in zip(lows, both)]
        else:
            currents = [
                2.0 * current - wide_dot(current, low) for current, low in zip(currents, lows)
            ]
    fold(currents[0], all_ref, (0,))
    fold(currents[1], all_ref, (1,))
    fold(currents[2] * used, all_ref, (2,))
    own_ref[...] = all_ref[2]
    out_ref[...] = currents[3]


def owned_body(here, beside, two_off, three_off, _, out_ref, held, sems):
    loads = start_all([here.at[2], beside.at[2], two_off, three_off], [held.at[k] for k in range(4)], sems)
    z = lax.axis_index("tensor")
    for k, load in enumerate(loads):
        load.wait()
        out_ref[z ^ k] = unfold(held[k])


def prepare_body(cot_ref, act_ref, got_ref, x_got, y_got, _, sum_ref, cot, held, got, x_in, y_in, sems):
    half = cot.shape[1] // 2
    share = held.shape[1]
    start = pl.multiple_of(lax.axis_index("dp") * share, share)
    loads = start_all(
        [cot_ref, act_ref.at[:, pl.ds(start, share)], got_ref.at[0], x_got.at[1], y_got.at[1]],
        [cot, held, got, x_in, y_in],
        sems,
    )
    loads[0].wait()
    left = cot[...].astype(f32).T.astype(bf16)
    loads[1].wait()
    product = jnp.dot(left, held[...], preferred_element_type=f32)
    for load in loads[2:]:
        load.wait()
    total = product + got[...]
    sum_ref[:half] = total[:half] + decode(x_in)
    sum_ref[half:] = total[half:] + decode(y_in)


def finish_body(*refs):
    sources, step_out = refs[:6], refs[6]
    held, (step, sems, out_sems) = refs[7:13], refs[13:]
    loads = start_all([source.at[pl.ds(0, 2)] for source in sources[:2]] + list(sources[2:]), held, sems)
    near, far, g_inverse, total, x_in, y_in = held
    half = total.shape[0] // 2
    odd = lax.axis_index("tensor") % 2
    width = FACTOR_BLOCK
    for load in loads[:2]:
        load.wait()
    inverses = [[unfold(part[p]) for part in (near, far)] for p in range(2)]
    for load in loads[2:]:
        load.wait()
    total[:half] += decode(y_in)
    total[half:] += decode(x_in)
    right = wide_dot(g_inverse[...], total[...], (((0,), (0,)), ((), ())))
    stores = []
    for p in range(2):
        block = right[:, p * width : (p + 1) * width], right[:, (p + 2) * width : (p + 3) * width]
        for k in range(2):
            at = odd if k == 0 else 1 - odd
            chosen = jnp.where(at == 0, block[0], block[1])
            step[2 * p + k] = wide_dot(inverses[p][k], chosen, (((1,), (1,)), ((), ())))
            start = pl.multiple_of((2 * at + p) * width, width)
            stores += start_all([step.at[2 * p + k]], [step_out.at[pl.ds(start, width), :]], out_sems, 2 * p + k)
    for store in stores:
        store.wait()


def square_device(activations, cotangent, sampled_rows, block_owner):
    tok_local, model_width = activations.shape
    group_w = cotangent.shape[1]
    dp_count = lax.axis_size("dp")
    depth = lax.axis_size("tensor")
    samples = sampled_rows.shape[0]
    row_share = model_width // dp_count
    half = group_w // 2

    def swap(block, bit, axis="dp"):
        count = lax.axis_size(axis)
        return lax.ppermute(block, axis, [(i, i ^ bit) for i in range(count)])

    theirs, own_theirs, picked = project(
        block_owner, sampled_rows, cotangent, activations, dp_count
    )
    got = swap(theirs, CORE)
    rows = lax.all_to_all(picked, "dp", split_axis=0, concat_axis=0, tiled=True)
    own_got = swap(own_theirs, CORE)

    def dma(count):
        return pltpu.SemaphoreType.DMA((count,))

    cot_vmem = pltpu.VMEM(cotangent.shape, bf16)
    three = len(MASKS) - 1
    wired = (fold_rows(half), row_share)
    piece = shaped((half, row_share))
    x_first, y_first, x_b, y_a = call(
        sum_body,
        "sum_cores",
        (shaped((2, *wired), bf16),) * 2 + (piece,) * 2,
        [ANY] * 3,
        (ANY,) * 4,
        [
            cot_vmem,
            pltpu.VMEM((three, tok_local, row_share), bf16),
            pltpu.VMEM((three, group_w, row_share), f32),
            pltpu.VMEM((group_w, tok_local), bf16),
            pltpu.VMEM((2 * three, *wired), bf16),
            pltpu.VMEM((2, half, row_share), f32),
            dma(1 + three),
            dma(three),
            dma(2 * three),
        ],
        moved=9 * MIB,
    )(cotangent, activations, got)
    x_got, y_got = swap(x_first, NEAR_X), swap(y_first, NEAR_Y)

    scales = (1.0 / (samples * dp_count), tok_local / samples)
    packed = (FACTOR_BLOCK // 2 + FOLD_ROWS, FACTOR_BLOCK)
    inverses, own, g_inverse = call(
        functools.partial(invert_body, scales),
        "invert_factors",
        (shaped((3, *packed)), shaped(packed), shaped((FACTOR_BLOCK, FACTOR_BLOCK))),
        [SMEM, VMEM, ANY, ANY],
        (VMEM,) * 3,
        flops=2 * 3 * 4 * 18 * FACTOR_BLOCK**3,
        moved=2 * MIB,
    )(block_owner, rows.reshape(-1, rows.shape[-1]), x_b, own_got)
    beside = swap(inverses, 1, "tensor")
    two_off, three_off = swap(own, 2, "tensor"), swap(own, 3, "tensor")

    piece_vmem = pltpu.VMEM((half, row_share), f32)
    wired_vmem = pltpu.VMEM(wired, bf16)
    x_last, y_last = call(
        hop_body,
        "hop",
        (shaped(wired, bf16),) * 2,
        [ANY] * 5,
        (ANY,) * 2,
        [piece_vmem] * 2 + [wired_vmem] * 4 + [dma(4), dma(2)],
    )(x_b, y_a, x_got, y_got, inverses)
    hopped = x_last
    x_last, y_last = swap(x_last, NEAR_X), swap(y_last, NEAR_Y)

    total = pltpu.VMEM((group_w, row_share), f32)
    square = (depth, FACTOR_BLOCK, FACTOR_BLOCK)
    owned = call(
        owned_body, "owned", shaped(square), [ANY] * 5, VMEM, [pltpu.VMEM((4, *packed), f32), dma(4)]
    )(inverses, beside, two_off, three_off, hopped)
    so_far = call(
        prepare_body,
        "prepare",
        shaped((group_w, row_share)),
        [ANY] * 6,
        VMEM,
        [cot_vmem, pltpu.VMEM((tok_local, row_share), bf16), total, wired_vmem, wired_vmem, dma(5)],
        flops=PREPARE_FLOPS,
    )(cotangent, activations, own_got, x_got, y_got, owned)
    step = call(
        finish_body,
        "finish",
        shaped((row_share, group_w)),
        [ANY] * 6,
        ANY,
        [pltpu.VMEM((2, *packed), f32)] * 2
        + [pltpu.VMEM((FACTOR_BLOCK, FACTOR_BLOCK), f32), total, wired_vmem, wired_vmem]
        + [pltpu.VMEM(square, f32), dma(6), dma(depth)],
        moved=6 * MIB,
    )(inverses, beside, g_inverse, so_far, x_last, y_last)
    return step, owned


def solution(mesh):
    def per_device(activations, cotangent, sampled_rows, block_owner):
        block_total = activations.shape[1] // FACTOR_BLOCK
        dp_count, depth = mesh.shape["dp"], mesh.shape["tensor"]
        fits = (
            dp_count == 8
            and depth == 4
            and block_total == dp_count * depth
            and cotangent.shape[1] == FACTOR_BLOCK
            and sampled_rows.shape[0] % 16 == 0
            and activations.shape[0] % 128 == 0
        )
        run = square_device if fits else general_device
        return run(activations, cotangent, sampled_rows, block_owner)

    return jax.shard_map(
        per_device,
        mesh=mesh,
        in_specs=(P("dp", None), P("dp", "tensor"), P("dp"), P()),
        out_specs=(P("dp", "tensor"), P("dp", None, None)),
        check_vma=False,
    )
```

```python
import functools

import jax
import jax.numpy as jnp
from jax import lax
from jax.experimental import pallas as pl
from jax.experimental.pallas import tpu as pltpu
from jax.sharding import PartitionSpec as P

S_DEV = 64
FACTOR_BLOCK = 256
ITERS = 10


DAMPING = 0.05
precise_mode = lax.Precision.HIGHEST
f32 = jnp.float32
bf16 = jnp.bfloat16


def block_rank(block_owner):
    block_total = block_owner.shape[0]
    same_owner = block_owner[:, None] == block_owner[None, :]
    positions = jnp.arange(block_total, dtype=jnp.int32)
    before = positions[None, :] < positions[:, None]
    return jnp.sum((same_owner & before).astype(jnp.int32), axis=1)


def from_partner(block, axis, apart):
    count = lax.axis_size(axis)
    route = []
    for low in range(count):
        high = low | 1 << apart
        if high != low and high < count:
            route += [(low, high), (high, low)]
    return lax.ppermute(block, axis, route)


def newton_inverse(matrix):
    extent = matrix.shape[-1]
    identity = jnp.eye(extent, dtype=jnp.float32)
    row_bound = jnp.max(jnp.sum(jnp.abs(matrix), axis=2), axis=1)
    initial = identity[None, :, :] / row_bound[:, None, None]

    def advance(turn_index, current):
        product = jnp.einsum("nij,njk->nik", matrix, current, precision=precise_mode)
        return jnp.einsum(
            "nij,njk->nik", current, 2.0 * identity[None, :, :] - product, precision=precise_mode
        )

    return lax.fori_loop(0, ITERS, advance, initial)


def owner_grams(received):
    return jnp.einsum("pcsk,pcsl->ckl", received, received, preferred_element_type=jnp.float32)


def general_device(activations, cotangent, sampled_rows, block_owner):
    tok_local = activations.shape[0]
    model_width = activations.shape[1]
    group_w = cotangent.shape[1]
    dp_count = lax.axis_size("dp")
    my_dp = lax.axis_index("dp")
    block_total = model_width // FACTOR_BLOCK
    capacity = max(1, block_total // dp_count)
    row_share = model_width // dp_count
    samples_all = S_DEV * dp_count
    grad_rows = lax.psum_scatter(
        lax.dot_general(
            activations, cotangent, (((0,), (0,)), ((), ())), preferred_element_type=jnp.float32
        ),
        "dp",
        scatter_dimension=0,
        tiled=True,
    )
    picked_acts = jnp.take(activations, sampled_rows, axis=0)
    picked_grads = jnp.take(cotangent, sampled_rows, axis=0)
    g_partial = lax.dot_general(
        picked_grads, picked_grads, (((0,), (0,)), ((), ())), preferred_element_type=jnp.float32
    )
    g_total = lax.psum(g_partial, "dp")
    g_factor = g_total * (tok_local / S_DEV) + DAMPING * jnp.eye(group_w, dtype=jnp.float32)
    slot_of = block_owner * capacity + block_rank(block_owner)
    dest_ids = jnp.arange(dp_count * capacity, dtype=jnp.int32)
    chooser = (slot_of[None, :] == dest_ids[:, None]).astype(jnp.bfloat16)
    row_blocks = picked_acts.reshape(S_DEV, block_total, FACTOR_BLOCK)
    outgoing = lax.dot_general(
        chooser, row_blocks, (((1,), (1,)), ((), ())), preferred_element_type=jnp.float32
    )
    outgoing = outgoing.astype(jnp.bfloat16).reshape(dp_count, capacity, S_DEV, FACTOR_BLOCK)
    gram_slots = owner_grams(
        lax.all_to_all(outgoing, "dp", split_axis=0, concat_axis=0, tiled=True)
    )
    a_factor = (
        gram_slots / samples_all + DAMPING * jnp.eye(FACTOR_BLOCK, dtype=jnp.float32)[None, :, :]
    )
    input_factor_inverse = newton_inverse(a_factor)
    owned_count = jnp.sum((block_owner == my_dp).astype(jnp.int32))
    slot_used = jnp.arange(capacity, dtype=jnp.int32) < owned_count
    owned_out = jnp.where(slot_used[:, None, None], input_factor_inverse, 0.0)
    g_inverse = newton_inverse(g_factor[None, :, :])[0]
    per_dev = max(1, row_share // FACTOR_BLOCK)
    rows_each = min(row_share, FACTOR_BLOCK)
    first_block = my_dp * row_share // FACTOR_BLOCK
    need_ids = first_block + jnp.arange(per_dev, dtype=jnp.int32)
    need_slots = jnp.take(slot_of, need_ids)
    row_offset = my_dp * row_share % FACTOR_BLOCK
    shard_piece = lax.all_gather(owned_out, "dp", axis=0, tiled=True)
    rows_part = lax.dynamic_slice_in_dim(shard_piece, row_offset, rows_each, 1)
    slot_ids = jnp.arange(shard_piece.shape[0], dtype=jnp.int32)
    selector = (need_slots[:, None] == slot_ids[None, :]).astype(jnp.float32)
    inverse_rows = jnp.einsum("jm,mkl->jkl", selector, rows_part, precision=precise_mode)
    grad_right = jnp.dot(
        grad_rows, g_inverse, precision=precise_mode, preferred_element_type=jnp.float32
    )
    if row_share < FACTOR_BLOCK:
        partner = from_partner(grad_right, "dp", 0)
        is_lower = my_dp % 2 == 0
        joined = jnp.where(
            is_lower,
            jnp.concatenate([grad_right, partner], 0),
            jnp.concatenate([partner, grad_right], 0),
        )
        complete_rows = joined[None, :, :]
    else:
        complete_rows = grad_right.reshape(per_dev, FACTOR_BLOCK, group_w)
    natural_step = jnp.einsum("jrk,jkl->jrl", inverse_rows, complete_rows, precision=precise_mode)
    return (natural_step.reshape(row_share, group_w), owned_out)


MIB = 1 << 20
VMEM_MIB = 64
AHEAD = 3
PROJECT_AHEAD = 6
HOP_PARTS = 2
SUM_PARTS = 2
OWNED_FLOPS = 20_000_000_000
ANY = pl.BlockSpec(memory_space=pl.ANY)
VMEM = pl.BlockSpec(memory_space=pltpu.VMEM)
SMEM = pl.BlockSpec(memory_space=pltpu.SMEM)
CORE, NEAR_X, NEAR_Y, FAR = 1, 2, 4, 6


def routes(me):
    first = jnp.where(me % 2 == 0, NEAR_X, NEAR_Y)
    return FAR, first, FAR - first, 0


def shaped(shape, dtype=f32):
    return jax.ShapeDtypeStruct(shape, dtype)


def call(body, name, out_shape, in_specs, out_specs, scratch=(), flops=0, moved=0):
    return pl.pallas_call(
        body,
        out_shape=out_shape,
        in_specs=in_specs,
        out_specs=out_specs,
        scratch_shapes=scratch,
        compiler_params=pltpu.CompilerParams(vmem_limit_bytes=VMEM_MIB * MIB),
        cost_estimate=pl.CostEstimate(flops=flops, bytes_accessed=moved, transcendentals=0),
        name=name,
    )


def start_all(sources, targets, sems, first=0):
    copies = [
        pltpu.make_async_copy(source, target, sems.at[first + i])
        for i, (source, target) in enumerate(zip(sources, targets))
    ]
    for copy in copies:
        copy.start()
    return copies


def fold_rows(rows):
    return rows + rows // 2


def encode(x, into):
    rows = x.shape[0]
    high = x.astype(bf16)
    into[:rows] = high
    base = high.astype(f32)
    left = (x - base) * pl.reciprocal(base, approx=True) * 256.0
    left = jnp.where(jnp.abs(base) < 1e-30, 0.0, jnp.clip(left, -1.0, 1.0))
    digit = jnp.floor(left * 63.5 + 64.0)
    first, second = digit[: rows // 2], digit[rows // 2 :]
    negative = second >= 64.0
    power = jnp.exp2(jnp.where(negative, second - 96.0, second - 32.0))
    packed = (first + 128.0) * power
    into[rows:] = jnp.where(negative, -packed, packed).astype(bf16)


def decode(ref):
    rows = ref.shape[0] * 2 // 3
    packed = ref[rows:].astype(f32)
    size = jnp.abs(packed)
    power = jnp.floor(jnp.log2(size) + 1e-3)
    first = jnp.floor(size * jnp.exp2(7.0 - power) + 0.5) - 128.0
    second = power + jnp.where(packed < 0.0, 89.0, 25.0)
    digit = jnp.concatenate([first, second], axis=0)
    base = ref[:rows].astype(f32)
    return base + base * ((digit - 63.5) * (1.0 / (63.5 * 256.0)))


def project_body(
    owner, rows_ref, cot_ref, act_ref, theirs, own_theirs, out_ref,
    held, cot, rows, left, grads, picks, slots, sems, out_sems, small_sems, pick_sems,
):
    count, tokens, share = held.shape
    group_w = cot.shape[1]
    samples = rows.shape[1]
    per_tile = share // FACTOR_BLOCK
    me = lax.axis_index("dp")
    z = lax.axis_index("tensor")
    half = count // 2
    tiles = [me ^ m ^ CORE for m in routes(me ^ CORE)] + [me ^ m for m in routes(me)]
    targets = [theirs.at[i] for i in range(half - 1)] + [own_theirs.at[0]]

    small = start_all([cot_ref, rows_ref], [cot, rows], small_sems)
    starts = [pl.multiple_of(t * share, share) for t in tiles]
    loads = [
        pltpu.make_async_copy(act_ref.at[:, pl.ds(start, share)], held.at[i], sems.at[i])
        for i, start in enumerate(starts)
    ]
    for load in loads[:PROJECT_AHEAD]:
        load.start()

    for d in range(count):
        slots[0, d] = 0
        slots[1, d] = 0
    for b in range(owner.shape[0]):
        holder = owner[b]
        rank = slots[0, holder]
        slots[0, holder] = rank + 1
        slots[1, holder] = jnp.where(rank == z, b, slots[1, holder])

    for copy in small:
        copy.wait()
    left[:group_w] = cot[...].astype(f32).T.astype(bf16)
    places = lax.broadcasted_iota(jnp.int32, (tokens, samples), 0)
    left[group_w:] = (places == rows[...]).astype(f32).T.astype(bf16)

    blocks = count * per_tile
    picks[blocks] = jnp.dot(left[group_w:], cot[...], preferred_element_type=f32).astype(bf16)
    stores = []

    def pass_on(block, many, dest, place, n):
        return start_all([picks.at[pl.ds(block, many)]], [out_ref.at[dest, pl.ds(place, many)]], pick_sems, n)

    for d in range(count):
        stores += pass_on(blocks, 1, d, 3, 3 * d + 2)
    for i in range(count):
        if i % 2 == 0:
            loads[i].wait()
            loads[i + 1].wait()
            for load in loads[i + PROJECT_AHEAD : i + PROJECT_AHEAD + 2]:
                load.start()
        if i < half:
            product = jnp.dot(left[...], held[i], preferred_element_type=f32)
            grads[i] = product[:group_w]
            stores += start_all([grads.at[i]], [targets[i]], out_sems, i)
            picked = product[group_w:]
        else:
            picked = jnp.dot(left[group_w:], held[i], preferred_element_type=f32)
        for j in range(per_tile):
            picks[tiles[i] * per_tile + j] = picked[
                :, j * FACTOR_BLOCK : (j + 1) * FACTOR_BLOCK
            ].astype(bf16)
        stores += pass_on(tiles[i] * per_tile + 2 * (z % 2), 2, tiles[i], 0, 3 * i)
    for d in range(count):
        stores += pass_on(slots[1, d], 1, d, 2, 3 * d + 1)
    for store in stores:
        store.wait()


def project(block_owner, sampled_rows, cotangent, activations, count):
    samples = sampled_rows.shape[0]
    tokens, group_w = cotangent.shape
    model_width = activations.shape[1]
    share = model_width // count
    one = shaped((1, group_w, share))
    rest = shaped((count // 2 - 1, group_w, share))
    return call(
        project_body,
        "project",
        (rest, one, shaped((count, 4, samples, FACTOR_BLOCK), bf16)),
        [SMEM, ANY, ANY, ANY],
        (ANY,) * 3,
        [
            pltpu.VMEM((count, tokens, share), bf16),
            pltpu.VMEM((tokens, group_w), bf16),
            pltpu.VMEM((1, samples), jnp.int32),
            pltpu.VMEM((group_w + samples, tokens), bf16),
            pltpu.VMEM((count // 2, group_w, share), f32),
            pltpu.VMEM((model_width // FACTOR_BLOCK + 1, samples, FACTOR_BLOCK), bf16),
            pltpu.SMEM((2, count), jnp.int32),
            pltpu.SemaphoreType.DMA((count,)),
            pltpu.SemaphoreType.DMA((count // 2,)),
            pltpu.SemaphoreType.DMA((2,)),
            pltpu.SemaphoreType.DMA((3 * count,)),
        ],
        flops=2 * tokens * (group_w + samples) * model_width,
        moved=2 * tokens * model_width + 2 * group_w * model_width,
    )(block_owner, sampled_rows[None, :], cotangent, activations)


def sum_body(which, cot_ref, act_ref, got_ref, *refs):
    count = len(which)
    outs, (cot, held, got, left, wire, plain, sems, got_sems, out_sems) = refs[-9 - count : -9], refs[-9:]
    width = held.shape[2]
    share = got_ref.shape[2]
    parts = share // width
    me = lax.axis_index("dp")
    starts = [pl.multiple_of((me ^ routes(me)[i]) * share, share) for i in which]
    work = [(i, p) for i in range(count) for p in range(parts)]
    first = start_all([cot_ref], [cot], sems)[0]

    def fetch(n):
        i, p = work[n]
        tile = act_ref.at[:, pl.ds(starts[i] + p * width, width)]
        come = got_ref.at[which[i], :, pl.ds(p * width, width)]
        return start_all([tile], [held.at[n]], sems, 1 + n) + start_all([come], [got.at[n]], got_sems, n)

    loads = [fetch(n) for n in range(min(AHEAD, len(work)))]
    first.wait()
    left[...] = cot[...].astype(f32).T.astype(bf16)
    stores = []
    for n, (i, p) in enumerate(work):
        loads[n][0].wait()
        if n + AHEAD < len(work):
            loads.append(fetch(n + AHEAD))
        product = jnp.dot(left[...], held[n], preferred_element_type=f32)
        loads[n][1].wait()
        if which[i] < 2:
            encode(product + got[n], wire.at[n])
            source = wire.at[n]
        else:
            plain[p] = product + got[n]
            source = plain.at[p]
        stores += start_all([source], [outs[i].at[:, pl.ds(p * width, width)]], out_sems, n)
    for store in stores:
        store.wait()


def hop_body(rest, come, _, out_ref, rest_in, come_in, out, sems, out_sems):
    parts = rest_in.shape[0]
    width = rest_in.shape[2]
    loads, stores = [], []
    for p in range(parts):
        columns = pl.ds(p * width, width)
        loads.append(start_all([rest.at[:, columns], come.at[:, columns]], [rest_in.at[p], come_in.at[p]], sems, 2 * p))
    for p in range(parts):
        for load in loads[p]:
            load.wait()
        encode(rest_in[p] + decode(come_in.at[p]), out.at[p])
        stores += start_all([out.at[p]], [out_ref.at[:, pl.ds(p * width, width)]], out_sems, p)
    for store in stores:
        store.wait()


def two(x):
    high = x.astype(bf16)
    return high, (x - high.astype(f32)).astype(bf16)


def newton_step(low, current, last):
    width = low.shape[0]
    high_part, low_part = two(low)

    def dot(a, b):
        return jnp.dot(a, b, preferred_element_type=f32)

    if current is None:
        mixed = dot(high_part, low_part)
        return 2.0 * low - (dot(high_part, high_part) + (mixed + mixed.T)), None
    current_high, current_low = two(current)
    if last:
        both = dot(jnp.concatenate([current_high, current_low], axis=0), high_part)
        return None, 2.0 * current - (both[:width] + (both[width:] + dot(current_high, low_part)))
    both = dot(jnp.concatenate([current_high, high_part, current_low], axis=0), high_part)
    mixed = dot(jnp.concatenate([current_high, high_part], axis=0), low_part)
    square = both[width : 2 * width] + (mixed[width:] + mixed[width:].T)
    return 2.0 * low - square, 2.0 * current - (both[:width] + (both[2 * width :] + mixed[:width]))


def places(extent):
    return (
        lax.broadcasted_iota(jnp.int32, (extent, extent), 0),
        lax.broadcasted_iota(jnp.int32, (extent, extent), 1),
    )


FOLD_ROWS = 16


def fold(matrix, into):
    half = matrix.shape[0] // 2
    row, column = places(half)
    low = matrix[half:, half:]
    both = jnp.where(row <= column, matrix[:half, :half], low)
    coded = fold_rows(half)
    encode(jnp.concatenate([both, matrix[:half, half:]], axis=1), into.at[:coded])
    left = jnp.sum(jnp.where(row == column, low, 0.0), axis=0, keepdims=True)
    line = lax.broadcasted_iota(jnp.int32, (FOLD_ROWS, 2 * half), 0)
    diagonal = jnp.zeros((FOLD_ROWS, 2 * half), f32)
    for part in range(3):
        high = left.astype(bf16).astype(f32)
        diagonal = jnp.where(line == part, jnp.concatenate([high, high], axis=1), diagonal)
        left = left - high
    into[coded:] = diagonal.astype(bf16)


def unfold(packed):
    half = packed.shape[1] // 2
    coded = fold_rows(half)
    row, column = places(half)
    values = decode(packed.at[:coded])
    diagonal = jnp.sum(packed[coded:].astype(f32), axis=0, keepdims=True)[:, :half]
    both, corner = values[:, :half], values[:, half:]
    turned = both.T
    top = jnp.where(row <= column, both, turned)
    low = jnp.where(row == column, diagonal, jnp.where(row > column, both, turned))
    return jnp.concatenate(
        [jnp.concatenate([top, corner], axis=1), jnp.concatenate([corner.T, low], axis=1)], axis=0
    )


def invert_body(scales, owner, rows_ref, _, all_ref, own_ref, out_ref):
    width = FACTOR_BLOCK
    me = lax.axis_index("dp")
    owned = jnp.int32(0)
    for b in range(owner.shape[0]):
        owned = owned + jnp.where(owner[b] == me, 1, 0)
    used = jnp.where(lax.axis_index("tensor") < owned, 1.0, 0.0).astype(f32)
    row, column = places(width)
    eye = (row == column).astype(f32)
    states = []
    for m in range(4):
        rows = rows_ref[:, m].reshape(-1, width)
        gram = lax.dot_general(
            rows, rows, (((0,), (0,)), ((), ())), preferred_element_type=f32
        )
        matrix = gram * scales[1 if m == 3 else 0] + DAMPING * eye
        bound = jnp.max(jnp.sum(jnp.abs(matrix), axis=1, keepdims=True), axis=0, keepdims=True)
        inverse_bound = 1.0 / bound
        low = matrix * inverse_bound
        states.append((low, (2.0 * eye - low) * inverse_bound))
    lows = [newton_step(low, None, False)[0] for low, _ in states]
    currents = [current for _, current in states]
    for turn in range(1, ITERS):
        stepped = [newton_step(low, current, turn == ITERS - 1) for low, current in zip(lows, currents)]
        lows, currents = [pair[0] for pair in stepped], [pair[1] for pair in stepped]
    fold(currents[0], all_ref.at[0])
    fold(currents[1], all_ref.at[1])
    fold(currents[2] * used, all_ref.at[2])
    own_ref[...] = all_ref[2]
    out_ref[...] = currents[3]


def owned_body(here, beside, two_off, three_off, _, out_ref, split, held, need, sems, need_sems):
    needs = start_all([here.at[pl.ds(0, 2)], beside.at[pl.ds(0, 2)]], [need.at[pl.ds(0, 2)], need.at[pl.ds(2, 2)]], need_sems)
    loads = start_all([here.at[2], beside.at[2], two_off, three_off], [held.at[k] for k in range(4)], sems)
    z = lax.axis_index("tensor")
    odd = z % 2
    for k in range(2):
        needs[k].wait()
        for p in range(2):
            high, low = two(unfold(need.at[2 * k + p]))
            at = 2 * (odd if k == 0 else 1 - odd) + p
            split[0, at] = high
            split[1, at] = low
    for k, load in enumerate(loads):
        load.wait()
        out_ref[z ^ k] = unfold(held.at[k])


def own_body(cot_ref, act_ref, got_ref, _, sum_ref, cot, held, got, sems):
    share = held.shape[1]
    start = pl.multiple_of(lax.axis_index("dp") * share, share)
    loads = start_all([cot_ref, act_ref.at[:, pl.ds(start, share)], got_ref.at[0]], [cot, held, got], sems)
    loads[0].wait()
    left = cot[...].astype(f32).T.astype(bf16)
    loads[1].wait()
    product = jnp.dot(left, held[...], preferred_element_type=f32)
    loads[2].wait()
    sum_ref[...] = product + got[...]


def near_body(own_ref, come, _, sum_ref, own, come_in, sems):
    loads = start_all([own_ref, come], [own, come_in], sems)
    for load in loads:
        load.wait()
    sum_ref[...] = own[...] + decode(come_in)


def finish_body(split_ref, g_ref, sum_ref, come, step_out, split, g_in, total, come_in, step, sems, out_sems):
    width = FACTOR_BLOCK
    loads = start_all([g_ref, come, sum_ref, split_ref], [g_in, come_in, total, split], sems)

    def dot(a, c, dims):
        return lax.dot_general(a, c, (dims, ((), ())), preferred_element_type=f32)

    loads[0].wait()
    left = jnp.concatenate([part.astype(f32).T for part in two(g_in[...])], axis=0).astype(bf16)
    for load in loads[1:3]:
        load.wait()
    sum_high, sum_low = two(total[...] + decode(come_in))
    both = dot(left, sum_high, ((1,), (0,)))
    right_high, right_low = two(both[:width] + (both[width:] + dot(left[:width], sum_low, ((1,), (0,)))))
    loads[3].wait()
    stores = []
    for b in range(split.shape[1]):
        part = slice(b * width, (b + 1) * width)
        both = dot(split[:, b].reshape(2 * width, width), right_high[:, part], ((1,), (1,)))
        step[b] = both[:width] + (both[width:] + dot(split[0, b], right_low[:, part], ((1,), (1,))))
        stores += start_all([step.at[b]], [step_out.at[part, :]], out_sems, b)
    for store in stores:
        store.wait()


def dma(count):
    return pltpu.SemaphoreType.DMA((count,))


def sum_cores(name, which, cotangent, activations, got, *after):
    tokens, group_w = cotangent.shape
    share = got.shape[2]
    wired = (fold_rows(group_w), share)
    steps, width = len(which) * SUM_PARTS, share // SUM_PARTS
    return call(
        functools.partial(sum_body, which),
        name,
        tuple(shaped(wired, bf16) if i < 2 else shaped((group_w, share)) for i in which),
        [ANY] * (3 + len(after)),
        (ANY,) * len(which),
        [
            pltpu.VMEM(cotangent.shape, bf16),
            pltpu.VMEM((steps, tokens, width), bf16),
            pltpu.VMEM((steps, group_w, width), f32),
            pltpu.VMEM((group_w, tokens), bf16),
            pltpu.VMEM((steps, wired[0], width), bf16),
            pltpu.VMEM((SUM_PARTS, group_w, width), f32),
            dma(1 + steps),
            dma(steps),
            dma(steps),
        ],
        moved=4 * MIB * len(which),
    )(cotangent, activations, got, *after)


def invert(block_owner, rows, after, scales):
    packed = shaped((fold_rows(FACTOR_BLOCK // 2) + FOLD_ROWS, FACTOR_BLOCK), bf16)
    return call(
        functools.partial(invert_body, scales),
        "invert_factors",
        (shaped((3, *packed.shape), bf16), packed, shaped((FACTOR_BLOCK, FACTOR_BLOCK))),
        [SMEM, VMEM, ANY],
        (VMEM,) * 3,
        flops=2 * 3 * 4 * 18 * FACTOR_BLOCK**3,
        moved=2 * MIB,
    )(block_owner, rows, after)


def hop(rest, come, after):
    group_w, share = rest.shape
    wired = come.shape
    width = share // HOP_PARTS
    return call(
        hop_body,
        "hop",
        shaped(wired, bf16),
        [ANY] * 3,
        ANY,
        [pltpu.VMEM((HOP_PARTS, group_w, width), f32)]
        + [pltpu.VMEM((HOP_PARTS, wired[0], width), bf16)] * 2
        + [dma(2 * HOP_PARTS), dma(HOP_PARTS)],
    )(rest, come, after)


def sum_own(cotangent, activations, own_got, after):
    tokens = cotangent.shape[0]
    _, group_w, share = own_got.shape
    return call(
        own_body,
        "sum_own",
        shaped((group_w, share)),
        [ANY] * 4,
        VMEM,
        [
            pltpu.VMEM(cotangent.shape, bf16),
            pltpu.VMEM((tokens, share), bf16),
            pltpu.VMEM((group_w, share), f32),
            dma(3),
        ],
    )(cotangent, activations, own_got, after)


def add_near(own, come, after):
    return call(
        near_body,
        "add_near",
        shaped(own.shape),
        [ANY] * 3,
        VMEM,
        [pltpu.VMEM(own.shape, f32), pltpu.VMEM(come.shape, bf16), dma(2)],
    )(own, come, after)


def owned_blocks(inverses, beside, two_off, three_off, after):
    square = (4, FACTOR_BLOCK, FACTOR_BLOCK)
    held = pltpu.VMEM((4, *two_off.shape), bf16)
    return call(
        owned_body,
        "owned",
        (shaped(square), shaped((2, *square), bf16)),
        [ANY] * 5,
        (VMEM,) * 2,
        [held, held, dma(4), dma(2)],
        flops=OWNED_FLOPS,
    )(inverses, beside, two_off, three_off, after)


def finish(split, g_inverse, so_far, come):
    group_w, share = so_far.shape
    blocks = share // FACTOR_BLOCK
    return call(
        finish_body,
        "finish",
        shaped((share, group_w)),
        [ANY] * 4,
        ANY,
        [
            pltpu.VMEM(split.shape, bf16),
            pltpu.VMEM(g_inverse.shape, f32),
            pltpu.VMEM(so_far.shape, f32),
            pltpu.VMEM(come.shape, bf16),
            pltpu.VMEM((blocks, FACTOR_BLOCK, group_w), f32),
            dma(4),
            dma(blocks),
        ],
        moved=6 * MIB,
    )(split, g_inverse, so_far, come)


def square_device(activations, cotangent, sampled_rows, block_owner):
    dp_count = lax.axis_size("dp")
    samples = sampled_rows.shape[0]

    def swap(block, bit, axis="dp"):
        count = lax.axis_size(axis)
        return lax.ppermute(block, axis, [(i, i ^ bit) for i in range(count)])

    def travel(block, even, odd):
        return lax.ppermute(block, "dp", [(i, i ^ (odd if i % 2 else even)) for i in range(dp_count)])

    theirs, own_theirs, picked = project(
        block_owner, sampled_rows, cotangent, activations, dp_count
    )
    got = swap(theirs, CORE)
    rows = lax.all_to_all(picked, "dp", split_axis=0, concat_axis=0, tiled=True)
    own_got = swap(own_theirs, CORE)

    (far,) = sum_cores("sum_far", (0,), cotangent, activations, got)
    far_come = travel(far, NEAR_X, NEAR_Y)
    near, rest = sum_cores("sum_near", (1, 2), cotangent, activations, got, far)
    near_come = travel(near, NEAR_X, NEAR_Y)
    own_sum = sum_own(cotangent, activations, own_got, rest)

    scales = (1.0 / (samples * dp_count), activations.shape[0] / samples)
    inverses, own, g_inverse = invert(block_owner, rows, own_sum, scales)
    beside = swap(inverses, 1, "tensor")
    two_off, three_off = swap(own, 2, "tensor"), swap(own, 3, "tensor")

    hopped = hop(rest, far_come, inverses)
    come_last = travel(hopped, NEAR_Y, NEAR_X)

    so_far = add_near(own_sum, near_come, hopped)
    owned, split = owned_blocks(inverses, beside, two_off, three_off, so_far)
    step = finish(split, g_inverse, so_far, come_last)
    return step, owned


def solution(mesh):
    def per_device(activations, cotangent, sampled_rows, block_owner):
        block_total = activations.shape[1] // FACTOR_BLOCK
        dp_count, depth = mesh.shape["dp"], mesh.shape["tensor"]
        fits = (
            dp_count == 8
            and depth == 4
            and block_total == dp_count * depth
            and cotangent.shape[1] == FACTOR_BLOCK
            and sampled_rows.shape[0] % 16 == 0
            and activations.shape[0] % 128 == 0
        )
        run = square_device if fits else general_device
        return run(activations, cotangent, sampled_rows, block_owner)

    return jax.shard_map(
        per_device,
        mesh=mesh,
        in_specs=(P("dp", None), P("dp", "tensor"), P("dp"), P()),
        out_specs=(P("dp", "tensor"), P("dp", None, None)),
        check_vma=False,
    )
```

```python
import functools

import jax
import jax.numpy as jnp
from jax import lax
from jax.experimental import pallas as pl
from jax.experimental.pallas import tpu as pltpu
from jax.sharding import PartitionSpec as P

S_DEV = 64
FACTOR_BLOCK = 256
ITERS = 10


DAMPING = 0.05
precise_mode = lax.Precision.HIGHEST
f32 = jnp.float32
bf16 = jnp.bfloat16


def block_rank(block_owner):
    block_total = block_owner.shape[0]
    same_owner = block_owner[:, None] == block_owner[None, :]
    positions = jnp.arange(block_total, dtype=jnp.int32)
    before = positions[None, :] < positions[:, None]
    return jnp.sum((same_owner & before).astype(jnp.int32), axis=1)


def from_partner(block, axis, apart):
    count = lax.axis_size(axis)
    route = []
    for low in range(count):
        high = low | 1 << apart
        if high != low and high < count:
            route += [(low, high), (high, low)]
    return lax.ppermute(block, axis, route)


def newton_inverse(matrix):
    extent = matrix.shape[-1]
    identity = jnp.eye(extent, dtype=jnp.float32)
    row_bound = jnp.max(jnp.sum(jnp.abs(matrix), axis=2), axis=1)
    initial = identity[None, :, :] / row_bound[:, None, None]

    def advance(turn_index, current):
        product = jnp.einsum("nij,njk->nik", matrix, current, precision=precise_mode)
        return jnp.einsum(
            "nij,njk->nik", current, 2.0 * identity[None, :, :] - product, precision=precise_mode
        )

    return lax.fori_loop(0, ITERS, advance, initial)


def owner_grams(received):
    return jnp.einsum("pcsk,pcsl->ckl", received, received, preferred_element_type=jnp.float32)


def general_device(activations, cotangent, sampled_rows, block_owner):
    tok_local = activations.shape[0]
    model_width = activations.shape[1]
    group_w = cotangent.shape[1]
    dp_count = lax.axis_size("dp")
    my_dp = lax.axis_index("dp")
    block_total = model_width // FACTOR_BLOCK
    capacity = max(1, block_total // dp_count)
    row_share = model_width // dp_count
    samples_all = S_DEV * dp_count
    grad_rows = lax.psum_scatter(
        lax.dot_general(
            activations, cotangent, (((0,), (0,)), ((), ())), preferred_element_type=jnp.float32
        ),
        "dp",
        scatter_dimension=0,
        tiled=True,
    )
    picked_acts = jnp.take(activations, sampled_rows, axis=0)
    picked_grads = jnp.take(cotangent, sampled_rows, axis=0)
    g_partial = lax.dot_general(
        picked_grads, picked_grads, (((0,), (0,)), ((), ())), preferred_element_type=jnp.float32
    )
    g_total = lax.psum(g_partial, "dp")
    g_factor = g_total * (tok_local / S_DEV) + DAMPING * jnp.eye(group_w, dtype=jnp.float32)
    slot_of = block_owner * capacity + block_rank(block_owner)
    dest_ids = jnp.arange(dp_count * capacity, dtype=jnp.int32)
    chooser = (slot_of[None, :] == dest_ids[:, None]).astype(jnp.bfloat16)
    row_blocks = picked_acts.reshape(S_DEV, block_total, FACTOR_BLOCK)
    outgoing = lax.dot_general(
        chooser, row_blocks, (((1,), (1,)), ((), ())), preferred_element_type=jnp.float32
    )
    outgoing = outgoing.astype(jnp.bfloat16).reshape(dp_count, capacity, S_DEV, FACTOR_BLOCK)
    gram_slots = owner_grams(
        lax.all_to_all(outgoing, "dp", split_axis=0, concat_axis=0, tiled=True)
    )
    a_factor = (
        gram_slots / samples_all + DAMPING * jnp.eye(FACTOR_BLOCK, dtype=jnp.float32)[None, :, :]
    )
    input_factor_inverse = newton_inverse(a_factor)
    owned_count = jnp.sum((block_owner == my_dp).astype(jnp.int32))
    slot_used = jnp.arange(capacity, dtype=jnp.int32) < owned_count
    owned_out = jnp.where(slot_used[:, None, None], input_factor_inverse, 0.0)
    g_inverse = newton_inverse(g_factor[None, :, :])[0]
    per_dev = max(1, row_share // FACTOR_BLOCK)
    rows_each = min(row_share, FACTOR_BLOCK)
    first_block = my_dp * row_share // FACTOR_BLOCK
    need_ids = first_block + jnp.arange(per_dev, dtype=jnp.int32)
    need_slots = jnp.take(slot_of, need_ids)
    row_offset = my_dp * row_share % FACTOR_BLOCK
    shard_piece = lax.all_gather(owned_out, "dp", axis=0, tiled=True)
    rows_part = lax.dynamic_slice_in_dim(shard_piece, row_offset, rows_each, 1)
    slot_ids = jnp.arange(shard_piece.shape[0], dtype=jnp.int32)
    selector = (need_slots[:, None] == slot_ids[None, :]).astype(jnp.float32)
    inverse_rows = jnp.einsum("jm,mkl->jkl", selector, rows_part, precision=precise_mode)
    grad_right = jnp.dot(
        grad_rows, g_inverse, precision=precise_mode, preferred_element_type=jnp.float32
    )
    if row_share < FACTOR_BLOCK:
        partner = from_partner(grad_right, "dp", 0)
        is_lower = my_dp % 2 == 0
        joined = jnp.where(
            is_lower,
            jnp.concatenate([grad_right, partner], 0),
            jnp.concatenate([partner, grad_right], 0),
        )
        complete_rows = joined[None, :, :]
    else:
        complete_rows = grad_right.reshape(per_dev, FACTOR_BLOCK, group_w)
    natural_step = jnp.einsum("jrk,jkl->jrl", inverse_rows, complete_rows, precision=precise_mode)
    return (natural_step.reshape(row_share, group_w), owned_out)


MIB = 1 << 20
VMEM_MIB = 64
AHEAD = 3
PROJECT_AHEAD = 6
HOP_PARTS = 2
SUM_PARTS = 2
OWNED_FLOPS = 20_000_000_000
ANY = pl.BlockSpec(memory_space=pl.ANY)
VMEM = pl.BlockSpec(memory_space=pltpu.VMEM)
SMEM = pl.BlockSpec(memory_space=pltpu.SMEM)
CORE, NEAR_X, NEAR_Y, FAR = 1, 2, 4, 6


def routes(me):
    first = jnp.where(me % 2 == 0, NEAR_X, NEAR_Y)
    return FAR, first, FAR - first, 0


def shaped(shape, dtype=f32):
    return jax.ShapeDtypeStruct(shape, dtype)


def call(body, name, out_shape, in_specs, out_specs, scratch=(), flops=0, moved=0):
    return pl.pallas_call(
        body,
        out_shape=out_shape,
        in_specs=in_specs,
        out_specs=out_specs,
        scratch_shapes=scratch,
        compiler_params=pltpu.CompilerParams(vmem_limit_bytes=VMEM_MIB * MIB),
        cost_estimate=pl.CostEstimate(flops=flops, bytes_accessed=moved, transcendentals=0),
        name=name,
    )


def start_all(sources, targets, sems, first=0):
    copies = [
        pltpu.make_async_copy(source, target, sems.at[first + i])
        for i, (source, target) in enumerate(zip(sources, targets))
    ]
    for copy in copies:
        copy.start()
    return copies


def fold_rows(rows):
    return rows + rows // 2


def encode(x, into):
    rows = x.shape[0]
    high = x.astype(bf16)
    into[:rows] = high
    base = high.astype(f32)
    left = (x - base) * pl.reciprocal(base, approx=True) * 256.0
    left = jnp.where(jnp.abs(base) < 1e-30, 0.0, jnp.clip(left, -1.0, 1.0))
    digit = jnp.floor(left * 63.5 + 64.0)
    first, second = digit[: rows // 2], digit[rows // 2 :]
    negative = second >= 64.0
    power = jnp.exp2(jnp.where(negative, second - 96.0, second - 32.0))
    packed = (first + 128.0) * power
    into[rows:] = jnp.where(negative, -packed, packed).astype(bf16)


def decode(ref):
    rows = ref.shape[0] * 2 // 3
    packed = ref[rows:].astype(f32)
    size = jnp.abs(packed)
    power = jnp.floor(jnp.log2(size) + 1e-3)
    first = jnp.floor(size * jnp.exp2(7.0 - power) + 0.5) - 128.0
    second = power + jnp.where(packed < 0.0, 89.0, 25.0)
    digit = jnp.concatenate([first, second], axis=0)
    base = ref[:rows].astype(f32)
    return base + base * ((digit - 63.5) * (1.0 / (63.5 * 256.0)))


def project_body(
    owner, rows_ref, cot_ref, act_ref, theirs, own_theirs, out_ref,
    held, cot, rows, left, grads, picks, slots, sems, out_sems, small_sems, pick_sems,
):
    count, tokens, share = held.shape
    group_w = cot.shape[1]
    samples = rows.shape[1]
    per_tile = share // FACTOR_BLOCK
    me = lax.axis_index("dp")
    z = lax.axis_index("tensor")
    half = count // 2
    tiles = [me ^ m ^ CORE for m in routes(me ^ CORE)] + [me ^ m for m in routes(me)]
    targets = [theirs.at[i] for i in range(half - 1)] + [own_theirs.at[0]]

    small = start_all([cot_ref, rows_ref], [cot, rows], small_sems)
    starts = [pl.multiple_of(t * share, share) for t in tiles]
    loads = [
        pltpu.make_async_copy(act_ref.at[:, pl.ds(start, share)], held.at[i], sems.at[i])
        for i, start in enumerate(starts)
    ]
    for load in loads[:PROJECT_AHEAD]:
        load.start()

    for d in range(count):
        slots[0, d] = 0
        slots[1, d] = 0
    for b in range(owner.shape[0]):
        holder = owner[b]
        rank = slots[0, holder]
        slots[0, holder] = rank + 1
        slots[1, holder] = jnp.where(rank == z, b, slots[1, holder])

    for copy in small:
        copy.wait()
    left[:group_w] = cot[...].astype(f32).T.astype(bf16)
    places = lax.broadcasted_iota(jnp.int32, (tokens, samples), 0)
    left[group_w:] = (places == rows[...]).astype(f32).T.astype(bf16)

    blocks = count * per_tile
    picks[blocks] = jnp.dot(left[group_w:], cot[...], preferred_element_type=f32).astype(bf16)
    stores = []

    def pass_on(block, many, dest, place, n):
        return start_all([picks.at[pl.ds(block, many)]], [out_ref.at[dest, pl.ds(place, many)]], pick_sems, n)

    for d in range(count):
        stores += pass_on(blocks, 1, d, 3, 3 * d + 2)
    for i in range(count):
        if i % 2 == 0:
            loads[i].wait()
            loads[i + 1].wait()
            for load in loads[i + PROJECT_AHEAD : i + PROJECT_AHEAD + 2]:
                load.start()
        if i < half:
            product = jnp.dot(left[...], held[i], preferred_element_type=f32)
            grads[i] = product[:group_w]
            stores += start_all([grads.at[i]], [targets[i]], out_sems, i)
            picked = product[group_w:]
        else:
            picked = jnp.dot(left[group_w:], held[i], preferred_element_type=f32)
        for j in range(per_tile):
            picks[tiles[i] * per_tile + j] = picked[
                :, j * FACTOR_BLOCK : (j + 1) * FACTOR_BLOCK
            ].astype(bf16)
        stores += pass_on(tiles[i] * per_tile + 2 * (z % 2), 2, tiles[i], 0, 3 * i)
    for d in range(count):
        stores += pass_on(slots[1, d], 1, d, 2, 3 * d + 1)
    for store in stores:
        store.wait()


def project(block_owner, sampled_rows, cotangent, activations, count):
    samples = sampled_rows.shape[0]
    tokens, group_w = cotangent.shape
    model_width = activations.shape[1]
    share = model_width // count
    one = shaped((1, group_w, share))
    rest = shaped((count // 2 - 1, group_w, share))
    return call(
        project_body,
        "project",
        (rest, one, shaped((count, 4, samples, FACTOR_BLOCK), bf16)),
        [SMEM, ANY, ANY, ANY],
        (ANY,) * 3,
        [
            pltpu.VMEM((count, tokens, share), bf16),
            pltpu.VMEM((tokens, group_w), bf16),
            pltpu.VMEM((1, samples), jnp.int32),
            pltpu.VMEM((group_w + samples, tokens), bf16),
            pltpu.VMEM((count // 2, group_w, share), f32),
            pltpu.VMEM((model_width // FACTOR_BLOCK + 1, samples, FACTOR_BLOCK), bf16),
            pltpu.SMEM((2, count), jnp.int32),
            pltpu.SemaphoreType.DMA((count,)),
            pltpu.SemaphoreType.DMA((count // 2,)),
            pltpu.SemaphoreType.DMA((2,)),
            pltpu.SemaphoreType.DMA((3 * count,)),
        ],
        flops=2 * tokens * (group_w + samples) * model_width,
        moved=2 * tokens * model_width + 2 * group_w * model_width,
    )(block_owner, sampled_rows[None, :], cotangent, activations)


def sum_body(which, cot_ref, act_ref, got_ref, *refs):
    count = len(which)
    outs, (cot, held, got, left, wire, plain, sems, got_sems, out_sems) = refs[-9 - count : -9], refs[-9:]
    width = held.shape[2]
    share = got_ref.shape[2]
    parts = share // width
    me = lax.axis_index("dp")
    starts = [pl.multiple_of((me ^ routes(me)[i]) * share, share) for i in which]
    work = [(i, p) for i in range(count) for p in range(parts)]
    first = start_all([cot_ref], [cot], sems)[0]

    def fetch(n):
        i, p = work[n]
        tile = act_ref.at[:, pl.ds(starts[i] + p * width, width)]
        come = got_ref.at[which[i], :, pl.ds(p * width, width)]
        return start_all([tile], [held.at[n]], sems, 1 + n) + start_all([come], [got.at[n]], got_sems, n)

    loads = [fetch(n) for n in range(min(AHEAD, len(work)))]
    first.wait()
    left[...] = cot[...].astype(f32).T.astype(bf16)
    stores = []
    for n, (i, p) in enumerate(work):
        loads[n][0].wait()
        if n + AHEAD < len(work):
            loads.append(fetch(n + AHEAD))
        product = jnp.dot(left[...], held[n], preferred_element_type=f32)
        loads[n][1].wait()
        if which[i] < 2:
            encode(product + got[n], wire.at[n])
            source = wire.at[n]
        else:
            plain[p] = product + got[n]
            source = plain.at[p]
        stores += start_all([source], [outs[i].at[:, pl.ds(p * width, width)]], out_sems, n)
    for store in stores:
        store.wait()


def hop_body(rest, come, _, out_ref, rest_in, come_in, out, sems, out_sems):
    parts = rest_in.shape[0]
    width = rest_in.shape[2]
    loads, stores = [], []
    for p in range(parts):
        columns = pl.ds(p * width, width)
        loads.append(start_all([rest.at[:, columns], come.at[:, columns]], [rest_in.at[p], come_in.at[p]], sems, 2 * p))
    for p in range(parts):
        for load in loads[p]:
            load.wait()
        encode(rest_in[p] + decode(come_in.at[p]), out.at[p])
        stores += start_all([out.at[p]], [out_ref.at[:, pl.ds(p * width, width)]], out_sems, p)
    for store in stores:
        store.wait()


def two(x):
    high = x.astype(bf16)
    return high, (x - high.astype(f32)).astype(bf16)


def newton_step(lows, currents, last):
    def dot(a, b):
        return jnp.dot(a, b, preferred_element_type=f32)

    parts = [two(low) for low in lows]
    next_lows, next_currents = [], []
    if not last:
        for low, (high_part, low_part) in zip(lows, parts):
            mixed = dot(high_part, low_part)
            next_lows.append(2.0 * low - (dot(high_part, high_part) + (mixed + mixed.T)))
    for current, (high_part, low_part) in zip(currents, parts):
        high, rest = two(current)
        product = dot(
            jnp.concatenate([high, rest, high], axis=1),
            jnp.concatenate([high_part, high_part, low_part], axis=0),
        )
        next_currents.append(2.0 * current - product)
    return next_lows, next_currents


def places(extent):
    return (
        lax.broadcasted_iota(jnp.int32, (extent, extent), 0),
        lax.broadcasted_iota(jnp.int32, (extent, extent), 1),
    )


FOLD_ROWS = 16


def fold(matrix, into):
    half = matrix.shape[0] // 2
    row, column = places(half)
    low = matrix[half:, half:]
    both = jnp.where(row <= column, matrix[:half, :half], low)
    coded = fold_rows(half)
    encode(jnp.concatenate([both, matrix[:half, half:]], axis=1), into.at[:coded])
    left = jnp.sum(jnp.where(row == column, low, 0.0), axis=0, keepdims=True)
    line = lax.broadcasted_iota(jnp.int32, (FOLD_ROWS, 2 * half), 0)
    diagonal = jnp.zeros((FOLD_ROWS, 2 * half), f32)
    for part in range(3):
        high = left.astype(bf16).astype(f32)
        diagonal = jnp.where(line == part, jnp.concatenate([high, high], axis=1), diagonal)
        left = left - high
    into[coded:] = diagonal.astype(bf16)


def unfold(packed):
    half = packed.shape[1] // 2
    coded = fold_rows(half)
    row, column = places(half)
    values = decode(packed.at[:coded])
    diagonal = jnp.sum(packed[coded:].astype(f32), axis=0, keepdims=True)[:, :half]
    both, corner = values[:, :half], values[:, half:]
    turned = both.T
    top = jnp.where(row <= column, both, turned)
    low = jnp.where(row == column, diagonal, jnp.where(row > column, both, turned))
    return jnp.concatenate(
        [jnp.concatenate([top, corner], axis=1), jnp.concatenate([corner.T, low], axis=1)], axis=0
    )


def inverses_of(samples, scale):
    row, column = places(FACTOR_BLOCK)
    eye = (row == column).astype(f32)
    lows, currents = [], []
    for rows in samples:
        gram = lax.dot_general(
            rows, rows, (((0,), (0,)), ((), ())), preferred_element_type=f32
        )
        matrix = gram * scale + DAMPING * eye
        bound = jnp.max(jnp.sum(jnp.abs(matrix), axis=1, keepdims=True), axis=0, keepdims=True)
        inverse_bound = 1.0 / bound
        low = matrix * inverse_bound
        lows.append(low)
        currents.append((2.0 * eye - low) * inverse_bound)
    lows = newton_step(lows, [], False)[0]
    for turn in range(1, ITERS):
        lows, currents = newton_step(lows, currents, turn == ITERS - 1)
    return currents


def invert_body(scale, owner, rows_ref, _, all_ref, own_ref, rows, sem):
    load = start_all([rows_ref.at[:, pl.ds(0, 3)]], [rows], sem)[0]
    me = lax.axis_index("dp")
    owned = jnp.int32(0)
    for b in range(owner.shape[0]):
        owned = owned + jnp.where(owner[b] == me, 1, 0)
    used = jnp.where(lax.axis_index("tensor") < owned, 1.0, 0.0).astype(f32)
    load.wait()
    first, second, own = inverses_of([rows[:, m].reshape(-1, FACTOR_BLOCK) for m in range(3)], scale)
    fold(first, all_ref.at[0])
    fold(second, all_ref.at[1])
    fold(own * used, all_ref.at[2])
    own_ref[...] = all_ref[2]


def group_body(scale, rows_ref, _, __, out_ref, rows, sem):
    load = start_all([rows_ref.at[:, 3]], [rows], sem)[0]
    load.wait()
    parts = two(inverses_of([rows[...].reshape(-1, FACTOR_BLOCK)], scale)[0].T)
    out_ref[...] = jnp.concatenate(parts, axis=0)


def owned_body(own_ref, near_ref, here, beside, two_off, three_off, _, sum_ref, out_ref, split, own, near, held, need, sems, need_sems):
    sums = start_all([own_ref, near_ref], [own, near], need_sems, 2)
    needs = start_all([here.at[pl.ds(0, 2)], beside.at[pl.ds(0, 2)]], [need.at[pl.ds(0, 2)], need.at[pl.ds(2, 2)]], need_sems)
    loads = start_all([here.at[2], beside.at[2], two_off, three_off], [held.at[k] for k in range(4)], sems)
    z = lax.axis_index("tensor")
    odd = z % 2
    for k in range(2):
        needs[k].wait()
        for p in range(2):
            high, low = two(unfold(need.at[2 * k + p]))
            at = 2 * (odd if k == 0 else 1 - odd) + p
            split[0, at] = high
            split[1, at] = low
    for load in sums:
        load.wait()
    sum_ref[...] = own[...] + decode(near)
    for k, load in enumerate(loads):
        load.wait()
        out_ref[z ^ k] = unfold(held.at[k])


def own_body(cot_ref, act_ref, got_ref, _, sum_ref, cot, held, got, sems):
    share = held.shape[1]
    start = pl.multiple_of(lax.axis_index("dp") * share, share)
    loads = start_all([cot_ref, act_ref.at[:, pl.ds(start, share)], got_ref.at[0]], [cot, held, got], sems)
    loads[0].wait()
    left = cot[...].astype(f32).T.astype(bf16)
    loads[1].wait()
    product = jnp.dot(left, held[...], preferred_element_type=f32)
    loads[2].wait()
    sum_ref[...] = product + got[...]


def finish_body(split_ref, g_ref, sum_ref, come, step_out, split, left, total, come_in, step, sems, out_sems):
    width = FACTOR_BLOCK
    loads = start_all([g_ref, sum_ref, come, split_ref], [left, total, come_in, split], sems)

    def dot(a, c, dims):
        return lax.dot_general(a, c, (dims, ((), ())), preferred_element_type=f32)

    for load in loads[:3]:
        load.wait()
    sum_high, sum_low = two(total[...] + decode(come_in))
    both = dot(left[...], sum_high, ((1,), (0,)))
    right_high, right_low = two(both[:width] + (both[width:] + dot(left[:width], sum_low, ((1,), (0,)))))
    loads[3].wait()
    stores = []
    for b in range(split.shape[1]):
        part = slice(b * width, (b + 1) * width)
        both = dot(split[:, b].reshape(2 * width, width), right_high[:, part], ((1,), (1,)))
        step[b] = both[:width] + (both[width:] + dot(split[0, b], right_low[:, part], ((1,), (1,))))
        stores += start_all([step.at[b]], [step_out.at[part, :]], out_sems, b)
    for store in stores:
        store.wait()


def dma(count):
    return pltpu.SemaphoreType.DMA((count,))


def sum_cores(name, which, cotangent, activations, got, *after):
    tokens, group_w = cotangent.shape
    share = got.shape[2]
    wired = (fold_rows(group_w), share)
    steps, width = len(which) * SUM_PARTS, share // SUM_PARTS
    return call(
        functools.partial(sum_body, which),
        name,
        tuple(shaped(wired, bf16) if i < 2 else shaped((group_w, share)) for i in which),
        [ANY] * (3 + len(after)),
        (ANY,) * len(which),
        [
            pltpu.VMEM(cotangent.shape, bf16),
            pltpu.VMEM((steps, tokens, width), bf16),
            pltpu.VMEM((steps, group_w, width), f32),
            pltpu.VMEM((group_w, tokens), bf16),
            pltpu.VMEM((steps, wired[0], width), bf16),
            pltpu.VMEM((SUM_PARTS, group_w, width), f32),
            dma(1 + steps),
            dma(steps),
            dma(steps),
        ],
        moved=4 * MIB * len(which),
    )(cotangent, activations, got, *after)


def invert(block_owner, rows, after, scale):
    _, kinds, samples, _ = rows.shape
    packed = shaped((fold_rows(FACTOR_BLOCK // 2) + FOLD_ROWS, FACTOR_BLOCK), bf16)
    return call(
        functools.partial(invert_body, scale),
        "invert_blocks",
        (shaped((3, *packed.shape), bf16), packed),
        [SMEM, ANY, ANY],
        (VMEM,) * 2,
        [pltpu.VMEM((rows.shape[0], 3, samples, FACTOR_BLOCK), bf16), dma(1)],
        flops=2 * 3 * 4 * 18 * FACTOR_BLOCK**3,
        moved=2 * MIB,
    )(block_owner, rows, after)


def invert_group(rows, after, and_after, scale):
    samples = rows.shape[2]
    return call(
        functools.partial(group_body, scale),
        "invert_group",
        shaped((2 * FACTOR_BLOCK, FACTOR_BLOCK), bf16),
        [ANY] * 3,
        VMEM,
        [pltpu.VMEM((rows.shape[0], samples, FACTOR_BLOCK), bf16), dma(1)],
    )(rows, after, and_after)


def hop(rest, come, after):
    group_w, share = rest.shape
    wired = come.shape
    width = share // HOP_PARTS
    return call(
        hop_body,
        "hop",
        shaped(wired, bf16),
        [ANY] * 3,
        ANY,
        [pltpu.VMEM((HOP_PARTS, group_w, width), f32)]
        + [pltpu.VMEM((HOP_PARTS, wired[0], width), bf16)] * 2
        + [dma(2 * HOP_PARTS), dma(HOP_PARTS)],
    )(rest, come, after)


def sum_own(cotangent, activations, own_got, after):
    tokens = cotangent.shape[0]
    _, group_w, share = own_got.shape
    return call(
        own_body,
        "sum_own",
        shaped((group_w, share)),
        [ANY] * 4,
        VMEM,
        [
            pltpu.VMEM(cotangent.shape, bf16),
            pltpu.VMEM((tokens, share), bf16),
            pltpu.VMEM((group_w, share), f32),
            dma(3),
        ],
    )(cotangent, activations, own_got, after)


def owned_blocks(own_sum, near, inverses, beside, two_off, three_off, after):
    square = (4, FACTOR_BLOCK, FACTOR_BLOCK)
    held = pltpu.VMEM((4, *two_off.shape), bf16)
    return call(
        owned_body,
        "owned",
        (shaped(own_sum.shape), shaped(square), shaped((2, *square), bf16)),
        [ANY] * 7,
        (VMEM,) * 3,
        [pltpu.VMEM(own_sum.shape, f32), pltpu.VMEM(near.shape, bf16), held, held, dma(4), dma(4)],
        flops=OWNED_FLOPS,
    )(own_sum, near, inverses, beside, two_off, three_off, after)


def finish(split, g_parts, so_far, come):
    group_w, share = so_far.shape
    blocks = share // FACTOR_BLOCK
    return call(
        finish_body,
        "finish",
        shaped((share, group_w)),
        [ANY] * 4,
        ANY,
        [
            pltpu.VMEM(split.shape, bf16),
            pltpu.VMEM(g_parts.shape, bf16),
            pltpu.VMEM(so_far.shape, f32),
            pltpu.VMEM(come.shape, bf16),
            pltpu.VMEM((blocks, FACTOR_BLOCK, group_w), f32),
            dma(4),
            dma(blocks),
        ],
        moved=6 * MIB,
    )(split, g_parts, so_far, come)


def square_device(activations, cotangent, sampled_rows, block_owner):
    dp_count = lax.axis_size("dp")
    samples = sampled_rows.shape[0]

    def swap(block, bit, axis="dp"):
        count = lax.axis_size(axis)
        return lax.ppermute(block, axis, [(i, i ^ bit) for i in range(count)])

    def travel(block, even, odd):
        return lax.ppermute(block, "dp", [(i, i ^ (odd if i % 2 else even)) for i in range(dp_count)])

    theirs, own_theirs, picked = project(
        block_owner, sampled_rows, cotangent, activations, dp_count
    )
    got = swap(theirs, CORE)
    rows = lax.all_to_all(picked, "dp", split_axis=0, concat_axis=0, tiled=True)
    own_got = swap(own_theirs, CORE)

    (far,) = sum_cores("sum_far", (0,), cotangent, activations, got)
    far_come = travel(far, NEAR_X, NEAR_Y)
    near, rest = sum_cores("sum_near", (1, 2), cotangent, activations, got, far)
    near_come = travel(near, NEAR_X, NEAR_Y)
    own_sum = sum_own(cotangent, activations, own_got, rest)

    inverses, own = invert(block_owner, rows, own_sum, 1.0 / (samples * dp_count))
    beside = swap(inverses, 1, "tensor")
    two_off, three_off = swap(own, 2, "tensor"), swap(own, 3, "tensor")

    hopped = hop(rest, far_come, inverses)
    come_last = travel(hopped, NEAR_Y, NEAR_X)

    g_parts = invert_group(rows, near_come, hopped, activations.shape[0] / samples)
    so_far, owned, split = owned_blocks(own_sum, near_come, inverses, beside, two_off, three_off, g_parts)
    step = finish(split, g_parts, so_far, come_last)
    return step, owned


def solution(mesh):
    def per_device(activations, cotangent, sampled_rows, block_owner):
        block_total = activations.shape[1] // FACTOR_BLOCK
        dp_count, depth = mesh.shape["dp"], mesh.shape["tensor"]
        fits = (
            dp_count == 8
            and depth == 4
            and block_total == dp_count * depth
            and cotangent.shape[1] == FACTOR_BLOCK
            and sampled_rows.shape[0] % 16 == 0
            and activations.shape[0] % 128 == 0
        )
        run = square_device if fits else general_device
        return run(activations, cotangent, sampled_rows, block_owner)

    return jax.shard_map(
        per_device,
        mesh=mesh,
        in_specs=(P("dp", None), P("dp", "tensor"), P("dp"), P()),
        out_specs=(P("dp", "tensor"), P("dp", None, None)),
        check_vma=False,
    )
```

```python
import functools

import jax
import jax.numpy as jnp
from jax import lax
from jax.experimental import pallas as pl
from jax.experimental.pallas import tpu as pltpu
from jax.sharding import PartitionSpec as P

S_DEV = 64
FACTOR_BLOCK = 256
ITERS = 10


DAMPING = 0.05
precise_mode = lax.Precision.HIGHEST
f32 = jnp.float32
bf16 = jnp.bfloat16


def block_rank(block_owner):
    block_total = block_owner.shape[0]
    same_owner = block_owner[:, None] == block_owner[None, :]
    positions = jnp.arange(block_total, dtype=jnp.int32)
    before = positions[None, :] < positions[:, None]
    return jnp.sum((same_owner & before).astype(jnp.int32), axis=1)


def from_partner(block, axis, apart):
    count = lax.axis_size(axis)
    route = []
    for low in range(count):
        high = low | 1 << apart
        if high != low and high < count:
            route += [(low, high), (high, low)]
    return lax.ppermute(block, axis, route)


def newton_inverse(matrix):
    extent = matrix.shape[-1]
    identity = jnp.eye(extent, dtype=jnp.float32)
    row_bound = jnp.max(jnp.sum(jnp.abs(matrix), axis=2), axis=1)
    initial = identity[None, :, :] / row_bound[:, None, None]

    def advance(turn_index, current):
        product = jnp.einsum("nij,njk->nik", matrix, current, precision=precise_mode)
        return jnp.einsum(
            "nij,njk->nik", current, 2.0 * identity[None, :, :] - product, precision=precise_mode
        )

    return lax.fori_loop(0, ITERS, advance, initial)


def owner_grams(received):
    return jnp.einsum("pcsk,pcsl->ckl", received, received, preferred_element_type=jnp.float32)


def general_device(activations, cotangent, sampled_rows, block_owner):
    tok_local = activations.shape[0]
    model_width = activations.shape[1]
    group_w = cotangent.shape[1]
    dp_count = lax.axis_size("dp")
    my_dp = lax.axis_index("dp")
    block_total = model_width // FACTOR_BLOCK
    capacity = max(1, block_total // dp_count)
    row_share = model_width // dp_count
    samples_all = S_DEV * dp_count
    grad_rows = lax.psum_scatter(
        lax.dot_general(
            activations, cotangent, (((0,), (0,)), ((), ())), preferred_element_type=jnp.float32
        ),
        "dp",
        scatter_dimension=0,
        tiled=True,
    )
    picked_acts = jnp.take(activations, sampled_rows, axis=0)
    picked_grads = jnp.take(cotangent, sampled_rows, axis=0)
    g_partial = lax.dot_general(
        picked_grads, picked_grads, (((0,), (0,)), ((), ())), preferred_element_type=jnp.float32
    )
    g_total = lax.psum(g_partial, "dp")
    g_factor = g_total * (tok_local / S_DEV) + DAMPING * jnp.eye(group_w, dtype=jnp.float32)
    slot_of = block_owner * capacity + block_rank(block_owner)
    dest_ids = jnp.arange(dp_count * capacity, dtype=jnp.int32)
    chooser = (slot_of[None, :] == dest_ids[:, None]).astype(jnp.bfloat16)
    row_blocks = picked_acts.reshape(S_DEV, block_total, FACTOR_BLOCK)
    outgoing = lax.dot_general(
        chooser, row_blocks, (((1,), (1,)), ((), ())), preferred_element_type=jnp.float32
    )
    outgoing = outgoing.astype(jnp.bfloat16).reshape(dp_count, capacity, S_DEV, FACTOR_BLOCK)
    gram_slots = owner_grams(
        lax.all_to_all(outgoing, "dp", split_axis=0, concat_axis=0, tiled=True)
    )
    a_factor = (
        gram_slots / samples_all + DAMPING * jnp.eye(FACTOR_BLOCK, dtype=jnp.float32)[None, :, :]
    )
    input_factor_inverse = newton_inverse(a_factor)
    owned_count = jnp.sum((block_owner == my_dp).astype(jnp.int32))
    slot_used = jnp.arange(capacity, dtype=jnp.int32) < owned_count
    owned_out = jnp.where(slot_used[:, None, None], input_factor_inverse, 0.0)
    g_inverse = newton_inverse(g_factor[None, :, :])[0]
    per_dev = max(1, row_share // FACTOR_BLOCK)
    rows_each = min(row_share, FACTOR_BLOCK)
    first_block = my_dp * row_share // FACTOR_BLOCK
    need_ids = first_block + jnp.arange(per_dev, dtype=jnp.int32)
    need_slots = jnp.take(slot_of, need_ids)
    row_offset = my_dp * row_share % FACTOR_BLOCK
    shard_piece = lax.all_gather(owned_out, "dp", axis=0, tiled=True)
    rows_part = lax.dynamic_slice_in_dim(shard_piece, row_offset, rows_each, 1)
    slot_ids = jnp.arange(shard_piece.shape[0], dtype=jnp.int32)
    selector = (need_slots[:, None] == slot_ids[None, :]).astype(jnp.float32)
    inverse_rows = jnp.einsum("jm,mkl->jkl", selector, rows_part, precision=precise_mode)
    grad_right = jnp.dot(
        grad_rows, g_inverse, precision=precise_mode, preferred_element_type=jnp.float32
    )
    if row_share < FACTOR_BLOCK:
        partner = from_partner(grad_right, "dp", 0)
        is_lower = my_dp % 2 == 0
        joined = jnp.where(
            is_lower,
            jnp.concatenate([grad_right, partner], 0),
            jnp.concatenate([partner, grad_right], 0),
        )
        complete_rows = joined[None, :, :]
    else:
        complete_rows = grad_right.reshape(per_dev, FACTOR_BLOCK, group_w)
    natural_step = jnp.einsum("jrk,jkl->jrl", inverse_rows, complete_rows, precision=precise_mode)
    return (natural_step.reshape(row_share, group_w), owned_out)


MIB = 1 << 20
VMEM_MIB = 32
PROJECT_MIB = 64
SUM_MIB = 64
AHEAD = 3
PROJECT_AHEAD = 6
HOP_PARTS = 2
SUM_PARTS = 2
OWNED_FLOPS = 20_000_000_000
ANY = pl.BlockSpec(memory_space=pl.ANY)
VMEM = pl.BlockSpec(memory_space=pltpu.VMEM)
SMEM = pl.BlockSpec(memory_space=pltpu.SMEM)
CORE, NEAR_X, NEAR_Y, FAR = 1, 2, 4, 6


def routes(me):
    first = jnp.where(me % 2 == 0, NEAR_X, NEAR_Y)
    return FAR, first, FAR - first, 0


def shaped(shape, dtype=f32):
    return jax.ShapeDtypeStruct(shape, dtype)


def call(body, name, out_shape, in_specs, out_specs, scratch=(), flops=0, moved=0, mib=VMEM_MIB):
    return pl.pallas_call(
        body,
        out_shape=out_shape,
        in_specs=in_specs,
        out_specs=out_specs,
        scratch_shapes=scratch,
        compiler_params=pltpu.CompilerParams(vmem_limit_bytes=mib * MIB),
        cost_estimate=pl.CostEstimate(flops=flops, bytes_accessed=moved, transcendentals=0),
        name=name,
    )


def start_all(sources, targets, sems, first=0):
    copies = [
        pltpu.make_async_copy(source, target, sems.at[first + i])
        for i, (source, target) in enumerate(zip(sources, targets))
    ]
    for copy in copies:
        copy.start()
    return copies


def fold_rows(rows):
    return rows + rows // 2


def encode(x, into):
    rows = x.shape[0]
    high = x.astype(bf16)
    into[:rows] = high
    base = high.astype(f32)
    left = (x - base) * pl.reciprocal(base, approx=True) * 256.0
    left = jnp.where(jnp.abs(base) < 1e-30, 0.0, jnp.clip(left, -1.0, 1.0))
    digit = jnp.floor(left * 63.5 + 64.0)
    first, second = digit[: rows // 2], digit[rows // 2 :]
    negative = second >= 64.0
    power = jnp.exp2(jnp.where(negative, second - 96.0, second - 32.0))
    packed = (first + 128.0) * power
    into[rows:] = jnp.where(negative, -packed, packed).astype(bf16)


def decode(ref):
    rows = ref.shape[0] * 2 // 3
    packed = ref[rows:].astype(f32)
    size = jnp.abs(packed)
    power = jnp.floor(jnp.log2(size) + 1e-3)
    first = jnp.floor(size * jnp.exp2(7.0 - power) + 0.5) - 128.0
    second = power + jnp.where(packed < 0.0, 89.0, 25.0)
    digit = jnp.concatenate([first, second], axis=0)
    base = ref[:rows].astype(f32)
    return base + base * ((digit - 63.5) * (1.0 / (63.5 * 256.0)))


def project_body(
    owner, rows_ref, cot_ref, act_ref, theirs, own_theirs, out_ref,
    held, cot, rows, left, grads, picks, slots, sems, out_sems, small_sems, pick_sems,
):
    count, tokens, share = held.shape
    group_w = cot.shape[1]
    samples = rows.shape[1]
    per_tile = share // FACTOR_BLOCK
    me = lax.axis_index("dp")
    z = lax.axis_index("tensor")
    half = count // 2
    tiles = [me ^ m ^ CORE for m in routes(me ^ CORE)] + [me ^ m for m in routes(me)]
    targets = [theirs.at[i] for i in range(half - 1)] + [own_theirs.at[0]]

    small = start_all([cot_ref, rows_ref], [cot, rows], small_sems)
    starts = [pl.multiple_of(t * share, share) for t in tiles]
    loads = [
        pltpu.make_async_copy(act_ref.at[:, pl.ds(start, share)], held.at[i], sems.at[i])
        for i, start in enumerate(starts)
    ]
    for load in loads[:PROJECT_AHEAD]:
        load.start()

    for d in range(count):
        slots[0, d] = 0
        slots[1, d] = 0
    for b in range(owner.shape[0]):
        holder = owner[b]
        rank = slots[0, holder]
        slots[0, holder] = rank + 1
        slots[1, holder] = jnp.where(rank == z, b, slots[1, holder])

    for copy in small:
        copy.wait()
    left[:group_w] = cot[...].astype(f32).T.astype(bf16)
    places = lax.broadcasted_iota(jnp.int32, (tokens, samples), 0)
    left[group_w:] = (places == rows[...]).astype(f32).T.astype(bf16)

    blocks = count * per_tile
    picks[blocks] = jnp.dot(left[group_w:], cot[...], preferred_element_type=f32).astype(bf16)
    stores = []

    def pass_on(block, many, dest, place, n):
        return start_all([picks.at[pl.ds(block, many)]], [out_ref.at[dest, pl.ds(place, many)]], pick_sems, n)

    for d in range(count):
        stores += pass_on(blocks, 1, d, 3, 3 * d + 2)
    for i in range(count):
        if i % 2 == 0:
            loads[i].wait()
            loads[i + 1].wait()
            for load in loads[i + PROJECT_AHEAD : i + PROJECT_AHEAD + 2]:
                load.start()
        if i < half:
            product = jnp.dot(left[...], held[i], preferred_element_type=f32)
            grads[i] = product[:group_w]
            stores += start_all([grads.at[i]], [targets[i]], out_sems, i)
            picked = product[group_w:]
        else:
            picked = jnp.dot(left[group_w:], held[i], preferred_element_type=f32)
        for j in range(per_tile):
            picks[tiles[i] * per_tile + j] = picked[
                :, j * FACTOR_BLOCK : (j + 1) * FACTOR_BLOCK
            ].astype(bf16)
        stores += pass_on(tiles[i] * per_tile + 2 * (z % 2), 2, tiles[i], 0, 3 * i)
    for d in range(count):
        stores += pass_on(slots[1, d], 1, d, 2, 3 * d + 1)
    for store in stores:
        store.wait()


def project(block_owner, sampled_rows, cotangent, activations, count):
    samples = sampled_rows.shape[0]
    tokens, group_w = cotangent.shape
    model_width = activations.shape[1]
    share = model_width // count
    one = shaped((1, group_w, share))
    rest = shaped((count // 2 - 1, group_w, share))
    return call(
        project_body,
        "project",
        (rest, one, shaped((count, 4, samples, FACTOR_BLOCK), bf16)),
        [SMEM, ANY, ANY, ANY],
        (ANY,) * 3,
        [
            pltpu.VMEM((count, tokens, share), bf16),
            pltpu.VMEM((tokens, group_w), bf16),
            pltpu.VMEM((1, samples), jnp.int32),
            pltpu.VMEM((group_w + samples, tokens), bf16),
            pltpu.VMEM((count // 2, group_w, share), f32),
            pltpu.VMEM((model_width // FACTOR_BLOCK + 1, samples, FACTOR_BLOCK), bf16),
            pltpu.SMEM((2, count), jnp.int32),
            pltpu.SemaphoreType.DMA((count,)),
            pltpu.SemaphoreType.DMA((count // 2,)),
            pltpu.SemaphoreType.DMA((2,)),
            pltpu.SemaphoreType.DMA((3 * count,)),
        ],
        flops=2 * tokens * (group_w + samples) * model_width,
        moved=2 * tokens * model_width + 2 * group_w * model_width,
        mib=PROJECT_MIB,
    )(block_owner, sampled_rows[None, :], cotangent, activations)


def sum_body(which, cot_ref, act_ref, got_ref, *refs):
    count = len(which)
    outs, (cot, held, got, left, wire, plain, sems, got_sems, out_sems) = refs[-9 - count : -9], refs[-9:]
    width = held.shape[2]
    share = got_ref.shape[2]
    parts = share // width
    me = lax.axis_index("dp")
    starts = [pl.multiple_of((me ^ routes(me)[i]) * share, share) for i in which]
    work = [(i, p) for i in range(count) for p in range(parts)]
    first = start_all([cot_ref], [cot], sems)[0]

    def fetch(n):
        i, p = work[n]
        tile = act_ref.at[:, pl.ds(starts[i] + p * width, width)]
        come = got_ref.at[which[i], :, pl.ds(p * width, width)]
        return start_all([tile], [held.at[n]], sems, 1 + n) + start_all([come], [got.at[n]], got_sems, n)

    loads = [fetch(n) for n in range(min(AHEAD, len(work)))]
    first.wait()
    left[...] = cot[...].astype(f32).T.astype(bf16)
    stores = []
    for n, (i, p) in enumerate(work):
        loads[n][0].wait()
        if n + AHEAD < len(work):
            loads.append(fetch(n + AHEAD))
        product = jnp.dot(left[...], held[n], preferred_element_type=f32)
        loads[n][1].wait()
        if which[i] < 2:
            encode(product + got[n], wire.at[n])
            source = wire.at[n]
        else:
            plain[p] = product + got[n]
            source = plain.at[p]
        stores += start_all([source], [outs[i].at[:, pl.ds(p * width, width)]], out_sems, n)
    for store in stores:
        store.wait()


def hop_body(rest, come, _, out_ref, rest_in, come_in, out, sems, out_sems):
    parts = rest_in.shape[0]
    width = rest_in.shape[2]
    loads, stores = [], []
    for p in range(parts):
        columns = pl.ds(p * width, width)
        loads.append(start_all([rest.at[:, columns], come.at[:, columns]], [rest_in.at[p], come_in.at[p]], sems, 2 * p))
    for p in range(parts):
        for load in loads[p]:
            load.wait()
        encode(rest_in[p] + decode(come_in.at[p]), out.at[p])
        stores += start_all([out.at[p]], [out_ref.at[:, pl.ds(p * width, width)]], out_sems, p)
    for store in stores:
        store.wait()


def two(x):
    high = x.astype(bf16)
    return high, (x - high.astype(f32)).astype(bf16)


def newton_step(lows, currents, last):
    def dot(a, b):
        return jnp.dot(a, b, preferred_element_type=f32)

    parts = [two(low) for low in lows]
    next_lows, next_currents = [], []
    if not last:
        for low, (high_part, low_part) in zip(lows, parts):
            mixed = dot(high_part, low_part)
            next_lows.append(2.0 * low - (dot(high_part, high_part) + (mixed + mixed.T)))
    for current, (high_part, low_part) in zip(currents, parts):
        high, rest = two(current)
        product = dot(
            jnp.concatenate([high, rest, high], axis=1),
            jnp.concatenate([high_part, high_part, low_part], axis=0),
        )
        next_currents.append(2.0 * current - product)
    return next_lows, next_currents


def places(extent):
    return (
        lax.broadcasted_iota(jnp.int32, (extent, extent), 0),
        lax.broadcasted_iota(jnp.int32, (extent, extent), 1),
    )


FOLD_ROWS = 16


def fold(matrix, into):
    half = matrix.shape[0] // 2
    row, column = places(half)
    low = matrix[half:, half:]
    both = jnp.where(row <= column, matrix[:half, :half], low)
    coded = fold_rows(half)
    encode(jnp.concatenate([both, matrix[:half, half:]], axis=1), into.at[:coded])
    left = jnp.sum(jnp.where(row == column, low, 0.0), axis=0, keepdims=True)
    line = lax.broadcasted_iota(jnp.int32, (FOLD_ROWS, 2 * half), 0)
    diagonal = jnp.zeros((FOLD_ROWS, 2 * half), f32)
    for part in range(3):
        high = left.astype(bf16).astype(f32)
        diagonal = jnp.where(line == part, jnp.concatenate([high, high], axis=1), diagonal)
        left = left - high
    into[coded:] = diagonal.astype(bf16)


def unfold(packed):
    half = packed.shape[1] // 2
    coded = fold_rows(half)
    row, column = places(half)
    values = decode(packed.at[:coded])
    diagonal = jnp.sum(packed[coded:].astype(f32), axis=0, keepdims=True)[:, :half]
    both, corner = values[:, :half], values[:, half:]
    turned = both.T
    top = jnp.where(row <= column, both, turned)
    low = jnp.where(row == column, diagonal, jnp.where(row > column, both, turned))
    return jnp.concatenate(
        [jnp.concatenate([top, corner], axis=1), jnp.concatenate([corner.T, low], axis=1)], axis=0
    )


def inverses_of(samples, scale):
    row, column = places(FACTOR_BLOCK)
    eye = (row == column).astype(f32)
    lows, currents = [], []
    for rows in samples:
        gram = lax.dot_general(
            rows, rows, (((0,), (0,)), ((), ())), preferred_element_type=f32
        )
        matrix = gram * scale + DAMPING * eye
        bound = jnp.max(jnp.sum(jnp.abs(matrix), axis=1, keepdims=True), axis=0, keepdims=True)
        inverse_bound = 1.0 / bound
        low = matrix * inverse_bound
        lows.append(low)
        currents.append((2.0 * eye - low) * inverse_bound)
    lows = newton_step(lows, [], False)[0]
    for turn in range(1, ITERS):
        lows, currents = newton_step(lows, currents, turn == ITERS - 1)
    return currents


def invert_body(scale, rows_ref, all_ref, own_ref, rows, sem):
    load = start_all([rows_ref.at[:, pl.ds(0, 3)]], [rows], sem)[0]
    load.wait()
    first, second, own = inverses_of([rows[:, m].reshape(-1, FACTOR_BLOCK) for m in range(3)], scale)
    fold(first, all_ref.at[0])
    fold(second, all_ref.at[1])
    fold(own, all_ref.at[2])
    own_ref[...] = all_ref[2]


def group_body(scale, rows_ref, _, __, out_ref, rows, sem):
    load = start_all([rows_ref.at[:, 3]], [rows], sem)[0]
    load.wait()
    parts = two(inverses_of([rows[...].reshape(-1, FACTOR_BLOCK)], scale)[0].T)
    out_ref[...] = jnp.concatenate(parts, axis=0)


def ready_body(own_ref, near_ref, here, beside, _, sum_ref, split, own, near, need, sems):
    loads = start_all(
        [here.at[pl.ds(0, 2)], beside.at[pl.ds(0, 2)], own_ref, near_ref],
        [need.at[pl.ds(0, 2)], need.at[pl.ds(2, 2)], own, near],
        sems,
    )
    odd = lax.axis_index("tensor") % 2
    for k in range(2):
        loads[k].wait()
        for p in range(2):
            high, low = two(unfold(need.at[2 * k + p]))
            at = 2 * (odd if k == 0 else 1 - odd) + p
            split[0, at] = high
            split[1, at] = low
    for load in loads[2:]:
        load.wait()
    sum_ref[...] = own[...] + decode(near)


def owned_body(owner, here, beside, two_off, three_off, _, out_ref, done_ref, held, sems):
    loads = start_all([here.at[2], beside.at[2], two_off, three_off], [held.at[k] for k in range(4)], sems)
    z = lax.axis_index("tensor")
    me = lax.axis_index("dp")
    count = jnp.int32(0)
    for b in range(owner.shape[0]):
        count = count + jnp.where(owner[b] == me, 1, 0)
    for k, load in enumerate(loads):
        load.wait()
        slot = z ^ k
        out_ref[slot] = jnp.where(slot < count, unfold(held.at[k]), 0.0)
    done_ref[...] = jnp.zeros(done_ref.shape, f32)


def own_body(cot_ref, act_ref, got_ref, _, sum_ref, cot, held, got, sems):
    share = held.shape[1]
    start = pl.multiple_of(lax.axis_index("dp") * share, share)
    loads = start_all([cot_ref, act_ref.at[:, pl.ds(start, share)], got_ref.at[0]], [cot, held, got], sems)
    loads[0].wait()
    left = cot[...].astype(f32).T.astype(bf16)
    loads[1].wait()
    product = jnp.dot(left, held[...], preferred_element_type=f32)
    loads[2].wait()
    sum_ref[...] = product + got[...]


def finish_body(split_ref, g_ref, sum_ref, come, _, step_out, split, left, total, come_in, step, sems, out_sems):
    width = FACTOR_BLOCK
    loads = start_all([g_ref, sum_ref, come, split_ref], [left, total, come_in, split], sems)

    def dot(a, c, dims):
        return lax.dot_general(a, c, (dims, ((), ())), preferred_element_type=f32)

    for load in loads[:3]:
        load.wait()
    sum_high, sum_low = two(total[...] + decode(come_in))
    both = dot(left[...], sum_high, ((1,), (0,)))
    right_high, right_low = two(both[:width] + (both[width:] + dot(left[:width], sum_low, ((1,), (0,)))))
    loads[3].wait()
    stores = []
    for b in range(split.shape[1]):
        part = slice(b * width, (b + 1) * width)
        both = dot(split[:, b].reshape(2 * width, width), right_high[:, part], ((1,), (1,)))
        step[b] = both[:width] + (both[width:] + dot(split[0, b], right_low[:, part], ((1,), (1,))))
        stores += start_all([step.at[b]], [step_out.at[part, :]], out_sems, b)
    for store in stores:
        store.wait()


def dma(count):
    return pltpu.SemaphoreType.DMA((count,))


def sum_cores(name, which, cotangent, activations, got, *after):
    tokens, group_w = cotangent.shape
    share = got.shape[2]
    wired = (fold_rows(group_w), share)
    steps, width = len(which) * SUM_PARTS, share // SUM_PARTS
    return call(
        functools.partial(sum_body, which),
        name,
        tuple(shaped(wired, bf16) if i < 2 else shaped((group_w, share)) for i in which),
        [ANY] * (3 + len(after)),
        (ANY,) * len(which),
        [
            pltpu.VMEM(cotangent.shape, bf16),
            pltpu.VMEM((steps, tokens, width), bf16),
            pltpu.VMEM((steps, group_w, width), f32),
            pltpu.VMEM((group_w, tokens), bf16),
            pltpu.VMEM((steps, wired[0], width), bf16),
            pltpu.VMEM((SUM_PARTS, group_w, width), f32),
            dma(1 + steps),
            dma(steps),
            dma(steps),
        ],
        moved=4 * MIB * len(which),
        mib=SUM_MIB,
    )(cotangent, activations, got, *after)


def invert(rows, scale):
    _, kinds, samples, _ = rows.shape
    packed = shaped((fold_rows(FACTOR_BLOCK // 2) + FOLD_ROWS, FACTOR_BLOCK), bf16)
    return call(
        functools.partial(invert_body, scale),
        "invert_blocks",
        (shaped((3, *packed.shape), bf16), packed),
        [ANY],
        (VMEM,) * 2,
        [pltpu.VMEM((rows.shape[0], 3, samples, FACTOR_BLOCK), bf16), dma(1)],
        flops=2 * 3 * 4 * 18 * FACTOR_BLOCK**3,
        moved=2 * MIB,
    )(rows)


def invert_group(rows, after, and_after, scale):
    samples = rows.shape[2]
    return call(
        functools.partial(group_body, scale),
        "invert_group",
        shaped((2 * FACTOR_BLOCK, FACTOR_BLOCK), bf16),
        [ANY] * 3,
        VMEM,
        [pltpu.VMEM((rows.shape[0], samples, FACTOR_BLOCK), bf16), dma(1)],
    )(rows, after, and_after)


def hop(rest, come, after):
    group_w, share = rest.shape
    wired = come.shape
    width = share // HOP_PARTS
    return call(
        hop_body,
        "hop",
        shaped(wired, bf16),
        [ANY] * 3,
        ANY,
        [pltpu.VMEM((HOP_PARTS, group_w, width), f32)]
        + [pltpu.VMEM((HOP_PARTS, wired[0], width), bf16)] * 2
        + [dma(2 * HOP_PARTS), dma(HOP_PARTS)],
    )(rest, come, after)


def sum_own(cotangent, activations, own_got, after):
    tokens = cotangent.shape[0]
    _, group_w, share = own_got.shape
    return call(
        own_body,
        "sum_own",
        shaped((group_w, share)),
        [ANY] * 4,
        VMEM,
        [
            pltpu.VMEM(cotangent.shape, bf16),
            pltpu.VMEM((tokens, share), bf16),
            pltpu.VMEM((group_w, share), f32),
            dma(3),
        ],
        mib=SUM_MIB,
    )(cotangent, activations, own_got, after)


def ready(own_sum, near, inverses, beside, after):
    square = (4, FACTOR_BLOCK, FACTOR_BLOCK)
    held = pltpu.VMEM((4, *inverses.shape[1:]), bf16)
    return call(
        ready_body,
        "ready",
        (shaped(own_sum.shape), shaped((2, *square), bf16)),
        [ANY] * 5,
        (VMEM,) * 2,
        [pltpu.VMEM(own_sum.shape, f32), pltpu.VMEM(near.shape, bf16), held, dma(4)],
    )(own_sum, near, inverses, beside, after)


def owned_blocks(block_owner, inverses, beside, two_off, three_off, after):
    return call(
        owned_body,
        "owned",
        (shaped((4, FACTOR_BLOCK, FACTOR_BLOCK)), shaped((8, 128))),
        [SMEM] + [ANY] * 5,
        (VMEM,) * 2,
        [pltpu.VMEM((4, *two_off.shape), bf16), dma(4)],
        flops=OWNED_FLOPS,
    )(block_owner, inverses, beside, two_off, three_off, after)


def finish(split, g_parts, so_far, come, after):
    group_w, share = so_far.shape
    blocks = share // FACTOR_BLOCK
    return call(
        finish_body,
        "finish",
        shaped((share, group_w)),
        [ANY] * 5,
        ANY,
        [
            pltpu.VMEM(split.shape, bf16),
            pltpu.VMEM(g_parts.shape, bf16),
            pltpu.VMEM(so_far.shape, f32),
            pltpu.VMEM(come.shape, bf16),
            pltpu.VMEM((blocks, FACTOR_BLOCK, group_w), f32),
            dma(4),
            dma(blocks),
        ],
        moved=6 * MIB,
    )(split, g_parts, so_far, come, after)


def square_device(activations, cotangent, sampled_rows, block_owner):
    dp_count = lax.axis_size("dp")
    samples = sampled_rows.shape[0]

    def swap(block, bit, axis="dp"):
        count = lax.axis_size(axis)
        return lax.ppermute(block, axis, [(i, i ^ bit) for i in range(count)])

    def travel(block, even, odd):
        return lax.ppermute(block, "dp", [(i, i ^ (odd if i % 2 else even)) for i in range(dp_count)])

    theirs, own_theirs, picked = project(
        block_owner, sampled_rows, cotangent, activations, dp_count
    )
    got = swap(theirs, CORE)
    rows = lax.all_to_all(picked, "dp", split_axis=0, concat_axis=0, tiled=True)
    own_got = swap(own_theirs, CORE)

    (far,) = sum_cores("sum_far", (0,), cotangent, activations, got)
    far_come = travel(far, NEAR_X, NEAR_Y)
    own_sum = sum_own(cotangent, activations, own_got, far)
    near, rest = sum_cores("sum_near", (1, 2), cotangent, activations, got, own_sum)
    near_come = travel(near, NEAR_X, NEAR_Y)

    inverses, own = invert(rows, 1.0 / (samples * dp_count))
    beside = swap(inverses, 1, "tensor")
    two_off, three_off = swap(own, 2, "tensor"), swap(own, 3, "tensor")

    hopped = hop(rest, far_come, inverses)
    come_last = travel(hopped, NEAR_Y, NEAR_X)

    g_parts = invert_group(rows, near_come, hopped, activations.shape[0] / samples)
    so_far, split = ready(own_sum, near_come, inverses, beside, g_parts)
    owned, done = owned_blocks(block_owner, inverses, beside, two_off, three_off, so_far)
    step = finish(split, g_parts, so_far, come_last, done)
    return step, owned


def solution(mesh):
    def per_device(activations, cotangent, sampled_rows, block_owner):
        block_total = activations.shape[1] // FACTOR_BLOCK
        dp_count, depth = mesh.shape["dp"], mesh.shape["tensor"]
        fits = (
            dp_count == 8
            and depth == 4
            and block_total == dp_count * depth
            and cotangent.shape[1] == FACTOR_BLOCK
            and sampled_rows.shape[0] % 16 == 0
            and activations.shape[0] % 128 == 0
        )
        run = square_device if fits else general_device
        return run(activations, cotangent, sampled_rows, block_owner)

    return jax.shard_map(
        per_device,
        mesh=mesh,
        in_specs=(P("dp", None), P("dp", "tensor"), P("dp"), P()),
        out_specs=(P("dp", "tensor"), P("dp", None, None)),
        check_vma=False,
    )
```

```python
import functools

import jax
import jax.numpy as jnp
from jax import lax
from jax.experimental import pallas as pl
from jax.experimental.pallas import tpu as pltpu
from jax.sharding import PartitionSpec as P

S_DEV = 64
FACTOR_BLOCK = 256
ITERS = 10


DAMPING = 0.05
precise_mode = lax.Precision.HIGHEST
f32 = jnp.float32
bf16 = jnp.bfloat16


def block_rank(block_owner):
    block_total = block_owner.shape[0]
    same_owner = block_owner[:, None] == block_owner[None, :]
    positions = jnp.arange(block_total, dtype=jnp.int32)
    before = positions[None, :] < positions[:, None]
    return jnp.sum((same_owner & before).astype(jnp.int32), axis=1)


def from_partner(block, axis, apart):
    count = lax.axis_size(axis)
    route = []
    for low in range(count):
        high = low | 1 << apart
        if high != low and high < count:
            route += [(low, high), (high, low)]
    return lax.ppermute(block, axis, route)


def newton_inverse(matrix):
    extent = matrix.shape[-1]
    identity = jnp.eye(extent, dtype=jnp.float32)
    row_bound = jnp.max(jnp.sum(jnp.abs(matrix), axis=2), axis=1)
    initial = identity[None, :, :] / row_bound[:, None, None]

    def advance(turn_index, current):
        product = jnp.einsum("nij,njk->nik", matrix, current, precision=precise_mode)
        return jnp.einsum(
            "nij,njk->nik", current, 2.0 * identity[None, :, :] - product, precision=precise_mode
        )

    return lax.fori_loop(0, ITERS, advance, initial)


def owner_grams(received):
    return jnp.einsum("pcsk,pcsl->ckl", received, received, preferred_element_type=jnp.float32)


def general_device(activations, cotangent, sampled_rows, block_owner):
    tok_local = activations.shape[0]
    model_width = activations.shape[1]
    group_w = cotangent.shape[1]
    dp_count = lax.axis_size("dp")
    my_dp = lax.axis_index("dp")
    block_total = model_width // FACTOR_BLOCK
    capacity = max(1, block_total // dp_count)
    row_share = model_width // dp_count
    samples_all = S_DEV * dp_count
    grad_rows = lax.psum_scatter(
        lax.dot_general(
            activations, cotangent, (((0,), (0,)), ((), ())), preferred_element_type=jnp.float32
        ),
        "dp",
        scatter_dimension=0,
        tiled=True,
    )
    picked_acts = jnp.take(activations, sampled_rows, axis=0)
    picked_grads = jnp.take(cotangent, sampled_rows, axis=0)
    g_partial = lax.dot_general(
        picked_grads, picked_grads, (((0,), (0,)), ((), ())), preferred_element_type=jnp.float32
    )
    g_total = lax.psum(g_partial, "dp")
    g_factor = g_total * (tok_local / S_DEV) + DAMPING * jnp.eye(group_w, dtype=jnp.float32)
    slot_of = block_owner * capacity + block_rank(block_owner)
    dest_ids = jnp.arange(dp_count * capacity, dtype=jnp.int32)
    chooser = (slot_of[None, :] == dest_ids[:, None]).astype(jnp.bfloat16)
    row_blocks = picked_acts.reshape(S_DEV, block_total, FACTOR_BLOCK)
    outgoing = lax.dot_general(
        chooser, row_blocks, (((1,), (1,)), ((), ())), preferred_element_type=jnp.float32
    )
    outgoing = outgoing.astype(jnp.bfloat16).reshape(dp_count, capacity, S_DEV, FACTOR_BLOCK)
    gram_slots = owner_grams(
        lax.all_to_all(outgoing, "dp", split_axis=0, concat_axis=0, tiled=True)
    )
    a_factor = (
        gram_slots / samples_all + DAMPING * jnp.eye(FACTOR_BLOCK, dtype=jnp.float32)[None, :, :]
    )
    input_factor_inverse = newton_inverse(a_factor)
    owned_count = jnp.sum((block_owner == my_dp).astype(jnp.int32))
    slot_used = jnp.arange(capacity, dtype=jnp.int32) < owned_count
    owned_out = jnp.where(slot_used[:, None, None], input_factor_inverse, 0.0)
    g_inverse = newton_inverse(g_factor[None, :, :])[0]
    per_dev = max(1, row_share // FACTOR_BLOCK)
    rows_each = min(row_share, FACTOR_BLOCK)
    first_block = my_dp * row_share // FACTOR_BLOCK
    need_ids = first_block + jnp.arange(per_dev, dtype=jnp.int32)
    need_slots = jnp.take(slot_of, need_ids)
    row_offset = my_dp * row_share % FACTOR_BLOCK
    shard_piece = lax.all_gather(owned_out, "dp", axis=0, tiled=True)
    rows_part = lax.dynamic_slice_in_dim(shard_piece, row_offset, rows_each, 1)
    slot_ids = jnp.arange(shard_piece.shape[0], dtype=jnp.int32)
    selector = (need_slots[:, None] == slot_ids[None, :]).astype(jnp.float32)
    inverse_rows = jnp.einsum("jm,mkl->jkl", selector, rows_part, precision=precise_mode)
    grad_right = jnp.dot(
        grad_rows, g_inverse, precision=precise_mode, preferred_element_type=jnp.float32
    )
    if row_share < FACTOR_BLOCK:
        partner = from_partner(grad_right, "dp", 0)
        is_lower = my_dp % 2 == 0
        joined = jnp.where(
            is_lower,
            jnp.concatenate([grad_right, partner], 0),
            jnp.concatenate([partner, grad_right], 0),
        )
        complete_rows = joined[None, :, :]
    else:
        complete_rows = grad_right.reshape(per_dev, FACTOR_BLOCK, group_w)
    natural_step = jnp.einsum("jrk,jkl->jrl", inverse_rows, complete_rows, precision=precise_mode)
    return (natural_step.reshape(row_share, group_w), owned_out)


MIB = 1 << 20
VMEM_MIB = 32
PROJECT_MIB = 64
SUM_MIB = 64
AHEAD = 3
PROJECT_AHEAD = 6
HOP_PARTS = 2
SUM_PARTS = 2
OWNED_FLOPS = 20_000_000_000
ANY = pl.BlockSpec(memory_space=pl.ANY)
VMEM = pl.BlockSpec(memory_space=pltpu.VMEM)
SMEM = pl.BlockSpec(memory_space=pltpu.SMEM)
CORE, NEAR_X, NEAR_Y, FAR = 1, 2, 4, 6


def routes(me):
    first = jnp.where(me % 2 == 0, NEAR_X, NEAR_Y)
    return FAR, first, FAR - first, 0


def shaped(shape, dtype=f32):
    return jax.ShapeDtypeStruct(shape, dtype)


def call(body, name, out_shape, in_specs, out_specs, scratch=(), flops=0, moved=0, mib=VMEM_MIB):
    return pl.pallas_call(
        body,
        out_shape=out_shape,
        in_specs=in_specs,
        out_specs=out_specs,
        scratch_shapes=scratch,
        compiler_params=pltpu.CompilerParams(vmem_limit_bytes=mib * MIB),
        cost_estimate=pl.CostEstimate(flops=flops, bytes_accessed=moved, transcendentals=0),
        name=name,
    )


def start_all(sources, targets, sems, first=0):
    copies = [
        pltpu.make_async_copy(source, target, sems.at[first + i])
        for i, (source, target) in enumerate(zip(sources, targets))
    ]
    for copy in copies:
        copy.start()
    return copies


def fold_rows(rows):
    return rows + rows // 2


def encode(x, into):
    rows = x.shape[0]
    high = x.astype(bf16)
    into[:rows] = high
    base = high.astype(f32)
    left = (x - base) * pl.reciprocal(base, approx=True) * 256.0
    left = jnp.where(jnp.abs(base) < 1e-30, 0.0, jnp.clip(left, -1.0, 1.0))
    digit = jnp.floor(left * 63.5 + 64.0)
    first, second = digit[: rows // 2], digit[rows // 2 :]
    negative = second >= 64.0
    power = jnp.exp2(jnp.where(negative, second - 96.0, second - 32.0))
    packed = (first + 128.0) * power
    into[rows:] = jnp.where(negative, -packed, packed).astype(bf16)


def decode(ref):
    rows = ref.shape[0] * 2 // 3
    packed = ref[rows:].astype(f32)
    size = jnp.abs(packed)
    power = jnp.floor(jnp.log2(size) + 1e-3)
    first = jnp.floor(size * jnp.exp2(7.0 - power) + 0.5) - 128.0
    second = power + jnp.where(packed < 0.0, 89.0, 25.0)
    digit = jnp.concatenate([first, second], axis=0)
    base = ref[:rows].astype(f32)
    return base + base * ((digit - 63.5) * (1.0 / (63.5 * 256.0)))


def project_body(
    owner, rows_ref, cot_ref, act_ref, theirs, own_theirs, out_ref,
    held, cot, rows, left, grads, picks, slots, sems, out_sems, small_sems, pick_sems,
):
    count, tokens, share = held.shape
    group_w = cot.shape[1]
    samples = rows.shape[1]
    per_tile = share // FACTOR_BLOCK
    me = lax.axis_index("dp")
    z = lax.axis_index("tensor")
    half = count // 2
    tiles = [me ^ m ^ CORE for m in routes(me ^ CORE)] + [me ^ m for m in routes(me)]
    targets = [theirs.at[i] for i in range(half - 1)] + [own_theirs.at[0]]

    small = start_all([cot_ref, rows_ref], [cot, rows], small_sems)
    starts = [pl.multiple_of(t * share, share) for t in tiles]
    loads = [
        pltpu.make_async_copy(act_ref.at[:, pl.ds(start, share)], held.at[i], sems.at[i])
        for i, start in enumerate(starts)
    ]
    for load in loads[:PROJECT_AHEAD]:
        load.start()

    for d in range(count):
        slots[0, d] = 0
        slots[1, d] = 0
    for b in range(owner.shape[0]):
        holder = owner[b]
        rank = slots[0, holder]
        slots[0, holder] = rank + 1
        slots[1, holder] = jnp.where(rank == z, b, slots[1, holder])

    for copy in small:
        copy.wait()
    left[:group_w] = cot[...].astype(f32).T.astype(bf16)
    places = lax.broadcasted_iota(jnp.int32, (tokens, samples), 0)
    left[group_w:] = (places == rows[...]).astype(f32).T.astype(bf16)

    blocks = count * per_tile
    stores = []

    def keep(block, values):
        for k in range(2):
            picks[2 * block + k] = values[k * samples // 2 : (k + 1) * samples // 2].astype(bf16)

    def pass_on(half_block, many, dest, place, n):
        return start_all([picks.at[pl.ds(half_block, many)]], [out_ref.at[dest, pl.ds(place, many)]], pick_sems, n)

    keep(blocks, jnp.dot(left[group_w:], cot[...], preferred_element_type=f32))
    for d in range(count):
        stores += pass_on(2 * blocks + d % 2, 1, d, 6, 3 * d + 2)
    for i in range(count):
        if i % 2 == 0:
            loads[i].wait()
            loads[i + 1].wait()
            for load in loads[i + PROJECT_AHEAD : i + PROJECT_AHEAD + 2]:
                load.start()
        if i < half:
            product = jnp.dot(left[...], held[i], preferred_element_type=f32)
            grads[i] = product[:group_w]
            stores += start_all([grads.at[i]], [targets[i]], out_sems, i)
            picked = product[group_w:]
        else:
            picked = jnp.dot(left[group_w:], held[i], preferred_element_type=f32)
        for j in range(per_tile):
            keep(tiles[i] * per_tile + j, picked[:, j * FACTOR_BLOCK : (j + 1) * FACTOR_BLOCK])
        stores += pass_on(2 * (tiles[i] * per_tile + 2 * (z % 2)), 4, tiles[i], 0, 3 * i)
    for d in range(count):
        stores += pass_on(2 * slots[1, d], 2, d, 4, 3 * d + 1)
    for store in stores:
        store.wait()


def project(block_owner, sampled_rows, cotangent, activations, count):
    samples = sampled_rows.shape[0]
    tokens, group_w = cotangent.shape
    model_width = activations.shape[1]
    share = model_width // count
    one = shaped((1, group_w, share))
    rest = shaped((count // 2 - 1, group_w, share))
    return call(
        project_body,
        "project",
        (rest, one, shaped((count, 7, samples // 2, FACTOR_BLOCK), bf16)),
        [SMEM, ANY, ANY, ANY],
        (ANY,) * 3,
        [
            pltpu.VMEM((count, tokens, share), bf16),
            pltpu.VMEM((tokens, group_w), bf16),
            pltpu.VMEM((1, samples), jnp.int32),
            pltpu.VMEM((group_w + samples, tokens), bf16),
            pltpu.VMEM((count // 2, group_w, share), f32),
            pltpu.VMEM((2 * (model_width // FACTOR_BLOCK + 1), samples // 2, FACTOR_BLOCK), bf16),
            pltpu.SMEM((2, count), jnp.int32),
            pltpu.SemaphoreType.DMA((count,)),
            pltpu.SemaphoreType.DMA((count // 2,)),
            pltpu.SemaphoreType.DMA((2,)),
            pltpu.SemaphoreType.DMA((3 * count,)),
        ],
        flops=2 * tokens * (group_w + samples) * model_width,
        moved=2 * tokens * model_width + 2 * group_w * model_width,
        mib=PROJECT_MIB,
    )(block_owner, sampled_rows[None, :], cotangent, activations)


def sum_body(which, cot_ref, act_ref, got_ref, own_got_ref, *refs):
    count = len(which)
    outs, (cot, held, got, left, wire, plain, sems, got_sems, out_sems) = refs[-9 - count : -9], refs[-9:]
    width = held.shape[2]
    share = got_ref.shape[2]
    parts = share // width
    me = lax.axis_index("dp")
    starts = [pl.multiple_of((me ^ routes(me)[i]) * share, share) for i in which]
    work = [(i, p) for i in range(count) for p in range(parts)]
    first = start_all([cot_ref], [cot], sems)[0]

    def fetch(n):
        i, p = work[n]
        tile = act_ref.at[:, pl.ds(starts[i] + p * width, width)]
        source, at = (own_got_ref, 0) if which[i] == 3 else (got_ref, which[i])
        come = source.at[at, :, pl.ds(p * width, width)]
        return start_all([tile], [held.at[n]], sems, 1 + n) + start_all([come], [got.at[n]], got_sems, n)

    loads = [fetch(n) for n in range(min(AHEAD, len(work)))]
    first.wait()
    left[...] = cot[...].astype(f32).T.astype(bf16)
    stores = []
    for n, (i, p) in enumerate(work):
        loads[n][0].wait()
        if n + AHEAD < len(work):
            loads.append(fetch(n + AHEAD))
        product = jnp.dot(left[...], held[n], preferred_element_type=f32)
        loads[n][1].wait()
        if which[i] < 2:
            encode(product + got[n], wire.at[n])
            source = wire.at[n]
        else:
            plain[n] = product + got[n]
            source = plain.at[n]
        stores += start_all([source], [outs[i].at[:, pl.ds(p * width, width)]], out_sems, n)
    for store in stores:
        store.wait()


def hop_body(rest, come, _, out_ref, rest_in, come_in, out, sems, out_sems):
    parts = rest_in.shape[0]
    width = rest_in.shape[2]
    loads, stores = [], []
    for p in range(parts):
        columns = pl.ds(p * width, width)
        loads.append(start_all([rest.at[:, columns], come.at[:, columns]], [rest_in.at[p], come_in.at[p]], sems, 2 * p))
    for p in range(parts):
        for load in loads[p]:
            load.wait()
        encode(rest_in[p] + decode(come_in.at[p]), out.at[p])
        stores += start_all([out.at[p]], [out_ref.at[:, pl.ds(p * width, width)]], out_sems, p)
    for store in stores:
        store.wait()


def two(x):
    high = x.astype(bf16)
    return high, (x - high.astype(f32)).astype(bf16)


def newton_step(lows, currents, last):
    def dot(a, b):
        return jnp.dot(a, b, preferred_element_type=f32)

    parts = [two(low) for low in lows]
    next_lows, next_currents = [], []
    if not last:
        for low, (high_part, low_part) in zip(lows, parts):
            mixed = dot(high_part, low_part)
            next_lows.append(2.0 * low - (dot(high_part, high_part) + (mixed + mixed.T)))
    for current, (high_part, low_part) in zip(currents, parts):
        high, rest = two(current)
        product = dot(
            jnp.concatenate([high, rest, high], axis=1),
            jnp.concatenate([high_part, high_part, low_part], axis=0),
        )
        next_currents.append(2.0 * current - product)
    return next_lows, next_currents


def places(extent):
    return (
        lax.broadcasted_iota(jnp.int32, (extent, extent), 0),
        lax.broadcasted_iota(jnp.int32, (extent, extent), 1),
    )


FOLD_ROWS = 16


def fold(matrix, into):
    half = matrix.shape[0] // 2
    row, column = places(half)
    low = matrix[half:, half:]
    both = jnp.where(row <= column, matrix[:half, :half], low)
    coded = fold_rows(half)
    encode(jnp.concatenate([both, matrix[:half, half:]], axis=1), into.at[:coded])
    left = jnp.sum(jnp.where(row == column, low, 0.0), axis=0, keepdims=True)
    line = lax.broadcasted_iota(jnp.int32, (FOLD_ROWS, 2 * half), 0)
    diagonal = jnp.zeros((FOLD_ROWS, 2 * half), f32)
    for part in range(3):
        high = left.astype(bf16).astype(f32)
        diagonal = jnp.where(line == part, jnp.concatenate([high, high], axis=1), diagonal)
        left = left - high
    into[coded:] = diagonal.astype(bf16)


def unfold(packed):
    half = packed.shape[1] // 2
    coded = fold_rows(half)
    row, column = places(half)
    values = decode(packed.at[:coded])
    diagonal = jnp.sum(packed[coded:].astype(f32), axis=0, keepdims=True)[:, :half]
    both, corner = values[:, :half], values[:, half:]
    turned = both.T
    top = jnp.where(row <= column, both, turned)
    low = jnp.where(row == column, diagonal, jnp.where(row > column, both, turned))
    return jnp.concatenate(
        [jnp.concatenate([top, corner], axis=1), jnp.concatenate([corner.T, low], axis=1)], axis=0
    )


def inverses_of(samples, scale):
    row, column = places(FACTOR_BLOCK)
    eye = (row == column).astype(f32)
    lows, currents = [], []
    for rows in samples:
        gram = lax.dot_general(
            rows, rows, (((0,), (0,)), ((), ())), preferred_element_type=f32
        )
        matrix = gram * scale + DAMPING * eye
        bound = jnp.max(jnp.sum(jnp.abs(matrix), axis=1, keepdims=True), axis=0, keepdims=True)
        inverse_bound = 1.0 / bound
        low = matrix * inverse_bound
        lows.append(low)
        currents.append((2.0 * eye - low) * inverse_bound)
    lows = newton_step(lows, [], False)[0]
    for turn in range(1, ITERS):
        lows, currents = newton_step(lows, currents, turn == ITERS - 1)
    return currents


def invert_body(scale, rows_ref, all_ref, own_ref, cot_ref, rows, sems):
    load, copy = start_all([rows_ref.at[:, pl.ds(0, 6)], rows_ref.at[:, 6]], [rows, cot_ref], sems)
    load.wait()
    first, second, own = inverses_of(
        [rows[:, 2 * m : 2 * m + 2].reshape(-1, FACTOR_BLOCK) for m in range(3)], scale
    )
    fold(first, all_ref.at[0])
    fold(second, all_ref.at[1])
    fold(own, all_ref.at[2])
    own_ref[...] = all_ref[2]
    copy.wait()


def group_body(scale, half_ref, other_ref, _, __, out_ref, rows, sems):
    loads = start_all([half_ref, other_ref], [rows.at[0], rows.at[1]], sems)
    for load in loads:
        load.wait()
    parts = two(inverses_of([rows[...].reshape(-1, FACTOR_BLOCK)], scale)[0].T)
    out_ref[...] = jnp.concatenate(parts, axis=0)


def ready_body(own_ref, near_ref, here, beside, _, sum_ref, split, own, near, need, sems):
    loads = start_all(
        [here.at[pl.ds(0, 2)], beside.at[pl.ds(0, 2)], own_ref, near_ref],
        [need.at[pl.ds(0, 2)], need.at[pl.ds(2, 2)], own, near],
        sems,
    )
    odd = lax.axis_index("tensor") % 2
    for k in range(2):
        loads[k].wait()
        for p in range(2):
            high, low = two(unfold(need.at[2 * k + p]))
            at = 2 * (odd if k == 0 else 1 - odd) + p
            split[0, at] = high
            split[1, at] = low
    for load in loads[2:]:
        load.wait()
    sum_ref[...] = own[...] + decode(near)


def owned_body(owner, here, beside, two_off, three_off, _, out_ref, done_ref, held, sems):
    loads = start_all([here.at[2], beside.at[2], two_off, three_off], [held.at[k] for k in range(4)], sems)
    z = lax.axis_index("tensor")
    me = lax.axis_index("dp")
    count = jnp.int32(0)
    for b in range(owner.shape[0]):
        count = count + jnp.where(owner[b] == me, 1, 0)
    for k, load in enumerate(loads):
        load.wait()
        slot = z ^ k
        out_ref[slot] = jnp.where(slot < count, unfold(held.at[k]), 0.0)
    done_ref[...] = jnp.zeros(done_ref.shape, f32)


def finish_body(split_ref, g_ref, sum_ref, come, _, step_out, split, left, total, come_in, step, sems, out_sems):
    width = FACTOR_BLOCK
    loads = start_all([g_ref, sum_ref, come, split_ref], [left, total, come_in, split], sems)

    def dot(a, c, dims):
        return lax.dot_general(a, c, (dims, ((), ())), preferred_element_type=f32)

    for load in loads[:3]:
        load.wait()
    sum_high, sum_low = two(total[...] + decode(come_in))
    both = dot(left[...], sum_high, ((1,), (0,)))
    right_high, right_low = two(both[:width] + (both[width:] + dot(left[:width], sum_low, ((1,), (0,)))))
    loads[3].wait()
    stores = []
    for b in range(split.shape[1]):
        part = slice(b * width, (b + 1) * width)
        both = dot(split[:, b].reshape(2 * width, width), right_high[:, part], ((1,), (1,)))
        step[b] = both[:width] + (both[width:] + dot(split[0, b], right_low[:, part], ((1,), (1,))))
        stores += start_all([step.at[b]], [step_out.at[part, :]], out_sems, b)
    for store in stores:
        store.wait()


def dma(count):
    return pltpu.SemaphoreType.DMA((count,))


def sum_cores(name, which, cotangent, activations, got, own_got, *after):
    tokens, group_w = cotangent.shape
    share = got.shape[2]
    wired = (fold_rows(group_w), share)
    steps, width = len(which) * SUM_PARTS, share // SUM_PARTS
    return call(
        functools.partial(sum_body, which),
        name,
        tuple(shaped(wired, bf16) if i < 2 else shaped((group_w, share)) for i in which),
        [ANY] * (4 + len(after)),
        (ANY,) * len(which),
        [
            pltpu.VMEM(cotangent.shape, bf16),
            pltpu.VMEM((steps, tokens, width), bf16),
            pltpu.VMEM((steps, group_w, width), f32),
            pltpu.VMEM((group_w, tokens), bf16),
            pltpu.VMEM((steps, wired[0], width), bf16),
            pltpu.VMEM((steps, group_w, width), f32),
            dma(1 + steps),
            dma(steps),
            dma(steps),
        ],
        moved=4 * MIB * len(which),
        mib=SUM_MIB,
    )(cotangent, activations, got, own_got, *after)


def invert(rows, scale):
    count, _, samples, _ = rows.shape
    packed = shaped((fold_rows(FACTOR_BLOCK // 2) + FOLD_ROWS, FACTOR_BLOCK), bf16)
    return call(
        functools.partial(invert_body, scale),
        "invert_blocks",
        (shaped((3, *packed.shape), bf16), packed, shaped((count, samples, FACTOR_BLOCK), bf16)),
        [ANY],
        (VMEM, VMEM, ANY),
        [pltpu.VMEM((count, 6, samples, FACTOR_BLOCK), bf16), dma(2)],
        flops=2 * 3 * 4 * 18 * FACTOR_BLOCK**3,
        moved=2 * MIB,
    )(rows)


def invert_group(half, other, after, and_after, scale):
    return call(
        functools.partial(group_body, scale),
        "invert_group",
        shaped((2 * FACTOR_BLOCK, FACTOR_BLOCK), bf16),
        [ANY] * 4,
        VMEM,
        [pltpu.VMEM((2, *half.shape), bf16), dma(2)],
    )(half, other, after, and_after)


def hop(rest, come, after):
    group_w, share = rest.shape
    wired = come.shape
    width = share // HOP_PARTS
    return call(
        hop_body,
        "hop",
        shaped(wired, bf16),
        [ANY] * 3,
        ANY,
        [pltpu.VMEM((HOP_PARTS, group_w, width), f32)]
        + [pltpu.VMEM((HOP_PARTS, wired[0], width), bf16)] * 2
        + [dma(2 * HOP_PARTS), dma(HOP_PARTS)],
    )(rest, come, after)


def ready(own_sum, near, inverses, beside, after):
    square = (4, FACTOR_BLOCK, FACTOR_BLOCK)
    held = pltpu.VMEM((4, *inverses.shape[1:]), bf16)
    return call(
        ready_body,
        "ready",
        (shaped(own_sum.shape), shaped((2, *square), bf16)),
        [ANY] * 5,
        (VMEM,) * 2,
        [pltpu.VMEM(own_sum.shape, f32), pltpu.VMEM(near.shape, bf16), held, dma(4)],
    )(own_sum, near, inverses, beside, after)


def owned_blocks(block_owner, inverses, beside, two_off, three_off, after):
    return call(
        owned_body,
        "owned",
        (shaped((4, FACTOR_BLOCK, FACTOR_BLOCK)), shaped((8, 128))),
        [SMEM] + [ANY] * 5,
        (VMEM,) * 2,
        [pltpu.VMEM((4, *two_off.shape), bf16), dma(4)],
        flops=OWNED_FLOPS,
    )(block_owner, inverses, beside, two_off, three_off, after)


def finish(split, g_parts, so_far, come, after):
    group_w, share = so_far.shape
    blocks = share // FACTOR_BLOCK
    return call(
        finish_body,
        "finish",
        shaped((share, group_w)),
        [ANY] * 5,
        ANY,
        [
            pltpu.VMEM(split.shape, bf16),
            pltpu.VMEM(g_parts.shape, bf16),
            pltpu.VMEM(so_far.shape, f32),
            pltpu.VMEM(come.shape, bf16),
            pltpu.VMEM((blocks, FACTOR_BLOCK, group_w), f32),
            dma(4),
            dma(blocks),
        ],
        moved=6 * MIB,
    )(split, g_parts, so_far, come, after)


def square_device(activations, cotangent, sampled_rows, block_owner):
    dp_count = lax.axis_size("dp")
    samples = sampled_rows.shape[0]

    def swap(block, bit, axis="dp"):
        count = lax.axis_size(axis)
        return lax.ppermute(block, axis, [(i, i ^ bit) for i in range(count)])

    def travel(block, even, odd):
        return lax.ppermute(block, "dp", [(i, i ^ (odd if i % 2 else even)) for i in range(dp_count)])

    theirs, own_theirs, picked = project(
        block_owner, sampled_rows, cotangent, activations, dp_count
    )
    got = swap(theirs, CORE)
    rows = lax.all_to_all(picked, "dp", split_axis=0, concat_axis=0, tiled=True)
    own_got = swap(own_theirs, CORE)

    (far,) = sum_cores("sum_far", (0,), cotangent, activations, got, got)
    far_come = travel(far, NEAR_X, NEAR_Y)
    near, rest, own_sum = sum_cores("sum_near", (1, 2, 3), cotangent, activations, got, own_got, far)
    near_come = travel(near, NEAR_X, NEAR_Y)

    inverses, own, half = invert(rows, 1.0 / (samples * dp_count))
    beside = swap(inverses, 1, "tensor")
    two_off, three_off = swap(own, 2, "tensor"), swap(own, 3, "tensor")

    hopped = hop(rest, far_come, inverses)
    come_last = travel(hopped, NEAR_Y, NEAR_X)

    other = swap(half, CORE)
    g_parts = invert_group(half, other, near_come, hopped, activations.shape[0] / samples)
    so_far, split = ready(own_sum, near_come, inverses, beside, g_parts)
    owned, done = owned_blocks(block_owner, inverses, beside, two_off, three_off, so_far)
    step = finish(split, g_parts, so_far, come_last, done)
    return step, owned


def solution(mesh):
    def per_device(activations, cotangent, sampled_rows, block_owner):
        block_total = activations.shape[1] // FACTOR_BLOCK
        dp_count, depth = mesh.shape["dp"], mesh.shape["tensor"]
        fits = (
            dp_count == 8
            and depth == 4
            and block_total == dp_count * depth
            and cotangent.shape[1] == FACTOR_BLOCK
            and sampled_rows.shape[0] % 16 == 0
            and activations.shape[0] % 128 == 0
        )
        run = square_device if fits else general_device
        return run(activations, cotangent, sampled_rows, block_owner)

    return jax.shard_map(
        per_device,
        mesh=mesh,
        in_specs=(P("dp", None), P("dp", "tensor"), P("dp"), P()),
        out_specs=(P("dp", "tensor"), P("dp", None, None)),
        check_vma=False,
    )
```

```python
import functools

import jax
import jax.numpy as jnp
from jax import lax
from jax.experimental import pallas as pl
from jax.experimental.pallas import tpu as pltpu
from jax.sharding import PartitionSpec as P

S_DEV = 64
FACTOR_BLOCK = 256
ITERS = 10


DAMPING = 0.05
precise_mode = lax.Precision.HIGHEST
f32 = jnp.float32
bf16 = jnp.bfloat16


def block_rank(block_owner):
    block_total = block_owner.shape[0]
    same_owner = block_owner[:, None] == block_owner[None, :]
    positions = jnp.arange(block_total, dtype=jnp.int32)
    before = positions[None, :] < positions[:, None]
    return jnp.sum((same_owner & before).astype(jnp.int32), axis=1)


def from_partner(block, axis, apart):
    count = lax.axis_size(axis)
    route = []
    for low in range(count):
        high = low | 1 << apart
        if high != low and high < count:
            route += [(low, high), (high, low)]
    return lax.ppermute(block, axis, route)


def newton_inverse(matrix):
    extent = matrix.shape[-1]
    identity = jnp.eye(extent, dtype=jnp.float32)
    row_bound = jnp.max(jnp.sum(jnp.abs(matrix), axis=2), axis=1)
    initial = identity[None, :, :] / row_bound[:, None, None]

    def advance(turn_index, current):
        product = jnp.einsum("nij,njk->nik", matrix, current, precision=precise_mode)
        return jnp.einsum(
            "nij,njk->nik", current, 2.0 * identity[None, :, :] - product, precision=precise_mode
        )

    return lax.fori_loop(0, ITERS, advance, initial)


def owner_grams(received):
    return jnp.einsum("pcsk,pcsl->ckl", received, received, preferred_element_type=jnp.float32)


def general_device(activations, cotangent, sampled_rows, block_owner):
    tok_local = activations.shape[0]
    model_width = activations.shape[1]
    group_w = cotangent.shape[1]
    dp_count = lax.axis_size("dp")
    my_dp = lax.axis_index("dp")
    block_total = model_width // FACTOR_BLOCK
    capacity = max(1, block_total // dp_count)
    row_share = model_width // dp_count
    samples_all = S_DEV * dp_count
    grad_rows = lax.psum_scatter(
        lax.dot_general(
            activations, cotangent, (((0,), (0,)), ((), ())), preferred_element_type=jnp.float32
        ),
        "dp",
        scatter_dimension=0,
        tiled=True,
    )
    picked_acts = jnp.take(activations, sampled_rows, axis=0)
    picked_grads = jnp.take(cotangent, sampled_rows, axis=0)
    g_partial = lax.dot_general(
        picked_grads, picked_grads, (((0,), (0,)), ((), ())), preferred_element_type=jnp.float32
    )
    g_total = lax.psum(g_partial, "dp")
    g_factor = g_total * (tok_local / S_DEV) + DAMPING * jnp.eye(group_w, dtype=jnp.float32)
    slot_of = block_owner * capacity + block_rank(block_owner)
    dest_ids = jnp.arange(dp_count * capacity, dtype=jnp.int32)
    chooser = (slot_of[None, :] == dest_ids[:, None]).astype(jnp.bfloat16)
    row_blocks = picked_acts.reshape(S_DEV, block_total, FACTOR_BLOCK)
    outgoing = lax.dot_general(
        chooser, row_blocks, (((1,), (1,)), ((), ())), preferred_element_type=jnp.float32
    )
    outgoing = outgoing.astype(jnp.bfloat16).reshape(dp_count, capacity, S_DEV, FACTOR_BLOCK)
    gram_slots = owner_grams(
        lax.all_to_all(outgoing, "dp", split_axis=0, concat_axis=0, tiled=True)
    )
    a_factor = (
        gram_slots / samples_all + DAMPING * jnp.eye(FACTOR_BLOCK, dtype=jnp.float32)[None, :, :]
    )
    input_factor_inverse = newton_inverse(a_factor)
    owned_count = jnp.sum((block_owner == my_dp).astype(jnp.int32))
    slot_used = jnp.arange(capacity, dtype=jnp.int32) < owned_count
    owned_out = jnp.where(slot_used[:, None, None], input_factor_inverse, 0.0)
    g_inverse = newton_inverse(g_factor[None, :, :])[0]
    per_dev = max(1, row_share // FACTOR_BLOCK)
    rows_each = min(row_share, FACTOR_BLOCK)
    first_block = my_dp * row_share // FACTOR_BLOCK
    need_ids = first_block + jnp.arange(per_dev, dtype=jnp.int32)
    need_slots = jnp.take(slot_of, need_ids)
    row_offset = my_dp * row_share % FACTOR_BLOCK
    shard_piece = lax.all_gather(owned_out, "dp", axis=0, tiled=True)
    rows_part = lax.dynamic_slice_in_dim(shard_piece, row_offset, rows_each, 1)
    slot_ids = jnp.arange(shard_piece.shape[0], dtype=jnp.int32)
    selector = (need_slots[:, None] == slot_ids[None, :]).astype(jnp.float32)
    inverse_rows = jnp.einsum("jm,mkl->jkl", selector, rows_part, precision=precise_mode)
    grad_right = jnp.dot(
        grad_rows, g_inverse, precision=precise_mode, preferred_element_type=jnp.float32
    )
    if row_share < FACTOR_BLOCK:
        partner = from_partner(grad_right, "dp", 0)
        is_lower = my_dp % 2 == 0
        joined = jnp.where(
            is_lower,
            jnp.concatenate([grad_right, partner], 0),
            jnp.concatenate([partner, grad_right], 0),
        )
        complete_rows = joined[None, :, :]
    else:
        complete_rows = grad_right.reshape(per_dev, FACTOR_BLOCK, group_w)
    natural_step = jnp.einsum("jrk,jkl->jrl", inverse_rows, complete_rows, precision=precise_mode)
    return (natural_step.reshape(row_share, group_w), owned_out)


MIB = 1 << 20
VMEM_MIB = 32
PROJECT_MIB = 64
SUM_MIB = 64
AHEAD = 3
PROJECT_AHEAD = 6
HOP_PARTS = 2
SUM_PARTS = 2
OWNED_FLOPS = 20_000_000_000
ANY = pl.BlockSpec(memory_space=pl.ANY)
VMEM = pl.BlockSpec(memory_space=pltpu.VMEM)
SMEM = pl.BlockSpec(memory_space=pltpu.SMEM)
CORE, NEAR_X, NEAR_Y, FAR = 1, 2, 4, 6


def routes(me):
    first = jnp.where(me % 2 == 0, NEAR_X, NEAR_Y)
    return FAR, first, FAR - first, 0


def shaped(shape, dtype=f32):
    return jax.ShapeDtypeStruct(shape, dtype)


def call(body, name, out_shape, in_specs, out_specs, scratch=(), flops=0, moved=0, mib=VMEM_MIB):
    return pl.pallas_call(
        body,
        out_shape=out_shape,
        in_specs=in_specs,
        out_specs=out_specs,
        scratch_shapes=scratch,
        compiler_params=pltpu.CompilerParams(vmem_limit_bytes=mib * MIB),
        cost_estimate=pl.CostEstimate(flops=flops, bytes_accessed=moved, transcendentals=0),
        name=name,
    )


def start_all(sources, targets, sems, first=0):
    copies = [
        pltpu.make_async_copy(source, target, sems.at[first + i])
        for i, (source, target) in enumerate(zip(sources, targets))
    ]
    for copy in copies:
        copy.start()
    return copies


def fold_rows(rows):
    return rows + rows // 2


def encode(x, into):
    rows = x.shape[0]
    high = x.astype(bf16)
    into[:rows] = high
    base = high.astype(f32)
    left = (x - base) * pl.reciprocal(base, approx=True) * 256.0
    left = jnp.where(jnp.abs(base) < 1e-30, 0.0, jnp.clip(left, -1.0, 1.0))
    digit = jnp.floor(left * 63.5 + 64.0)
    first, second = digit[: rows // 2], digit[rows // 2 :]
    negative = second >= 64.0
    power = jnp.exp2(jnp.where(negative, second - 96.0, second - 32.0))
    packed = (first + 128.0) * power
    into[rows:] = jnp.where(negative, -packed, packed).astype(bf16)


def decode(ref):
    rows = ref.shape[0] * 2 // 3
    packed = ref[rows:].astype(f32)
    size = jnp.abs(packed)
    power = jnp.floor(jnp.log2(size) + 1e-3)
    first = jnp.floor(size * jnp.exp2(7.0 - power) + 0.5) - 128.0
    second = power + jnp.where(packed < 0.0, 89.0, 25.0)
    digit = jnp.concatenate([first, second], axis=0)
    base = ref[:rows].astype(f32)
    return base + base * ((digit - 63.5) * (1.0 / (63.5 * 256.0)))


def project_body(
    owner, rows_ref, cot_ref, act_ref, theirs, own_theirs, out_ref,
    held, cot, rows, left, grads, picks, slots, sems, out_sems, small_sems, pick_sems,
):
    count, tokens, share = held.shape
    group_w = cot.shape[1]
    samples = rows.shape[1]
    per_tile = share // FACTOR_BLOCK
    me = lax.axis_index("dp")
    z = lax.axis_index("tensor")
    half = count // 2
    tiles = [me ^ m ^ CORE for m in routes(me ^ CORE)] + [me ^ m for m in routes(me)]
    targets = [theirs.at[i] for i in range(half - 1)] + [own_theirs.at[0]]

    small = start_all([cot_ref, rows_ref], [cot, rows], small_sems)
    starts = [pl.multiple_of(t * share, share) for t in tiles]
    loads = [
        pltpu.make_async_copy(act_ref.at[:, pl.ds(start, share)], held.at[i], sems.at[i])
        for i, start in enumerate(starts)
    ]
    for load in loads[:PROJECT_AHEAD]:
        load.start()

    for d in range(count):
        slots[0, d] = 0
        slots[1, d] = 0
    for b in range(owner.shape[0]):
        holder = owner[b]
        rank = slots[0, holder]
        slots[0, holder] = rank + 1
        slots[1, holder] = jnp.where(rank == z, b, slots[1, holder])

    for copy in small:
        copy.wait()
    left[:group_w] = cot[...].astype(f32).T.astype(bf16)
    places = lax.broadcasted_iota(jnp.int32, (tokens, samples), 0)
    left[group_w:] = (places == rows[...]).astype(f32).T.astype(bf16)

    blocks = count * per_tile
    stores = []

    def keep(block, values):
        for k in range(2):
            picks[2 * block + k] = values[k * samples // 2 : (k + 1) * samples // 2].astype(bf16)

    def pass_on(half_block, many, dest, place, n):
        return start_all([picks.at[pl.ds(half_block, many)]], [out_ref.at[dest, pl.ds(place, many)]], pick_sems, n)

    keep(blocks, jnp.dot(left[group_w:], cot[...], preferred_element_type=f32))
    for d in range(count):
        stores += pass_on(2 * blocks + d % 2, 1, d, 6, 3 * d + 2)
    for i in range(count):
        if i % 2 == 0:
            loads[i].wait()
            loads[i + 1].wait()
            for load in loads[i + PROJECT_AHEAD : i + PROJECT_AHEAD + 2]:
                load.start()
        if i < half:
            product = jnp.dot(left[...], held[i], preferred_element_type=f32)
            grads[i] = product[:group_w]
            stores += start_all([grads.at[i]], [targets[i]], out_sems, i)
            picked = product[group_w:]
        else:
            picked = jnp.dot(left[group_w:], held[i], preferred_element_type=f32)
        for j in range(per_tile):
            keep(tiles[i] * per_tile + j, picked[:, j * FACTOR_BLOCK : (j + 1) * FACTOR_BLOCK])
        stores += pass_on(2 * (tiles[i] * per_tile + 2 * (z % 2)), 4, tiles[i], 0, 3 * i)
    for d in range(count):
        stores += pass_on(2 * slots[1, d], 2, d, 4, 3 * d + 1)
    for store in stores:
        store.wait()


def project(block_owner, sampled_rows, cotangent, activations, count):
    samples = sampled_rows.shape[0]
    tokens, group_w = cotangent.shape
    model_width = activations.shape[1]
    share = model_width // count
    one = shaped((1, group_w, share))
    rest = shaped((count // 2 - 1, group_w, share))
    return call(
        project_body,
        "project",
        (rest, one, shaped((count, 7, samples // 2, FACTOR_BLOCK), bf16)),
        [SMEM, ANY, ANY, ANY],
        (ANY,) * 3,
        [
            pltpu.VMEM((count, tokens, share), bf16),
            pltpu.VMEM((tokens, group_w), bf16),
            pltpu.VMEM((1, samples), jnp.int32),
            pltpu.VMEM((group_w + samples, tokens), bf16),
            pltpu.VMEM((count // 2, group_w, share), f32),
            pltpu.VMEM((2 * (model_width // FACTOR_BLOCK + 1), samples // 2, FACTOR_BLOCK), bf16),
            pltpu.SMEM((2, count), jnp.int32),
            pltpu.SemaphoreType.DMA((count,)),
            pltpu.SemaphoreType.DMA((count // 2,)),
            pltpu.SemaphoreType.DMA((2,)),
            pltpu.SemaphoreType.DMA((3 * count,)),
        ],
        flops=2 * tokens * (group_w + samples) * model_width,
        moved=2 * tokens * model_width + 2 * group_w * model_width,
        mib=PROJECT_MIB,
    )(block_owner, sampled_rows[None, :], cotangent, activations)


def sum_body(which, cot_ref, act_ref, got_ref, own_got_ref, *refs):
    count = len(which)
    outs, (cot, held, got, left, wire, plain, sems, got_sems, out_sems) = refs[-9 - count : -9], refs[-9:]
    width = held.shape[2]
    share = got_ref.shape[2]
    parts = share // width
    me = lax.axis_index("dp")
    starts = [pl.multiple_of((me ^ routes(me)[i]) * share, share) for i in which]
    work = [(i, p) for i in range(count) for p in range(parts)]
    first = start_all([cot_ref], [cot], sems)[0]

    def fetch(n):
        i, p = work[n]
        tile = act_ref.at[:, pl.ds(starts[i] + p * width, width)]
        source, at = (own_got_ref, 0) if which[i] == 3 else (got_ref, which[i])
        come = source.at[at, :, pl.ds(p * width, width)]
        return start_all([tile], [held.at[n]], sems, 1 + n) + start_all([come], [got.at[n]], got_sems, n)

    loads = [fetch(n) for n in range(min(AHEAD, len(work)))]
    first.wait()
    left[...] = cot[...].astype(f32).T.astype(bf16)
    stores = []
    for n, (i, p) in enumerate(work):
        loads[n][0].wait()
        if n + AHEAD < len(work):
            loads.append(fetch(n + AHEAD))
        product = jnp.dot(left[...], held[n], preferred_element_type=f32)
        loads[n][1].wait()
        if which[i] < 2:
            encode(product + got[n], wire.at[n])
            source = wire.at[n]
        else:
            plain[n] = product + got[n]
            source = plain.at[n]
        stores += start_all([source], [outs[i].at[:, pl.ds(p * width, width)]], out_sems, n)
    for store in stores:
        store.wait()


def hop_body(rest, come, _, out_ref, rest_in, come_in, out, sems, out_sems):
    parts = rest_in.shape[0]
    width = rest_in.shape[2]
    loads, stores = [], []
    for p in range(parts):
        columns = pl.ds(p * width, width)
        loads.append(start_all([rest.at[:, columns], come.at[:, columns]], [rest_in.at[p], come_in.at[p]], sems, 2 * p))
    for p in range(parts):
        for load in loads[p]:
            load.wait()
        encode(rest_in[p] + decode(come_in.at[p]), out.at[p])
        stores += start_all([out.at[p]], [out_ref.at[:, pl.ds(p * width, width)]], out_sems, p)
    for store in stores:
        store.wait()


def two(x):
    high = x.astype(bf16)
    return high, (x - high.astype(f32)).astype(bf16)


def newton_step(lows, currents, last):
    def dot(a, b):
        return jnp.dot(a, b, preferred_element_type=f32)

    parts = [two(low) for low in lows]
    next_lows, next_currents = [], []
    if not last:
        for low, (high_part, low_part) in zip(lows, parts):
            mixed = dot(high_part, low_part)
            next_lows.append(2.0 * low - (dot(high_part, high_part) + (mixed + mixed.T)))
    for current, (high_part, low_part) in zip(currents, parts):
        high, rest = two(current)
        product = dot(
            jnp.concatenate([high, rest, high], axis=1),
            jnp.concatenate([high_part, high_part, low_part], axis=0),
        )
        next_currents.append(2.0 * current - product)
    return next_lows, next_currents


def places(extent):
    return (
        lax.broadcasted_iota(jnp.int32, (extent, extent), 0),
        lax.broadcasted_iota(jnp.int32, (extent, extent), 1),
    )


FOLD_ROWS = 16


def fold(matrix, into):
    half = matrix.shape[0] // 2
    row, column = places(half)
    low = matrix[half:, half:]
    both = jnp.where(row <= column, matrix[:half, :half], low)
    coded = fold_rows(half)
    encode(jnp.concatenate([both, matrix[:half, half:]], axis=1), into.at[:coded])
    left = jnp.sum(jnp.where(row == column, low, 0.0), axis=0, keepdims=True)
    line = lax.broadcasted_iota(jnp.int32, (FOLD_ROWS, 2 * half), 0)
    diagonal = jnp.zeros((FOLD_ROWS, 2 * half), f32)
    for part in range(3):
        high = left.astype(bf16).astype(f32)
        diagonal = jnp.where(line == part, jnp.concatenate([high, high], axis=1), diagonal)
        left = left - high
    into[coded:] = diagonal.astype(bf16)


def unfold(packed):
    half = packed.shape[1] // 2
    coded = fold_rows(half)
    row, column = places(half)
    values = decode(packed.at[:coded])
    diagonal = jnp.sum(packed[coded:].astype(f32), axis=0, keepdims=True)[:, :half]
    both, corner = values[:, :half], values[:, half:]
    turned = both.T
    top = jnp.where(row <= column, both, turned)
    low = jnp.where(row == column, diagonal, jnp.where(row > column, both, turned))
    return jnp.concatenate(
        [jnp.concatenate([top, corner], axis=1), jnp.concatenate([corner.T, low], axis=1)], axis=0
    )


def inverses_of(samples, scale):
    row, column = places(FACTOR_BLOCK)
    eye = (row == column).astype(f32)
    lows, currents = [], []
    for rows in samples:
        gram = lax.dot_general(
            rows, rows, (((0,), (0,)), ((), ())), preferred_element_type=f32
        )
        matrix = gram * scale + DAMPING * eye
        bound = jnp.max(jnp.sum(jnp.abs(matrix), axis=1, keepdims=True), axis=0, keepdims=True)
        inverse_bound = 1.0 / bound
        low = matrix * inverse_bound
        lows.append(low)
        currents.append((2.0 * eye - low) * inverse_bound)
    lows = newton_step(lows, [], False)[0]
    for turn in range(1, ITERS):
        lows, currents = newton_step(lows, currents, turn == ITERS - 1)
    return currents


def invert_body(scale, rows_ref, all_ref, own_ref, cot_ref, rows, sems):
    load, copy = start_all([rows_ref.at[:, pl.ds(0, 6)], rows_ref.at[:, 6]], [rows, cot_ref], sems)
    load.wait()
    first, second, own = inverses_of(
        [rows[:, 2 * m : 2 * m + 2].reshape(-1, FACTOR_BLOCK) for m in range(3)], scale
    )
    fold(first, all_ref.at[0])
    fold(second, all_ref.at[1])
    fold(own, all_ref.at[2])
    own_ref[...] = all_ref[2]
    copy.wait()


def group_body(scale, half, other, _, __, out_ref):
    rows = jnp.concatenate([half[...].reshape(-1, FACTOR_BLOCK), other[...].reshape(-1, FACTOR_BLOCK)], axis=0)
    parts = two(inverses_of([rows], scale)[0].T)
    out_ref[...] = jnp.concatenate(parts, axis=0)


def ready_body(own, near, here, beside, _, sum_ref, split):
    odd = lax.axis_index("tensor") % 2
    for k, held in enumerate((here, beside)):
        for p in range(2):
            high, low = two(unfold(held.at[p]))
            at = 2 * (odd if k == 0 else 1 - odd) + p
            split[0, at] = high
            split[1, at] = low
    sum_ref[...] = own[...] + decode(near)


def owned_body(owner, here, beside, two_off, three_off, _, out_ref, done_ref):
    z = lax.axis_index("tensor")
    me = lax.axis_index("dp")
    count = jnp.int32(0)
    for b in range(owner.shape[0]):
        count = count + jnp.where(owner[b] == me, 1, 0)
    for k, held in enumerate((here.at[2], beside.at[2], two_off, three_off)):
        slot = z ^ k
        out_ref[slot] = jnp.where(slot < count, unfold(held), 0.0)
    done_ref[...] = jnp.zeros(done_ref.shape, f32)


def finish_body(split, left, so_far, come, _, step_out, step, out_sems):
    width = FACTOR_BLOCK

    def dot(a, c, dims):
        return lax.dot_general(a, c, (dims, ((), ())), preferred_element_type=f32)

    sum_high, sum_low = two(so_far[...] + decode(come))
    both = dot(left[...], sum_high, ((1,), (0,)))
    right_high, right_low = two(both[:width] + (both[width:] + dot(left[:width], sum_low, ((1,), (0,)))))
    stores = []
    for b in range(split.shape[1]):
        part = slice(b * width, (b + 1) * width)
        both = dot(split[:, b].reshape(2 * width, width), right_high[:, part], ((1,), (1,)))
        step[b] = both[:width] + (both[width:] + dot(split[0, b], right_low[:, part], ((1,), (1,))))
        stores += start_all([step.at[b]], [step_out.at[part, :]], out_sems, b)
    for store in stores:
        store.wait()


def dma(count):
    return pltpu.SemaphoreType.DMA((count,))


def sum_cores(name, which, cotangent, activations, got, own_got, *after):
    tokens, group_w = cotangent.shape
    share = got.shape[2]
    wired = (fold_rows(group_w), share)
    steps, width = len(which) * SUM_PARTS, share // SUM_PARTS
    return call(
        functools.partial(sum_body, which),
        name,
        tuple(shaped(wired, bf16) if i < 2 else shaped((group_w, share)) for i in which),
        [ANY] * (4 + len(after)),
        (ANY,) * len(which),
        [
            pltpu.VMEM(cotangent.shape, bf16),
            pltpu.VMEM((steps, tokens, width), bf16),
            pltpu.VMEM((steps, group_w, width), f32),
            pltpu.VMEM((group_w, tokens), bf16),
            pltpu.VMEM((steps, wired[0], width), bf16),
            pltpu.VMEM((steps, group_w, width), f32),
            dma(1 + steps),
            dma(steps),
            dma(steps),
        ],
        moved=4 * MIB * len(which),
        mib=SUM_MIB,
    )(cotangent, activations, got, own_got, *after)


def invert(rows, scale):
    count, _, samples, _ = rows.shape
    packed = shaped((fold_rows(FACTOR_BLOCK // 2) + FOLD_ROWS, FACTOR_BLOCK), bf16)
    return call(
        functools.partial(invert_body, scale),
        "invert_blocks",
        (shaped((3, *packed.shape), bf16), packed, shaped((count, samples, FACTOR_BLOCK), bf16)),
        [ANY],
        (VMEM, VMEM, ANY),
        [pltpu.VMEM((count, 6, samples, FACTOR_BLOCK), bf16), dma(2)],
        flops=2 * 3 * 4 * 18 * FACTOR_BLOCK**3,
        moved=2 * MIB,
    )(rows)


def invert_group(half, other, after, and_after, scale):
    return call(
        functools.partial(group_body, scale),
        "invert_group",
        shaped((2 * FACTOR_BLOCK, FACTOR_BLOCK), bf16),
        [VMEM, VMEM, ANY, ANY],
        VMEM,
    )(half, other, after, and_after)


def hop(rest, come, after):
    group_w, share = rest.shape
    wired = come.shape
    width = share // HOP_PARTS
    return call(
        hop_body,
        "hop",
        shaped(wired, bf16),
        [ANY] * 3,
        ANY,
        [pltpu.VMEM((HOP_PARTS, group_w, width), f32)]
        + [pltpu.VMEM((HOP_PARTS, wired[0], width), bf16)] * 2
        + [dma(2 * HOP_PARTS), dma(HOP_PARTS)],
    )(rest, come, after)


def ready(own_sum, near, inverses, beside, after):
    square = (4, FACTOR_BLOCK, FACTOR_BLOCK)
    return call(
        ready_body,
        "ready",
        (shaped(own_sum.shape), shaped((2, *square), bf16)),
        [VMEM] * 4 + [ANY],
        (VMEM,) * 2,
    )(own_sum, near, inverses, beside, after)


def owned_blocks(block_owner, inverses, beside, two_off, three_off, after):
    return call(
        owned_body,
        "owned",
        (shaped((4, FACTOR_BLOCK, FACTOR_BLOCK)), shaped((8, 128))),
        [SMEM] + [VMEM] * 4 + [ANY],
        (VMEM,) * 2,
        flops=OWNED_FLOPS,
    )(block_owner, inverses, beside, two_off, three_off, after)


def finish(split, g_parts, so_far, come, after):
    group_w, share = so_far.shape
    blocks = share // FACTOR_BLOCK
    return call(
        finish_body,
        "finish",
        shaped((share, group_w)),
        [VMEM] * 4 + [ANY],
        ANY,
        [pltpu.VMEM((blocks, FACTOR_BLOCK, group_w), f32), dma(blocks)],
        moved=6 * MIB,
    )(split, g_parts, so_far, come, after)


def square_device(activations, cotangent, sampled_rows, block_owner):
    dp_count = lax.axis_size("dp")
    samples = sampled_rows.shape[0]

    def swap(block, bit, axis="dp"):
        count = lax.axis_size(axis)
        return lax.ppermute(block, axis, [(i, i ^ bit) for i in range(count)])

    def travel(block, even, odd):
        return lax.ppermute(block, "dp", [(i, i ^ (odd if i % 2 else even)) for i in range(dp_count)])

    theirs, own_theirs, picked = project(
        block_owner, sampled_rows, cotangent, activations, dp_count
    )
    got = swap(theirs, CORE)
    rows = lax.all_to_all(picked, "dp", split_axis=0, concat_axis=0, tiled=True)
    own_got = swap(own_theirs, CORE)

    (far,) = sum_cores("sum_far", (0,), cotangent, activations, got, got)
    far_come = travel(far, NEAR_X, NEAR_Y)
    near, rest, own_sum = sum_cores("sum_near", (1, 2, 3), cotangent, activations, got, own_got, far)
    near_come = travel(near, NEAR_X, NEAR_Y)

    inverses, own, half = invert(rows, 1.0 / (samples * dp_count))
    beside = swap(inverses, 1, "tensor")
    two_off, three_off = swap(own, 2, "tensor"), swap(own, 3, "tensor")

    hopped = hop(rest, far_come, inverses)
    come_last = travel(hopped, NEAR_Y, NEAR_X)

    other = swap(half, CORE)
    g_parts = invert_group(half, other, near_come, hopped, activations.shape[0] / samples)
    so_far, split = ready(own_sum, near_come, inverses, beside, g_parts)
    owned, done = owned_blocks(block_owner, inverses, beside, two_off, three_off, so_far)
    step = finish(split, g_parts, so_far, come_last, done)
    return step, owned


def solution(mesh):
    def per_device(activations, cotangent, sampled_rows, block_owner):
        block_total = activations.shape[1] // FACTOR_BLOCK
        dp_count, depth = mesh.shape["dp"], mesh.shape["tensor"]
        fits = (
            dp_count == 8
            and depth == 4
            and block_total == dp_count * depth
            and cotangent.shape[1] == FACTOR_BLOCK
            and sampled_rows.shape[0] % 16 == 0
            and activations.shape[0] % 128 == 0
        )
        run = square_device if fits else general_device
        return run(activations, cotangent, sampled_rows, block_owner)

    return jax.shard_map(
        per_device,
        mesh=mesh,
        in_specs=(P("dp", None), P("dp", "tensor"), P("dp"), P()),
        out_specs=(P("dp", "tensor"), P("dp", None, None)),
        check_vma=False,
    )
```

```python
import functools

import jax
import jax.numpy as jnp
from jax import lax
from jax.experimental import pallas as pl
from jax.experimental.pallas import tpu as pltpu
from jax.sharding import PartitionSpec as P

S_DEV = 64
FACTOR_BLOCK = 256
ITERS = 10


DAMPING = 0.05
precise_mode = lax.Precision.HIGHEST
f32 = jnp.float32
bf16 = jnp.bfloat16


def block_rank(block_owner):
    block_total = block_owner.shape[0]
    same_owner = block_owner[:, None] == block_owner[None, :]
    positions = jnp.arange(block_total, dtype=jnp.int32)
    before = positions[None, :] < positions[:, None]
    return jnp.sum((same_owner & before).astype(jnp.int32), axis=1)


def from_partner(block, axis, apart):
    count = lax.axis_size(axis)
    route = []
    for low in range(count):
        high = low | 1 << apart
        if high != low and high < count:
            route += [(low, high), (high, low)]
    return lax.ppermute(block, axis, route)


def newton_inverse(matrix):
    extent = matrix.shape[-1]
    identity = jnp.eye(extent, dtype=jnp.float32)
    row_bound = jnp.max(jnp.sum(jnp.abs(matrix), axis=2), axis=1)
    initial = identity[None, :, :] / row_bound[:, None, None]

    def advance(turn_index, current):
        product = jnp.einsum("nij,njk->nik", matrix, current, precision=precise_mode)
        return jnp.einsum(
            "nij,njk->nik", current, 2.0 * identity[None, :, :] - product, precision=precise_mode
        )

    return lax.fori_loop(0, ITERS, advance, initial)


def owner_grams(received):
    return jnp.einsum("pcsk,pcsl->ckl", received, received, preferred_element_type=jnp.float32)


def general_device(activations, cotangent, sampled_rows, block_owner):
    tok_local = activations.shape[0]
    model_width = activations.shape[1]
    group_w = cotangent.shape[1]
    dp_count = lax.axis_size("dp")
    my_dp = lax.axis_index("dp")
    block_total = model_width // FACTOR_BLOCK
    capacity = max(1, block_total // dp_count)
    row_share = model_width // dp_count
    samples_all = S_DEV * dp_count
    grad_rows = lax.psum_scatter(
        lax.dot_general(
            activations, cotangent, (((0,), (0,)), ((), ())), preferred_element_type=jnp.float32
        ),
        "dp",
        scatter_dimension=0,
        tiled=True,
    )
    picked_acts = jnp.take(activations, sampled_rows, axis=0)
    picked_grads = jnp.take(cotangent, sampled_rows, axis=0)
    g_partial = lax.dot_general(
        picked_grads, picked_grads, (((0,), (0,)), ((), ())), preferred_element_type=jnp.float32
    )
    g_total = lax.psum(g_partial, "dp")
    g_factor = g_total * (tok_local / S_DEV) + DAMPING * jnp.eye(group_w, dtype=jnp.float32)
    slot_of = block_owner * capacity + block_rank(block_owner)
    dest_ids = jnp.arange(dp_count * capacity, dtype=jnp.int32)
    chooser = (slot_of[None, :] == dest_ids[:, None]).astype(jnp.bfloat16)
    row_blocks = picked_acts.reshape(S_DEV, block_total, FACTOR_BLOCK)
    outgoing = lax.dot_general(
        chooser, row_blocks, (((1,), (1,)), ((), ())), preferred_element_type=jnp.float32
    )
    outgoing = outgoing.astype(jnp.bfloat16).reshape(dp_count, capacity, S_DEV, FACTOR_BLOCK)
    gram_slots = owner_grams(
        lax.all_to_all(outgoing, "dp", split_axis=0, concat_axis=0, tiled=True)
    )
    a_factor = (
        gram_slots / samples_all + DAMPING * jnp.eye(FACTOR_BLOCK, dtype=jnp.float32)[None, :, :]
    )
    input_factor_inverse = newton_inverse(a_factor)
    owned_count = jnp.sum((block_owner == my_dp).astype(jnp.int32))
    slot_used = jnp.arange(capacity, dtype=jnp.int32) < owned_count
    owned_out = jnp.where(slot_used[:, None, None], input_factor_inverse, 0.0)
    g_inverse = newton_inverse(g_factor[None, :, :])[0]
    per_dev = max(1, row_share // FACTOR_BLOCK)
    rows_each = min(row_share, FACTOR_BLOCK)
    first_block = my_dp * row_share // FACTOR_BLOCK
    need_ids = first_block + jnp.arange(per_dev, dtype=jnp.int32)
    need_slots = jnp.take(slot_of, need_ids)
    row_offset = my_dp * row_share % FACTOR_BLOCK
    shard_piece = lax.all_gather(owned_out, "dp", axis=0, tiled=True)
    rows_part = lax.dynamic_slice_in_dim(shard_piece, row_offset, rows_each, 1)
    slot_ids = jnp.arange(shard_piece.shape[0], dtype=jnp.int32)
    selector = (need_slots[:, None] == slot_ids[None, :]).astype(jnp.float32)
    inverse_rows = jnp.einsum("jm,mkl->jkl", selector, rows_part, precision=precise_mode)
    grad_right = jnp.dot(
        grad_rows, g_inverse, precision=precise_mode, preferred_element_type=jnp.float32
    )
    if row_share < FACTOR_BLOCK:
        partner = from_partner(grad_right, "dp", 0)
        is_lower = my_dp % 2 == 0
        joined = jnp.where(
            is_lower,
            jnp.concatenate([grad_right, partner], 0),
            jnp.concatenate([partner, grad_right], 0),
        )
        complete_rows = joined[None, :, :]
    else:
        complete_rows = grad_right.reshape(per_dev, FACTOR_BLOCK, group_w)
    natural_step = jnp.einsum("jrk,jkl->jrl", inverse_rows, complete_rows, precision=precise_mode)
    return (natural_step.reshape(row_share, group_w), owned_out)


MIB = 1 << 20
VMEM_MIB = 32
PROJECT_MIB = 64
SUM_MIB = 62
AHEAD = 3
PROJECT_AHEAD = 6
HOP_PARTS = 2
SUM_PARTS = 2
OWNED_FLOPS = 20_000_000_000
ANY = pl.BlockSpec(memory_space=pl.ANY)
VMEM = pl.BlockSpec(memory_space=pltpu.VMEM)
SMEM = pl.BlockSpec(memory_space=pltpu.SMEM)
CORE, NEAR_X, NEAR_Y, FAR = 1, 2, 4, 6


def routes(me):
    first = jnp.where(me % 2 == 0, NEAR_X, NEAR_Y)
    return FAR, first, FAR - first, 0


def shaped(shape, dtype=f32):
    return jax.ShapeDtypeStruct(shape, dtype)


def call(body, name, out_shape, in_specs, out_specs, scratch=(), flops=0, moved=0, mib=VMEM_MIB):
    return pl.pallas_call(
        body,
        out_shape=out_shape,
        in_specs=in_specs,
        out_specs=out_specs,
        scratch_shapes=scratch,
        compiler_params=pltpu.CompilerParams(vmem_limit_bytes=mib * MIB),
        cost_estimate=pl.CostEstimate(flops=flops, bytes_accessed=moved, transcendentals=0),
        name=name,
    )


def start_all(sources, targets, sems, first=0):
    copies = [
        pltpu.make_async_copy(source, target, sems.at[first + i])
        for i, (source, target) in enumerate(zip(sources, targets))
    ]
    for copy in copies:
        copy.start()
    return copies


def fold_rows(rows):
    return rows + rows // 2


def encode(x, into):
    rows = x.shape[0]
    high = x.astype(bf16)
    into[:rows] = high
    base = high.astype(f32)
    left = (x - base) * pl.reciprocal(base, approx=True) * 256.0
    left = jnp.where(jnp.abs(base) < 1e-30, 0.0, jnp.clip(left, -1.0, 1.0))
    digit = jnp.floor(left * 63.5 + 64.0)
    first, second = digit[: rows // 2], digit[rows // 2 :]
    negative = second >= 64.0
    power = jnp.exp2(jnp.where(negative, second - 96.0, second - 32.0))
    packed = (first + 128.0) * power
    into[rows:] = jnp.where(negative, -packed, packed).astype(bf16)


def decode(ref):
    rows = ref.shape[0] * 2 // 3
    packed = ref[rows:].astype(f32)
    size = jnp.abs(packed)
    power = jnp.floor(jnp.log2(size) + 1e-3)
    first = jnp.floor(size * jnp.exp2(7.0 - power) + 0.5) - 128.0
    second = power + jnp.where(packed < 0.0, 89.0, 25.0)
    digit = jnp.concatenate([first, second], axis=0)
    base = ref[:rows].astype(f32)
    return base + base * ((digit - 63.5) * (1.0 / (63.5 * 256.0)))


def project_body(
    owner, rows_ref, cot_ref, act_ref, theirs, own_theirs, out_ref,
    held, cot, rows, left, grads, picks, slots, sems, out_sems, small_sems, pick_sems,
):
    count, tokens, share = held.shape
    group_w = cot.shape[1]
    samples = rows.shape[1]
    per_tile = share // FACTOR_BLOCK
    me = lax.axis_index("dp")
    z = lax.axis_index("tensor")
    half = count // 2
    tiles = [me ^ m ^ CORE for m in routes(me ^ CORE)] + [me ^ m for m in routes(me)]
    targets = [theirs.at[i] for i in range(half - 1)] + [own_theirs.at[0]]

    small = start_all([cot_ref, rows_ref], [cot, rows], small_sems)
    starts = [pl.multiple_of(t * share, share) for t in tiles]
    loads = [
        pltpu.make_async_copy(act_ref.at[:, pl.ds(start, share)], held.at[i], sems.at[i])
        for i, start in enumerate(starts)
    ]
    for load in loads[:PROJECT_AHEAD]:
        load.start()

    for d in range(count):
        slots[0, d] = 0
        slots[1, d] = 0
    for b in range(owner.shape[0]):
        holder = owner[b]
        rank = slots[0, holder]
        slots[0, holder] = rank + 1
        slots[1, holder] = jnp.where(rank == z, b, slots[1, holder])

    for copy in small:
        copy.wait()
    left[:group_w] = cot[...].astype(f32).T.astype(bf16)
    places = lax.broadcasted_iota(jnp.int32, (tokens, samples), 0)
    left[group_w:] = (places == rows[...]).astype(f32).T.astype(bf16)

    blocks = count * per_tile
    stores = []

    def keep(block, values):
        for k in range(2):
            picks[2 * block + k] = values[k * samples // 2 : (k + 1) * samples // 2].astype(bf16)

    def pass_on(half_block, many, dest, place, n):
        return start_all([picks.at[pl.ds(half_block, many)]], [out_ref.at[dest, pl.ds(place, many)]], pick_sems, n)

    keep(blocks, jnp.dot(left[group_w:], cot[...], preferred_element_type=f32))
    for d in range(count):
        stores += pass_on(2 * blocks + d % 2, 1, d, 6, 3 * d + 2)
    for i in range(count):
        if i % 2 == 0:
            loads[i].wait()
            loads[i + 1].wait()
            for load in loads[i + PROJECT_AHEAD : i + PROJECT_AHEAD + 2]:
                load.start()
        if i < half:
            product = jnp.dot(left[...], held[i], preferred_element_type=f32)
            grads[i] = product[:group_w]
            stores += start_all([grads.at[i]], [targets[i]], out_sems, i)
            picked = product[group_w:]
        else:
            picked = jnp.dot(left[group_w:], held[i], preferred_element_type=f32)
        for j in range(per_tile):
            keep(tiles[i] * per_tile + j, picked[:, j * FACTOR_BLOCK : (j + 1) * FACTOR_BLOCK])
        stores += pass_on(2 * (tiles[i] * per_tile + 2 * (z % 2)), 4, tiles[i], 0, 3 * i)
    for d in range(count):
        stores += pass_on(2 * slots[1, d], 2, d, 4, 3 * d + 1)
    for store in stores:
        store.wait()


def project(block_owner, sampled_rows, cotangent, activations, count):
    samples = sampled_rows.shape[0]
    tokens, group_w = cotangent.shape
    model_width = activations.shape[1]
    share = model_width // count
    one = shaped((1, group_w, share))
    rest = shaped((count // 2 - 1, group_w, share))
    return call(
        project_body,
        "project",
        (rest, one, shaped((count, 7, samples // 2, FACTOR_BLOCK), bf16)),
        [SMEM, ANY, ANY, ANY],
        (ANY,) * 3,
        [
            pltpu.VMEM((count, tokens, share), bf16),
            pltpu.VMEM((tokens, group_w), bf16),
            pltpu.VMEM((1, samples), jnp.int32),
            pltpu.VMEM((group_w + samples, tokens), bf16),
            pltpu.VMEM((count // 2, group_w, share), f32),
            pltpu.VMEM((2 * (model_width // FACTOR_BLOCK + 1), samples // 2, FACTOR_BLOCK), bf16),
            pltpu.SMEM((2, count), jnp.int32),
            pltpu.SemaphoreType.DMA((count,)),
            pltpu.SemaphoreType.DMA((count // 2,)),
            pltpu.SemaphoreType.DMA((2,)),
            pltpu.SemaphoreType.DMA((3 * count,)),
        ],
        flops=2 * tokens * (group_w + samples) * model_width,
        moved=2 * tokens * model_width + 2 * group_w * model_width,
        mib=PROJECT_MIB,
    )(block_owner, sampled_rows[None, :], cotangent, activations)


def sum_body(which, cot_ref, act_ref, got_ref, own_got_ref, *refs):
    count = len(which)
    outs, (cot, held, got, left, wire, plain, sems, got_sems, out_sems) = refs[-9 - count : -9], refs[-9:]
    width = held.shape[2]
    share = got_ref.shape[2]
    parts = share // width
    me = lax.axis_index("dp")
    starts = [pl.multiple_of((me ^ routes(me)[i]) * share, share) for i in which]
    work = [(i, p) for i in range(count) for p in range(parts)]
    first = start_all([cot_ref], [cot], sems)[0]

    def fetch(n):
        i, p = work[n]
        tile = act_ref.at[:, pl.ds(starts[i] + p * width, width)]
        source, at = (own_got_ref, 0) if which[i] == 3 else (got_ref, which[i])
        come = source.at[at, :, pl.ds(p * width, width)]
        return start_all([tile], [held.at[n]], sems, 1 + n) + start_all([come], [got.at[n]], got_sems, n)

    loads = [fetch(n) for n in range(min(AHEAD, len(work)))]
    first.wait()
    left[...] = cot[...].astype(f32).T.astype(bf16)
    stores = []
    for n, (i, p) in enumerate(work):
        loads[n][0].wait()
        if n + AHEAD < len(work):
            loads.append(fetch(n + AHEAD))
        product = jnp.dot(left[...], held[n], preferred_element_type=f32)
        loads[n][1].wait()
        if which[i] < 2:
            encode(product + got[n], wire.at[n])
            source = wire.at[n]
        else:
            plain[n] = product + got[n]
            source = plain.at[n]
        stores += start_all([source], [outs[i].at[:, pl.ds(p * width, width)]], out_sems, n)
    for store in stores:
        store.wait()


def hop_body(rest, come, _, out_ref, rest_in, come_in, out, sems, out_sems):
    parts = rest_in.shape[0]
    width = rest_in.shape[2]
    loads, stores = [], []
    for p in range(parts):
        columns = pl.ds(p * width, width)
        loads.append(start_all([rest.at[:, columns], come.at[:, columns]], [rest_in.at[p], come_in.at[p]], sems, 2 * p))
    for p in range(parts):
        for load in loads[p]:
            load.wait()
        encode(rest_in[p] + decode(come_in.at[p]), out.at[p])
        stores += start_all([out.at[p]], [out_ref.at[:, pl.ds(p * width, width)]], out_sems, p)
    for store in stores:
        store.wait()


def two(x):
    high = x.astype(bf16)
    return high, (x - high.astype(f32)).astype(bf16)


def newton_step(lows, currents, last):
    def dot(a, b):
        return jnp.dot(a, b, preferred_element_type=f32)

    parts = [two(low) for low in lows]
    next_lows, next_currents = [], []
    if not last:
        for low, (high_part, low_part) in zip(lows, parts):
            mixed = dot(high_part, low_part)
            next_lows.append(2.0 * low - (dot(high_part, high_part) + (mixed + mixed.T)))
    for current, (high_part, low_part) in zip(currents, parts):
        high, rest = two(current)
        product = dot(
            jnp.concatenate([high, rest, high], axis=1),
            jnp.concatenate([high_part, high_part, low_part], axis=0),
        )
        next_currents.append(2.0 * current - product)
    return next_lows, next_currents


def places(extent):
    return (
        lax.broadcasted_iota(jnp.int32, (extent, extent), 0),
        lax.broadcasted_iota(jnp.int32, (extent, extent), 1),
    )


FOLD_ROWS = 16


def fold(matrix, into):
    half = matrix.shape[0] // 2
    row, column = places(half)
    low = matrix[half:, half:]
    both = jnp.where(row <= column, matrix[:half, :half], low)
    coded = fold_rows(half)
    encode(jnp.concatenate([both, matrix[:half, half:]], axis=1), into.at[:coded])
    left = jnp.sum(jnp.where(row == column, low, 0.0), axis=0, keepdims=True)
    line = lax.broadcasted_iota(jnp.int32, (FOLD_ROWS, 2 * half), 0)
    diagonal = jnp.zeros((FOLD_ROWS, 2 * half), f32)
    for part in range(3):
        high = left.astype(bf16).astype(f32)
        diagonal = jnp.where(line == part, jnp.concatenate([high, high], axis=1), diagonal)
        left = left - high
    into[coded:] = diagonal.astype(bf16)


def unfold(packed):
    half = packed.shape[1] // 2
    coded = fold_rows(half)
    row, column = places(half)
    values = decode(packed.at[:coded])
    diagonal = jnp.sum(packed[coded:].astype(f32), axis=0, keepdims=True)[:, :half]
    both, corner = values[:, :half], values[:, half:]
    turned = both.T
    top = jnp.where(row <= column, both, turned)
    low = jnp.where(row == column, diagonal, jnp.where(row > column, both, turned))
    return jnp.concatenate(
        [jnp.concatenate([top, corner], axis=1), jnp.concatenate([corner.T, low], axis=1)], axis=0
    )


def inverses_of(samples, scale):
    row, column = places(FACTOR_BLOCK)
    eye = (row == column).astype(f32)
    lows, currents = [], []
    for rows in samples:
        gram = lax.dot_general(
            rows, rows, (((0,), (0,)), ((), ())), preferred_element_type=f32
        )
        matrix = gram * scale + DAMPING * eye
        bound = jnp.max(jnp.sum(jnp.abs(matrix), axis=1, keepdims=True), axis=0, keepdims=True)
        inverse_bound = 1.0 / bound
        low = matrix * inverse_bound
        lows.append(low)
        currents.append((2.0 * eye - low) * inverse_bound)
    lows = newton_step(lows, [], False)[0]
    for turn in range(1, ITERS):
        lows, currents = newton_step(lows, currents, turn == ITERS - 1)
    return currents


def invert_body(scale, rows_ref, all_ref, own_ref, cot_ref, rows, sems):
    load, copy = start_all([rows_ref.at[:, pl.ds(0, 6)], rows_ref.at[:, 6]], [rows, cot_ref], sems)
    load.wait()
    first, second, own = inverses_of(
        [rows[:, 2 * m : 2 * m + 2].reshape(-1, FACTOR_BLOCK) for m in range(3)], scale
    )
    fold(first, all_ref.at[0])
    fold(second, all_ref.at[1])
    fold(own, all_ref.at[2])
    own_ref[...] = all_ref[2]
    copy.wait()


def group_body(scale, half, other, _, __, out_ref):
    rows = jnp.concatenate([half[...].reshape(-1, FACTOR_BLOCK), other[...].reshape(-1, FACTOR_BLOCK)], axis=0)
    parts = two(inverses_of([rows], scale)[0].T)
    out_ref[...] = jnp.concatenate(parts, axis=0)


def ready_body(own, near, here, beside, _, sum_ref, split):
    odd = lax.axis_index("tensor") % 2
    for k, held in enumerate((here, beside)):
        for p in range(2):
            high, low = two(unfold(held.at[p]))
            at = 2 * (odd if k == 0 else 1 - odd) + p
            split[0, at] = high
            split[1, at] = low
    sum_ref[...] = own[...] + decode(near)


def owned_body(owner, here, beside, two_off, three_off, _, out_ref, done_ref):
    z = lax.axis_index("tensor")
    me = lax.axis_index("dp")
    count = jnp.int32(0)
    for b in range(owner.shape[0]):
        count = count + jnp.where(owner[b] == me, 1, 0)
    for k, held in enumerate((here.at[2], beside.at[2], two_off, three_off)):
        slot = z ^ k
        out_ref[slot] = jnp.where(slot < count, unfold(held), 0.0)
    done_ref[...] = jnp.zeros(done_ref.shape, f32)


def finish_body(split, left, so_far, come, _, step_out, step, out_sems):
    width = FACTOR_BLOCK

    def dot(a, c, dims):
        return lax.dot_general(a, c, (dims, ((), ())), preferred_element_type=f32)

    sum_high, sum_low = two(so_far[...] + decode(come))
    both = dot(left[...], sum_high, ((1,), (0,)))
    right_high, right_low = two(both[:width] + (both[width:] + dot(left[:width], sum_low, ((1,), (0,)))))
    stores = []
    for b in range(split.shape[1]):
        part = slice(b * width, (b + 1) * width)
        both = dot(split[:, b].reshape(2 * width, width), right_high[:, part], ((1,), (1,)))
        step[b] = both[:width] + (both[width:] + dot(split[0, b], right_low[:, part], ((1,), (1,))))
        stores += start_all([step.at[b]], [step_out.at[part, :]], out_sems, b)
    for store in stores:
        store.wait()


def dma(count):
    return pltpu.SemaphoreType.DMA((count,))


def sum_cores(name, which, cotangent, activations, got, own_got, *after):
    tokens, group_w = cotangent.shape
    share = got.shape[2]
    wired = (fold_rows(group_w), share)
    steps, width = len(which) * SUM_PARTS, share // SUM_PARTS
    return call(
        functools.partial(sum_body, which),
        name,
        tuple(shaped(wired, bf16) if i < 2 else shaped((group_w, share)) for i in which),
        [ANY] * (4 + len(after)),
        (ANY,) * len(which),
        [
            pltpu.VMEM(cotangent.shape, bf16),
            pltpu.VMEM((steps, tokens, width), bf16),
            pltpu.VMEM((steps, group_w, width), f32),
            pltpu.VMEM((group_w, tokens), bf16),
            pltpu.VMEM((steps, wired[0], width), bf16),
            pltpu.VMEM((steps, group_w, width), f32),
            dma(1 + steps),
            dma(steps),
            dma(steps),
        ],
        moved=4 * MIB * len(which),
        mib=SUM_MIB,
    )(cotangent, activations, got, own_got, *after)


def invert(rows, scale):
    count, _, samples, _ = rows.shape
    packed = shaped((fold_rows(FACTOR_BLOCK // 2) + FOLD_ROWS, FACTOR_BLOCK), bf16)
    return call(
        functools.partial(invert_body, scale),
        "invert_blocks",
        (shaped((3, *packed.shape), bf16), packed, shaped((count, samples, FACTOR_BLOCK), bf16)),
        [ANY],
        (VMEM, VMEM, ANY),
        [pltpu.VMEM((count, 6, samples, FACTOR_BLOCK), bf16), dma(2)],
        flops=2 * 3 * 4 * 18 * FACTOR_BLOCK**3,
        moved=2 * MIB,
    )(rows)


def invert_group(half, other, after, and_after, scale):
    return call(
        functools.partial(group_body, scale),
        "invert_group",
        shaped((2 * FACTOR_BLOCK, FACTOR_BLOCK), bf16),
        [VMEM, VMEM, ANY, ANY],
        VMEM,
    )(half, other, after, and_after)


def hop(rest, come, after):
    group_w, share = rest.shape
    wired = come.shape
    width = share // HOP_PARTS
    return call(
        hop_body,
        "hop",
        shaped(wired, bf16),
        [ANY] * 3,
        ANY,
        [pltpu.VMEM((HOP_PARTS, group_w, width), f32)]
        + [pltpu.VMEM((HOP_PARTS, wired[0], width), bf16)] * 2
        + [dma(2 * HOP_PARTS), dma(HOP_PARTS)],
    )(rest, come, after)


def ready(own_sum, near, inverses, beside, after):
    square = (4, FACTOR_BLOCK, FACTOR_BLOCK)
    return call(
        ready_body,
        "ready",
        (shaped(own_sum.shape), shaped((2, *square), bf16)),
        [VMEM] * 4 + [ANY],
        (VMEM,) * 2,
    )(own_sum, near, inverses, beside, after)


def owned_blocks(block_owner, inverses, beside, two_off, three_off, after):
    return call(
        owned_body,
        "owned",
        (shaped((4, FACTOR_BLOCK, FACTOR_BLOCK)), shaped((8, 128))),
        [SMEM] + [VMEM] * 4 + [ANY],
        (VMEM,) * 2,
        flops=OWNED_FLOPS,
    )(block_owner, inverses, beside, two_off, three_off, after)


def finish(split, g_parts, so_far, come, after):
    group_w, share = so_far.shape
    blocks = share // FACTOR_BLOCK
    return call(
        finish_body,
        "finish",
        shaped((share, group_w)),
        [VMEM] * 4 + [ANY],
        ANY,
        [pltpu.VMEM((blocks, FACTOR_BLOCK, group_w), f32), dma(blocks)],
        moved=6 * MIB,
    )(split, g_parts, so_far, come, after)


def square_device(activations, cotangent, sampled_rows, block_owner):
    dp_count = lax.axis_size("dp")
    samples = sampled_rows.shape[0]

    def swap(block, bit, axis="dp"):
        count = lax.axis_size(axis)
        return lax.ppermute(block, axis, [(i, i ^ bit) for i in range(count)])

    def travel(block, even, odd):
        return lax.ppermute(block, "dp", [(i, i ^ (odd if i % 2 else even)) for i in range(dp_count)])

    theirs, own_theirs, picked = project(
        block_owner, sampled_rows, cotangent, activations, dp_count
    )
    got = swap(theirs, CORE)
    rows = lax.all_to_all(picked, "dp", split_axis=0, concat_axis=0, tiled=True)
    own_got = swap(own_theirs, CORE)

    (far,) = sum_cores("sum_far", (0,), cotangent, activations, got, got)
    far_come = travel(far, NEAR_X, NEAR_Y)
    near, rest, own_sum = sum_cores("sum_near", (1, 2, 3), cotangent, activations, got, own_got, far)
    near_come = travel(near, NEAR_X, NEAR_Y)

    inverses, own, half = invert(rows, 1.0 / (samples * dp_count))
    beside = swap(inverses, 1, "tensor")
    two_off, three_off = swap(own, 2, "tensor"), swap(own, 3, "tensor")

    hopped = hop(rest, far_come, inverses)
    come_last = travel(hopped, NEAR_Y, NEAR_X)

    other = swap(half, CORE)
    g_parts = invert_group(half, other, near_come, hopped, activations.shape[0] / samples)
    so_far, split = ready(own_sum, near_come, inverses, beside, g_parts)
    owned, done = owned_blocks(block_owner, inverses, beside, two_off, three_off, so_far)
    step = finish(split, g_parts, so_far, come_last, done)
    return step, owned


def solution(mesh):
    def per_device(activations, cotangent, sampled_rows, block_owner):
        block_total = activations.shape[1] // FACTOR_BLOCK
        dp_count, depth = mesh.shape["dp"], mesh.shape["tensor"]
        fits = (
            dp_count == 8
            and depth == 4
            and block_total == dp_count * depth
            and cotangent.shape[1] == FACTOR_BLOCK
            and sampled_rows.shape[0] % 16 == 0
            and activations.shape[0] % 128 == 0
        )
        run = square_device if fits else general_device
        return run(activations, cotangent, sampled_rows, block_owner)

    return jax.shard_map(
        per_device,
        mesh=mesh,
        in_specs=(P("dp", None), P("dp", "tensor"), P("dp"), P()),
        out_specs=(P("dp", "tensor"), P("dp", None, None)),
        check_vma=False,
    )
```

```python
import functools

import jax
import jax.numpy as jnp
from jax import lax
from jax.experimental import pallas as pl
from jax.experimental.pallas import tpu as pltpu
from jax.sharding import PartitionSpec as P

S_DEV = 64
FACTOR_BLOCK = 256
ITERS = 10


DAMPING = 0.05
precise_mode = lax.Precision.HIGHEST
f32 = jnp.float32
bf16 = jnp.bfloat16


def block_rank(block_owner):
    block_total = block_owner.shape[0]
    same_owner = block_owner[:, None] == block_owner[None, :]
    positions = jnp.arange(block_total, dtype=jnp.int32)
    before = positions[None, :] < positions[:, None]
    return jnp.sum((same_owner & before).astype(jnp.int32), axis=1)


def from_partner(block, axis, apart):
    count = lax.axis_size(axis)
    route = []
    for low in range(count):
        high = low | 1 << apart
        if high != low and high < count:
            route += [(low, high), (high, low)]
    return lax.ppermute(block, axis, route)


def newton_inverse(matrix):
    extent = matrix.shape[-1]
    identity = jnp.eye(extent, dtype=jnp.float32)
    row_bound = jnp.max(jnp.sum(jnp.abs(matrix), axis=2), axis=1)
    initial = identity[None, :, :] / row_bound[:, None, None]

    def advance(turn_index, current):
        product = jnp.einsum("nij,njk->nik", matrix, current, precision=precise_mode)
        return jnp.einsum(
            "nij,njk->nik", current, 2.0 * identity[None, :, :] - product, precision=precise_mode
        )

    return lax.fori_loop(0, ITERS, advance, initial)


def owner_grams(received):
    return jnp.einsum("pcsk,pcsl->ckl", received, received, preferred_element_type=jnp.float32)


def general_device(activations, cotangent, sampled_rows, block_owner):
    tok_local = activations.shape[0]
    model_width = activations.shape[1]
    group_w = cotangent.shape[1]
    dp_count = lax.axis_size("dp")
    my_dp = lax.axis_index("dp")
    block_total = model_width // FACTOR_BLOCK
    capacity = max(1, block_total // dp_count)
    row_share = model_width // dp_count
    samples_all = S_DEV * dp_count
    grad_rows = lax.psum_scatter(
        lax.dot_general(
            activations, cotangent, (((0,), (0,)), ((), ())), preferred_element_type=jnp.float32
        ),
        "dp",
        scatter_dimension=0,
        tiled=True,
    )
    picked_acts = jnp.take(activations, sampled_rows, axis=0)
    picked_grads = jnp.take(cotangent, sampled_rows, axis=0)
    g_partial = lax.dot_general(
        picked_grads, picked_grads, (((0,), (0,)), ((), ())), preferred_element_type=jnp.float32
    )
    g_total = lax.psum(g_partial, "dp")
    g_factor = g_total * (tok_local / S_DEV) + DAMPING * jnp.eye(group_w, dtype=jnp.float32)
    slot_of = block_owner * capacity + block_rank(block_owner)
    dest_ids = jnp.arange(dp_count * capacity, dtype=jnp.int32)
    chooser = (slot_of[None, :] == dest_ids[:, None]).astype(jnp.bfloat16)
    row_blocks = picked_acts.reshape(S_DEV, block_total, FACTOR_BLOCK)
    outgoing = lax.dot_general(
        chooser, row_blocks, (((1,), (1,)), ((), ())), preferred_element_type=jnp.float32
    )
    outgoing = outgoing.astype(jnp.bfloat16).reshape(dp_count, capacity, S_DEV, FACTOR_BLOCK)
    gram_slots = owner_grams(
        lax.all_to_all(outgoing, "dp", split_axis=0, concat_axis=0, tiled=True)
    )
    a_factor = (
        gram_slots / samples_all + DAMPING * jnp.eye(FACTOR_BLOCK, dtype=jnp.float32)[None, :, :]
    )
    input_factor_inverse = newton_inverse(a_factor)
    owned_count = jnp.sum((block_owner == my_dp).astype(jnp.int32))
    slot_used = jnp.arange(capacity, dtype=jnp.int32) < owned_count
    owned_out = jnp.where(slot_used[:, None, None], input_factor_inverse, 0.0)
    g_inverse = newton_inverse(g_factor[None, :, :])[0]
    per_dev = max(1, row_share // FACTOR_BLOCK)
    rows_each = min(row_share, FACTOR_BLOCK)
    first_block = my_dp * row_share // FACTOR_BLOCK
    need_ids = first_block + jnp.arange(per_dev, dtype=jnp.int32)
    need_slots = jnp.take(slot_of, need_ids)
    row_offset = my_dp * row_share % FACTOR_BLOCK
    shard_piece = lax.all_gather(owned_out, "dp", axis=0, tiled=True)
    rows_part = lax.dynamic_slice_in_dim(shard_piece, row_offset, rows_each, 1)
    slot_ids = jnp.arange(shard_piece.shape[0], dtype=jnp.int32)
    selector = (need_slots[:, None] == slot_ids[None, :]).astype(jnp.float32)
    inverse_rows = jnp.einsum("jm,mkl->jkl", selector, rows_part, precision=precise_mode)
    grad_right = jnp.dot(
        grad_rows, g_inverse, precision=precise_mode, preferred_element_type=jnp.float32
    )
    if row_share < FACTOR_BLOCK:
        partner = from_partner(grad_right, "dp", 0)
        is_lower = my_dp % 2 == 0
        joined = jnp.where(
            is_lower,
            jnp.concatenate([grad_right, partner], 0),
            jnp.concatenate([partner, grad_right], 0),
        )
        complete_rows = joined[None, :, :]
    else:
        complete_rows = grad_right.reshape(per_dev, FACTOR_BLOCK, group_w)
    natural_step = jnp.einsum("jrk,jkl->jrl", inverse_rows, complete_rows, precision=precise_mode)
    return (natural_step.reshape(row_share, group_w), owned_out)


MIB = 1 << 20
VMEM_MIB = 32
PROJECT_MIB = 64
SUM_MIB = 62
AHEAD = 3
PROJECT_AHEAD = 6
HOP_PARTS = 1
SUM_PARTS = 2
OWNED_FLOPS = 20_000_000_000
ANY = pl.BlockSpec(memory_space=pl.ANY)
VMEM = pl.BlockSpec(memory_space=pltpu.VMEM)
SMEM = pl.BlockSpec(memory_space=pltpu.SMEM)
CORE, NEAR_X, NEAR_Y, FAR = 1, 2, 4, 6


def routes(me):
    first = jnp.where(me % 2 == 0, NEAR_X, NEAR_Y)
    return FAR, first, FAR - first, 0


def shaped(shape, dtype=f32):
    return jax.ShapeDtypeStruct(shape, dtype)


def call(body, name, out_shape, in_specs, out_specs, scratch=(), flops=0, moved=0, mib=VMEM_MIB):
    return pl.pallas_call(
        body,
        out_shape=out_shape,
        in_specs=in_specs,
        out_specs=out_specs,
        scratch_shapes=scratch,
        compiler_params=pltpu.CompilerParams(vmem_limit_bytes=mib * MIB),
        cost_estimate=pl.CostEstimate(flops=flops, bytes_accessed=moved, transcendentals=0),
        name=name,
    )


def start_all(sources, targets, sems, first=0):
    copies = [
        pltpu.make_async_copy(source, target, sems.at[first + i])
        for i, (source, target) in enumerate(zip(sources, targets))
    ]
    for copy in copies:
        copy.start()
    return copies


def fold_rows(rows):
    return rows + rows // 2


def encode(x, into):
    rows = x.shape[0]
    high = x.astype(bf16)
    into[:rows] = high
    base = high.astype(f32)
    left = (x - base) * pl.reciprocal(base, approx=True) * 256.0
    left = jnp.where(jnp.abs(base) < 1e-35, 0.0, jnp.clip(left, -1.0, 1.0))
    digit = jnp.floor(left * 63.5 + 64.0)
    first, second = digit[: rows // 2], digit[rows // 2 :]
    negative = second >= 64.0
    power = jnp.exp2(jnp.where(negative, second - 96.0, second - 32.0))
    packed = (first + 128.0) * power
    into[rows:] = jnp.where(negative, -packed, packed).astype(bf16)


def decode(ref):
    rows = ref.shape[0] * 2 // 3
    packed = ref[rows:].astype(f32)
    size = jnp.abs(packed)
    power = jnp.floor(jnp.log2(size) + 1e-3)
    first = jnp.floor(size * jnp.exp2(7.0 - power) + 0.5) - 128.0
    second = power + jnp.where(packed < 0.0, 89.0, 25.0)
    digit = jnp.concatenate([first, second], axis=0)
    base = ref[:rows].astype(f32)
    return base + base * ((digit - 63.5) * (1.0 / (63.5 * 256.0)))


def project_body(
    owner, rows_ref, cot_ref, act_ref, theirs, own_theirs, out_ref,
    held, cot, rows, left, grads, picks, slots, sems, out_sems, small_sems, pick_sems,
):
    count, tokens, share = held.shape
    group_w = cot.shape[1]
    samples = rows.shape[1]
    per_tile = share // FACTOR_BLOCK
    me = lax.axis_index("dp")
    z = lax.axis_index("tensor")
    half = count // 2
    tiles = [me ^ m ^ CORE for m in routes(me ^ CORE)] + [me ^ m for m in routes(me)]
    targets = [theirs.at[i] for i in range(half - 1)] + [own_theirs.at[0]]

    small = start_all([cot_ref, rows_ref], [cot, rows], small_sems)
    starts = [pl.multiple_of(t * share, share) for t in tiles]
    loads = [
        pltpu.make_async_copy(act_ref.at[:, pl.ds(start, share)], held.at[i], sems.at[i])
        for i, start in enumerate(starts)
    ]
    for load in loads[:PROJECT_AHEAD]:
        load.start()

    for d in range(count):
        slots[0, d] = 0
        slots[1, d] = 0
    for b in range(owner.shape[0]):
        holder = owner[b]
        rank = slots[0, holder]
        slots[0, holder] = rank + 1
        slots[1, holder] = jnp.where(rank == z, b, slots[1, holder])

    for copy in small:
        copy.wait()
    left[:group_w] = cot[...].astype(f32).T.astype(bf16)
    places = lax.broadcasted_iota(jnp.int32, (tokens, samples), 0)
    left[group_w:] = (places == rows[...]).astype(f32).T.astype(bf16)

    blocks = count * per_tile
    stores = []

    def keep(block, values):
        for k in range(2):
            picks[2 * block + k] = values[k * samples // 2 : (k + 1) * samples // 2].astype(bf16)

    def pass_on(half_block, many, dest, place, n):
        return start_all([picks.at[pl.ds(half_block, many)]], [out_ref.at[dest, pl.ds(place, many)]], pick_sems, n)

    keep(blocks, jnp.dot(left[group_w:], cot[...], preferred_element_type=f32))
    for d in range(count):
        stores += pass_on(2 * blocks + d % 2, 1, d, 6, 3 * d + 2)
    for i in range(count):
        if i % 2 == 0:
            loads[i].wait()
            loads[i + 1].wait()
            for load in loads[i + PROJECT_AHEAD : i + PROJECT_AHEAD + 2]:
                load.start()
        if i < half:
            product = jnp.dot(left[...], held[i], preferred_element_type=f32)
            grads[i] = product[:group_w]
            stores += start_all([grads.at[i]], [targets[i]], out_sems, i)
            picked = product[group_w:]
        else:
            picked = jnp.dot(left[group_w:], held[i], preferred_element_type=f32)
        for j in range(per_tile):
            keep(tiles[i] * per_tile + j, picked[:, j * FACTOR_BLOCK : (j + 1) * FACTOR_BLOCK])
        stores += pass_on(2 * (tiles[i] * per_tile + 2 * (z % 2)), 4, tiles[i], 0, 3 * i)
    for d in range(count):
        stores += pass_on(2 * slots[1, d], 2, d, 4, 3 * d + 1)
    for store in stores:
        store.wait()


def project(block_owner, sampled_rows, cotangent, activations, count):
    samples = sampled_rows.shape[0]
    tokens, group_w = cotangent.shape
    model_width = activations.shape[1]
    share = model_width // count
    one = shaped((1, group_w, share))
    rest = shaped((count // 2 - 1, group_w, share))
    return call(
        project_body,
        "project",
        (rest, one, shaped((count, 7, samples // 2, FACTOR_BLOCK), bf16)),
        [SMEM, ANY, ANY, ANY],
        (ANY,) * 3,
        [
            pltpu.VMEM((count, tokens, share), bf16),
            pltpu.VMEM((tokens, group_w), bf16),
            pltpu.VMEM((1, samples), jnp.int32),
            pltpu.VMEM((group_w + samples, tokens), bf16),
            pltpu.VMEM((count // 2, group_w, share), f32),
            pltpu.VMEM((2 * (model_width // FACTOR_BLOCK + 1), samples // 2, FACTOR_BLOCK), bf16),
            pltpu.SMEM((2, count), jnp.int32),
            pltpu.SemaphoreType.DMA((count,)),
            pltpu.SemaphoreType.DMA((count // 2,)),
            pltpu.SemaphoreType.DMA((2,)),
            pltpu.SemaphoreType.DMA((3 * count,)),
        ],
        flops=2 * tokens * (group_w + samples) * model_width,
        moved=2 * tokens * model_width + 2 * group_w * model_width,
        mib=PROJECT_MIB,
    )(block_owner, sampled_rows[None, :], cotangent, activations)


def sum_body(which, cot_ref, act_ref, got_ref, own_got_ref, *refs):
    count = len(which)
    outs, (cot, held, got, left, wire, plain, sems, got_sems, out_sems) = refs[-9 - count : -9], refs[-9:]
    width = held.shape[2]
    share = got_ref.shape[2]
    parts = share // width
    me = lax.axis_index("dp")
    starts = [pl.multiple_of((me ^ routes(me)[i]) * share, share) for i in which]
    work = [(i, p) for i in range(count) for p in range(parts)]
    first = start_all([cot_ref], [cot], sems)[0]

    def fetch(n):
        i, p = work[n]
        tile = act_ref.at[:, pl.ds(starts[i] + p * width, width)]
        source, at = (own_got_ref, 0) if which[i] == 3 else (got_ref, which[i])
        come = source.at[at, :, pl.ds(p * width, width)]
        return start_all([tile], [held.at[n]], sems, 1 + n) + start_all([come], [got.at[n]], got_sems, n)

    loads = [fetch(n) for n in range(min(AHEAD, len(work)))]
    first.wait()
    left[...] = cot[...].astype(f32).T.astype(bf16)
    stores = []
    for n, (i, p) in enumerate(work):
        loads[n][0].wait()
        if n + AHEAD < len(work):
            loads.append(fetch(n + AHEAD))
        product = jnp.dot(left[...], held[n], preferred_element_type=f32)
        loads[n][1].wait()
        if which[i] < 2:
            encode(product + got[n], wire.at[n])
            source = wire.at[n]
        else:
            plain[n] = product + got[n]
            source = plain.at[n]
        stores += start_all([source], [outs[i].at[:, pl.ds(p * width, width)]], out_sems, n)
    for store in stores:
        store.wait()


def hop_body(rest, come, _, out_ref, rest_in, come_in, out, sems, out_sems):
    parts = rest_in.shape[0]
    width = rest_in.shape[2]
    loads, stores = [], []
    for p in range(parts):
        columns = pl.ds(p * width, width)
        loads.append(start_all([rest.at[:, columns], come.at[:, columns]], [rest_in.at[p], come_in.at[p]], sems, 2 * p))
    for p in range(parts):
        for load in loads[p]:
            load.wait()
        encode(rest_in[p] + decode(come_in.at[p]), out.at[p])
        stores += start_all([out.at[p]], [out_ref.at[:, pl.ds(p * width, width)]], out_sems, p)
    for store in stores:
        store.wait()


def two(x):
    high = x.astype(bf16)
    return high, (x - high.astype(f32)).astype(bf16)


def newton_step(lows, currents, last):
    def dot(a, b):
        return jnp.dot(a, b, preferred_element_type=f32)

    parts = [two(low) for low in lows]
    next_lows, next_currents = [], []
    if not last:
        for low, (high_part, low_part) in zip(lows, parts):
            mixed = dot(high_part, low_part)
            next_lows.append(2.0 * low - (dot(high_part, high_part) + (mixed + mixed.T)))
    for current, (high_part, low_part) in zip(currents, parts):
        high, rest = two(current)
        product = dot(
            jnp.concatenate([high, rest, high], axis=1),
            jnp.concatenate([high_part, high_part, low_part], axis=0),
        )
        next_currents.append(2.0 * current - product)
    return next_lows, next_currents


def places(extent):
    return (
        lax.broadcasted_iota(jnp.int32, (extent, extent), 0),
        lax.broadcasted_iota(jnp.int32, (extent, extent), 1),
    )


FOLD_ROWS = 16


def fold(matrix, into):
    half = matrix.shape[0] // 2
    row, column = places(half)
    low = matrix[half:, half:]
    both = jnp.where(row <= column, matrix[:half, :half], low)
    coded = fold_rows(half)
    encode(jnp.concatenate([both, matrix[:half, half:]], axis=1), into.at[:coded])
    left = jnp.sum(jnp.where(row == column, low, 0.0), axis=0, keepdims=True)
    line = lax.broadcasted_iota(jnp.int32, (FOLD_ROWS, 2 * half), 0)
    diagonal = jnp.zeros((FOLD_ROWS, 2 * half), f32)
    for part in range(3):
        high = left.astype(bf16).astype(f32)
        diagonal = jnp.where(line == part, jnp.concatenate([high, high], axis=1), diagonal)
        left = left - high
    into[coded:] = diagonal.astype(bf16)


def unfold(packed):
    half = packed.shape[1] // 2
    coded = fold_rows(half)
    row, column = places(half)
    values = decode(packed.at[:coded])
    diagonal = jnp.sum(packed[coded:].astype(f32), axis=0, keepdims=True)[:, :half]
    both, corner = values[:, :half], values[:, half:]
    turned = both.T
    top = jnp.where(row <= column, both, turned)
    low = jnp.where(row == column, diagonal, jnp.where(row > column, both, turned))
    return jnp.concatenate(
        [jnp.concatenate([top, corner], axis=1), jnp.concatenate([corner.T, low], axis=1)], axis=0
    )


def inverses_of(samples, scale):
    row, column = places(FACTOR_BLOCK)
    eye = (row == column).astype(f32)
    lows, currents = [], []
    for rows in samples:
        gram = lax.dot_general(
            rows, rows, (((0,), (0,)), ((), ())), preferred_element_type=f32
        )
        matrix = gram * scale + DAMPING * eye
        bound = jnp.max(jnp.sum(jnp.abs(matrix), axis=1, keepdims=True), axis=0, keepdims=True)
        inverse_bound = 1.0 / bound
        low = matrix * inverse_bound
        lows.append(low)
        currents.append((2.0 * eye - low) * inverse_bound)
    lows = newton_step(lows, [], False)[0]
    for turn in range(1, ITERS):
        lows, currents = newton_step(lows, currents, turn == ITERS - 1)
    return currents


def invert_body(scale, rows_ref, all_ref, own_ref, cot_ref, rows, sems):
    load, copy = start_all([rows_ref.at[:, pl.ds(0, 6)], rows_ref.at[:, 6]], [rows, cot_ref], sems)
    load.wait()
    first, second, own = inverses_of(
        [rows[:, 2 * m : 2 * m + 2].reshape(-1, FACTOR_BLOCK) for m in range(3)], scale
    )
    fold(first, all_ref.at[0])
    fold(second, all_ref.at[1])
    fold(own, all_ref.at[2])
    own_ref[...] = all_ref[2]
    copy.wait()


def group_body(scale, half, other, _, __, out_ref):
    rows = jnp.concatenate([half[...].reshape(-1, FACTOR_BLOCK), other[...].reshape(-1, FACTOR_BLOCK)], axis=0)
    parts = two(inverses_of([rows], scale)[0].T)
    out_ref[...] = jnp.concatenate(parts, axis=0)


def ready_body(own, near, here, beside, _, sum_ref, split):
    odd = lax.axis_index("tensor") % 2
    for k, held in enumerate((here, beside)):
        for p in range(2):
            high, low = two(unfold(held.at[p]))
            at = 2 * (odd if k == 0 else 1 - odd) + p
            split[0, at] = high
            split[1, at] = low
    sum_ref[...] = own[...] + decode(near)


def owned_body(owner, here, beside, two_off, three_off, _, out_ref, done_ref):
    z = lax.axis_index("tensor")
    me = lax.axis_index("dp")
    count = jnp.int32(0)
    for b in range(owner.shape[0]):
        count = count + jnp.where(owner[b] == me, 1, 0)
    for k, held in enumerate((here.at[2], beside.at[2], two_off, three_off)):
        slot = z ^ k
        out_ref[slot] = jnp.where(slot < count, unfold(held), 0.0)
    done_ref[...] = jnp.zeros(done_ref.shape, f32)


def finish_body(split, left, so_far, come, _, step_out, step, out_sems):
    width = FACTOR_BLOCK

    def dot(a, c, dims):
        return lax.dot_general(a, c, (dims, ((), ())), preferred_element_type=f32)

    sum_high, sum_low = two(so_far[...] + decode(come))
    both = dot(left[...], sum_high, ((1,), (0,)))
    right_high, right_low = two(both[:width] + (both[width:] + dot(left[:width], sum_low, ((1,), (0,)))))
    stores = []
    for b in range(split.shape[1]):
        part = slice(b * width, (b + 1) * width)
        both = dot(split[:, b].reshape(2 * width, width), right_high[:, part], ((1,), (1,)))
        step[b] = both[:width] + (both[width:] + dot(split[0, b], right_low[:, part], ((1,), (1,))))
        stores += start_all([step.at[b]], [step_out.at[part, :]], out_sems, b)
    for store in stores:
        store.wait()


def dma(count):
    return pltpu.SemaphoreType.DMA((count,))


def sum_cores(name, which, cotangent, activations, got, own_got, *after):
    tokens, group_w = cotangent.shape
    share = got.shape[2]
    wired = (fold_rows(group_w), share)
    steps, width = len(which) * SUM_PARTS, share // SUM_PARTS
    return call(
        functools.partial(sum_body, which),
        name,
        tuple(shaped(wired, bf16) if i < 2 else shaped((group_w, share)) for i in which),
        [ANY] * (4 + len(after)),
        (ANY,) * len(which),
        [
            pltpu.VMEM(cotangent.shape, bf16),
            pltpu.VMEM((steps, tokens, width), bf16),
            pltpu.VMEM((steps, group_w, width), f32),
            pltpu.VMEM((group_w, tokens), bf16),
            pltpu.VMEM((steps, wired[0], width), bf16),
            pltpu.VMEM((steps, group_w, width), f32),
            dma(1 + steps),
            dma(steps),
            dma(steps),
        ],
        moved=4 * MIB * len(which),
        mib=SUM_MIB,
    )(cotangent, activations, got, own_got, *after)


def invert(rows, scale):
    count, _, samples, _ = rows.shape
    packed = shaped((fold_rows(FACTOR_BLOCK // 2) + FOLD_ROWS, FACTOR_BLOCK), bf16)
    return call(
        functools.partial(invert_body, scale),
        "invert_blocks",
        (shaped((3, *packed.shape), bf16), packed, shaped((count, samples, FACTOR_BLOCK), bf16)),
        [ANY],
        (VMEM, VMEM, ANY),
        [pltpu.VMEM((count, 6, samples, FACTOR_BLOCK), bf16), dma(2)],
        flops=2 * 3 * 4 * 18 * FACTOR_BLOCK**3,
        moved=2 * MIB,
    )(rows)


def invert_group(half, other, after, and_after, scale):
    return call(
        functools.partial(group_body, scale),
        "invert_group",
        shaped((2 * FACTOR_BLOCK, FACTOR_BLOCK), bf16),
        [VMEM, VMEM, ANY, ANY],
        VMEM,
    )(half, other, after, and_after)


def hop(rest, come, after):
    group_w, share = rest.shape
    wired = come.shape
    width = share // HOP_PARTS
    return call(
        hop_body,
        "hop",
        shaped(wired, bf16),
        [ANY] * 3,
        ANY,
        [pltpu.VMEM((HOP_PARTS, group_w, width), f32)]
        + [pltpu.VMEM((HOP_PARTS, wired[0], width), bf16)] * 2
        + [dma(2 * HOP_PARTS), dma(HOP_PARTS)],
    )(rest, come, after)


def ready(own_sum, near, inverses, beside, after):
    square = (4, FACTOR_BLOCK, FACTOR_BLOCK)
    return call(
        ready_body,
        "ready",
        (shaped(own_sum.shape), shaped((2, *square), bf16)),
        [VMEM] * 4 + [ANY],
        (VMEM,) * 2,
    )(own_sum, near, inverses, beside, after)


def owned_blocks(block_owner, inverses, beside, two_off, three_off, after):
    return call(
        owned_body,
        "owned",
        (shaped((4, FACTOR_BLOCK, FACTOR_BLOCK)), shaped((8, 128))),
        [SMEM] + [VMEM] * 4 + [ANY],
        (VMEM,) * 2,
        flops=OWNED_FLOPS,
    )(block_owner, inverses, beside, two_off, three_off, after)


def finish(split, g_parts, so_far, come, after):
    group_w, share = so_far.shape
    blocks = share // FACTOR_BLOCK
    return call(
        finish_body,
        "finish",
        shaped((share, group_w)),
        [VMEM] * 4 + [ANY],
        ANY,
        [pltpu.VMEM((blocks, FACTOR_BLOCK, group_w), f32), dma(blocks)],
        moved=6 * MIB,
    )(split, g_parts, so_far, come, after)


def square_device(activations, cotangent, sampled_rows, block_owner):
    dp_count = lax.axis_size("dp")
    samples = sampled_rows.shape[0]

    def swap(block, bit, axis="dp"):
        count = lax.axis_size(axis)
        return lax.ppermute(block, axis, [(i, i ^ bit) for i in range(count)])

    def travel(block, even, odd):
        return lax.ppermute(block, "dp", [(i, i ^ (odd if i % 2 else even)) for i in range(dp_count)])

    theirs, own_theirs, picked = project(
        block_owner, sampled_rows, cotangent, activations, dp_count
    )
    got = swap(theirs, CORE)
    rows = lax.all_to_all(picked, "dp", split_axis=0, concat_axis=0, tiled=True)
    own_got = swap(own_theirs, CORE)

    (far,) = sum_cores("sum_far", (0,), cotangent, activations, got, got)
    far_come = travel(far, NEAR_X, NEAR_Y)
    near, rest, own_sum = sum_cores("sum_near", (1, 2, 3), cotangent, activations, got, own_got, far)
    near_come = travel(near, NEAR_X, NEAR_Y)

    inverses, own, half = invert(rows, 1.0 / (samples * dp_count))
    beside = swap(inverses, 1, "tensor")
    two_off, three_off = swap(own, 2, "tensor"), swap(own, 3, "tensor")

    hopped = hop(rest, far_come, inverses)
    come_last = travel(hopped, NEAR_Y, NEAR_X)

    other = swap(half, CORE)
    g_parts = invert_group(half, other, near_come, hopped, activations.shape[0] / samples)
    so_far, split = ready(own_sum, near_come, inverses, beside, g_parts)
    owned, done = owned_blocks(block_owner, inverses, beside, two_off, three_off, so_far)
    step = finish(split, g_parts, so_far, come_last, done)
    return step, owned


def solution(mesh):
    def per_device(activations, cotangent, sampled_rows, block_owner):
        block_total = activations.shape[1] // FACTOR_BLOCK
        dp_count, depth = mesh.shape["dp"], mesh.shape["tensor"]
        fits = (
            dp_count == 8
            and depth == 4
            and block_total == dp_count * depth
            and cotangent.shape[1] == FACTOR_BLOCK
            and sampled_rows.shape[0] % 16 == 0
            and activations.shape[0] % 128 == 0
        )
        run = square_device if fits else general_device
        return run(activations, cotangent, sampled_rows, block_owner)

    return jax.shard_map(
        per_device,
        mesh=mesh,
        in_specs=(P("dp", None), P("dp", "tensor"), P("dp"), P()),
        out_specs=(P("dp", "tensor"), P("dp", None, None)),
        check_vma=False,
    )
```

```python
import functools

import jax
import jax.numpy as jnp
from jax import lax
from jax.experimental import pallas as pl
from jax.experimental.pallas import tpu as pltpu
from jax.sharding import PartitionSpec as P

S_DEV = 64
FACTOR_BLOCK = 256
ITERS = 10


DAMPING = 0.05
precise_mode = lax.Precision.HIGHEST
f32 = jnp.float32
bf16 = jnp.bfloat16


def block_rank(block_owner):
    block_total = block_owner.shape[0]
    same_owner = block_owner[:, None] == block_owner[None, :]
    positions = jnp.arange(block_total, dtype=jnp.int32)
    before = positions[None, :] < positions[:, None]
    return jnp.sum((same_owner & before).astype(jnp.int32), axis=1)


def from_partner(block, axis, apart):
    count = lax.axis_size(axis)
    route = []
    for low in range(count):
        high = low | 1 << apart
        if high != low and high < count:
            route += [(low, high), (high, low)]
    return lax.ppermute(block, axis, route)


def newton_inverse(matrix):
    extent = matrix.shape[-1]
    identity = jnp.eye(extent, dtype=jnp.float32)
    row_bound = jnp.max(jnp.sum(jnp.abs(matrix), axis=2), axis=1)
    initial = identity[None, :, :] / row_bound[:, None, None]

    def advance(turn_index, current):
        product = jnp.einsum("nij,njk->nik", matrix, current, precision=precise_mode)
        return jnp.einsum(
            "nij,njk->nik", current, 2.0 * identity[None, :, :] - product, precision=precise_mode
        )

    return lax.fori_loop(0, ITERS, advance, initial)


def owner_grams(received):
    return jnp.einsum("pcsk,pcsl->ckl", received, received, preferred_element_type=jnp.float32)


def general_device(activations, cotangent, sampled_rows, block_owner):
    tok_local = activations.shape[0]
    model_width = activations.shape[1]
    group_w = cotangent.shape[1]
    dp_count = lax.axis_size("dp")
    my_dp = lax.axis_index("dp")
    block_total = model_width // FACTOR_BLOCK
    capacity = max(1, block_total // dp_count)
    row_share = model_width // dp_count
    samples_all = S_DEV * dp_count
    grad_rows = lax.psum_scatter(
        lax.dot_general(
            activations, cotangent, (((0,), (0,)), ((), ())), preferred_element_type=jnp.float32
        ),
        "dp",
        scatter_dimension=0,
        tiled=True,
    )
    picked_acts = jnp.take(activations, sampled_rows, axis=0)
    picked_grads = jnp.take(cotangent, sampled_rows, axis=0)
    g_partial = lax.dot_general(
        picked_grads, picked_grads, (((0,), (0,)), ((), ())), preferred_element_type=jnp.float32
    )
    g_total = lax.psum(g_partial, "dp")
    g_factor = g_total * (tok_local / S_DEV) + DAMPING * jnp.eye(group_w, dtype=jnp.float32)
    slot_of = block_owner * capacity + block_rank(block_owner)
    dest_ids = jnp.arange(dp_count * capacity, dtype=jnp.int32)
    chooser = (slot_of[None, :] == dest_ids[:, None]).astype(jnp.bfloat16)
    row_blocks = picked_acts.reshape(S_DEV, block_total, FACTOR_BLOCK)
    outgoing = lax.dot_general(
        chooser, row_blocks, (((1,), (1,)), ((), ())), preferred_element_type=jnp.float32
    )
    outgoing = outgoing.astype(jnp.bfloat16).reshape(dp_count, capacity, S_DEV, FACTOR_BLOCK)
    gram_slots = owner_grams(
        lax.all_to_all(outgoing, "dp", split_axis=0, concat_axis=0, tiled=True)
    )
    a_factor = (
        gram_slots / samples_all + DAMPING * jnp.eye(FACTOR_BLOCK, dtype=jnp.float32)[None, :, :]
    )
    input_factor_inverse = newton_inverse(a_factor)
    owned_count = jnp.sum((block_owner == my_dp).astype(jnp.int32))
    slot_used = jnp.arange(capacity, dtype=jnp.int32) < owned_count
    owned_out = jnp.where(slot_used[:, None, None], input_factor_inverse, 0.0)
    g_inverse = newton_inverse(g_factor[None, :, :])[0]
    per_dev = max(1, row_share // FACTOR_BLOCK)
    rows_each = min(row_share, FACTOR_BLOCK)
    first_block = my_dp * row_share // FACTOR_BLOCK
    need_ids = first_block + jnp.arange(per_dev, dtype=jnp.int32)
    need_slots = jnp.take(slot_of, need_ids)
    row_offset = my_dp * row_share % FACTOR_BLOCK
    shard_piece = lax.all_gather(owned_out, "dp", axis=0, tiled=True)
    rows_part = lax.dynamic_slice_in_dim(shard_piece, row_offset, rows_each, 1)
    slot_ids = jnp.arange(shard_piece.shape[0], dtype=jnp.int32)
    selector = (need_slots[:, None] == slot_ids[None, :]).astype(jnp.float32)
    inverse_rows = jnp.einsum("jm,mkl->jkl", selector, rows_part, precision=precise_mode)
    grad_right = jnp.dot(
        grad_rows, g_inverse, precision=precise_mode, preferred_element_type=jnp.float32
    )
    if row_share < FACTOR_BLOCK:
        partner = from_partner(grad_right, "dp", 0)
        is_lower = my_dp % 2 == 0
        joined = jnp.where(
            is_lower,
            jnp.concatenate([grad_right, partner], 0),
            jnp.concatenate([partner, grad_right], 0),
        )
        complete_rows = joined[None, :, :]
    else:
        complete_rows = grad_right.reshape(per_dev, FACTOR_BLOCK, group_w)
    natural_step = jnp.einsum("jrk,jkl->jrl", inverse_rows, complete_rows, precision=precise_mode)
    return (natural_step.reshape(row_share, group_w), owned_out)


MIB = 1 << 20
VMEM_MIB = 24
PROJECT_MIB = 64
SUM_MIB = 62
AHEAD = 3
PROJECT_AHEAD = 6
HOP_PARTS = 1
SUM_PARTS = 2
OWNED_FLOPS = 20_000_000_000
ANY = pl.BlockSpec(memory_space=pl.ANY)
VMEM = pl.BlockSpec(memory_space=pltpu.VMEM)
SMEM = pl.BlockSpec(memory_space=pltpu.SMEM)
CORE, NEAR_X, NEAR_Y, FAR = 1, 2, 4, 6


def routes(me):
    first = jnp.where(me % 2 == 0, NEAR_X, NEAR_Y)
    return FAR, first, FAR - first, 0


def shaped(shape, dtype=f32):
    return jax.ShapeDtypeStruct(shape, dtype)


def call(body, name, out_shape, in_specs, out_specs, scratch=(), flops=0, moved=0, mib=VMEM_MIB):
    return pl.pallas_call(
        body,
        out_shape=out_shape,
        in_specs=in_specs,
        out_specs=out_specs,
        scratch_shapes=scratch,
        compiler_params=pltpu.CompilerParams(vmem_limit_bytes=mib * MIB),
        cost_estimate=pl.CostEstimate(flops=flops, bytes_accessed=moved, transcendentals=0),
        name=name,
    )


def start_all(sources, targets, sems, first=0):
    copies = [
        pltpu.make_async_copy(source, target, sems.at[first + i])
        for i, (source, target) in enumerate(zip(sources, targets))
    ]
    for copy in copies:
        copy.start()
    return copies


def fold_rows(rows):
    return rows + rows // 2


def encode(x, into):
    rows = x.shape[0]
    high = x.astype(bf16)
    into[:rows] = high
    base = high.astype(f32)
    left = (x - base) * pl.reciprocal(base, approx=True) * 256.0
    left = jnp.where(jnp.abs(base) < 1e-35, 0.0, jnp.clip(left, -1.0, 1.0))
    digit = jnp.floor(left * 63.5 + 64.0)
    first, second = digit[: rows // 2], digit[rows // 2 :]
    negative = second >= 64.0
    power = jnp.exp2(jnp.where(negative, second - 96.0, second - 32.0))
    packed = (first + 128.0) * power
    into[rows:] = jnp.where(negative, -packed, packed).astype(bf16)


def decode(ref):
    rows = ref.shape[0] * 2 // 3
    packed = ref[rows:].astype(f32)
    size = jnp.abs(packed)
    power = jnp.floor(jnp.log2(size) + 1e-3)
    first = jnp.floor(size * jnp.exp2(7.0 - power) + 0.5) - 128.0
    second = power + jnp.where(packed < 0.0, 89.0, 25.0)
    digit = jnp.concatenate([first, second], axis=0)
    base = ref[:rows].astype(f32)
    return base + base * ((digit - 63.5) * (1.0 / (63.5 * 256.0)))


def project_body(
    owner, rows_ref, cot_ref, act_ref, theirs, own_theirs, out_ref,
    held, cot, rows, left, grads, picks, slots, sems, out_sems, small_sems, pick_sems,
):
    count, tokens, share = held.shape
    group_w = cot.shape[1]
    samples = rows.shape[1]
    per_tile = share // FACTOR_BLOCK
    me = lax.axis_index("dp")
    z = lax.axis_index("tensor")
    half = count // 2
    tiles = [me ^ m ^ CORE for m in routes(me ^ CORE)] + [me ^ m for m in routes(me)]
    targets = [theirs.at[i] for i in range(half - 1)] + [own_theirs.at[0]]

    small = start_all([cot_ref, rows_ref], [cot, rows], small_sems)
    starts = [pl.multiple_of(t * share, share) for t in tiles]
    loads = [
        pltpu.make_async_copy(act_ref.at[:, pl.ds(start, share)], held.at[i], sems.at[i])
        for i, start in enumerate(starts)
    ]
    for load in loads[:PROJECT_AHEAD]:
        load.start()

    for d in range(count):
        slots[0, d] = 0
        slots[1, d] = 0
    for b in range(owner.shape[0]):
        holder = owner[b]
        rank = slots[0, holder]
        slots[0, holder] = rank + 1
        slots[1, holder] = jnp.where(rank == z, b, slots[1, holder])

    for copy in small:
        copy.wait()
    left[:group_w] = cot[...].astype(f32).T.astype(bf16)
    places = lax.broadcasted_iota(jnp.int32, (tokens, samples), 0)
    left[group_w:] = (places == rows[...]).astype(f32).T.astype(bf16)

    blocks = count * per_tile
    stores = []

    def keep(block, values):
        for k in range(2):
            picks[2 * block + k] = values[k * samples // 2 : (k + 1) * samples // 2].astype(bf16)

    def pass_on(half_block, many, dest, place, n):
        return start_all([picks.at[pl.ds(half_block, many)]], [out_ref.at[dest, pl.ds(place, many)]], pick_sems, n)

    keep(blocks, jnp.dot(left[group_w:], cot[...], preferred_element_type=f32))
    for d in range(count):
        stores += pass_on(2 * blocks + d % 2, 1, d, 6, 3 * d + 2)
    for i in range(count):
        if i % 2 == 0:
            loads[i].wait()
            loads[i + 1].wait()
            for load in loads[i + PROJECT_AHEAD : i + PROJECT_AHEAD + 2]:
                load.start()
        if i < half:
            product = jnp.dot(left[...], held[i], preferred_element_type=f32)
            grads[i] = product[:group_w]
            stores += start_all([grads.at[i]], [targets[i]], out_sems, i)
            picked = product[group_w:]
        else:
            picked = jnp.dot(left[group_w:], held[i], preferred_element_type=f32)
        for j in range(per_tile):
            keep(tiles[i] * per_tile + j, picked[:, j * FACTOR_BLOCK : (j + 1) * FACTOR_BLOCK])
        stores += pass_on(2 * (tiles[i] * per_tile + 2 * (z % 2)), 4, tiles[i], 0, 3 * i)
    for d in range(count):
        stores += pass_on(2 * slots[1, d], 2, d, 4, 3 * d + 1)
    for store in stores:
        store.wait()


def project(block_owner, sampled_rows, cotangent, activations, count):
    samples = sampled_rows.shape[0]
    tokens, group_w = cotangent.shape
    model_width = activations.shape[1]
    share = model_width // count
    one = shaped((1, group_w, share))
    rest = shaped((count // 2 - 1, group_w, share))
    return call(
        project_body,
        "project",
        (rest, one, shaped((count, 7, samples // 2, FACTOR_BLOCK), bf16)),
        [SMEM, ANY, ANY, ANY],
        (ANY,) * 3,
        [
            pltpu.VMEM((count, tokens, share), bf16),
            pltpu.VMEM((tokens, group_w), bf16),
            pltpu.VMEM((1, samples), jnp.int32),
            pltpu.VMEM((group_w + samples, tokens), bf16),
            pltpu.VMEM((count // 2, group_w, share), f32),
            pltpu.VMEM((2 * (model_width // FACTOR_BLOCK + 1), samples // 2, FACTOR_BLOCK), bf16),
            pltpu.SMEM((2, count), jnp.int32),
            pltpu.SemaphoreType.DMA((count,)),
            pltpu.SemaphoreType.DMA((count // 2,)),
            pltpu.SemaphoreType.DMA((2,)),
            pltpu.SemaphoreType.DMA((3 * count,)),
        ],
        flops=2 * tokens * (group_w + samples) * model_width,
        moved=2 * tokens * model_width + 2 * group_w * model_width,
        mib=PROJECT_MIB,
    )(block_owner, sampled_rows[None, :], cotangent, activations)


def sum_body(which, cot_ref, act_ref, got_ref, own_got_ref, *refs):
    count = len(which)
    outs, (cot, held, got, left, wire, plain, sems, got_sems, out_sems) = refs[-9 - count : -9], refs[-9:]
    width = held.shape[2]
    share = got_ref.shape[2]
    parts = share // width
    me = lax.axis_index("dp")
    starts = [pl.multiple_of((me ^ routes(me)[i]) * share, share) for i in which]
    work = [(i, p) for i in range(count) for p in range(parts)]
    first = start_all([cot_ref], [cot], sems)[0]

    def fetch(n):
        i, p = work[n]
        tile = act_ref.at[:, pl.ds(starts[i] + p * width, width)]
        source, at = (own_got_ref, 0) if which[i] == 3 else (got_ref, which[i])
        come = source.at[at, :, pl.ds(p * width, width)]
        return start_all([tile], [held.at[n]], sems, 1 + n) + start_all([come], [got.at[n]], got_sems, n)

    loads = [fetch(n) for n in range(min(AHEAD, len(work)))]
    first.wait()
    left[...] = cot[...].astype(f32).T.astype(bf16)
    stores = []
    for n, (i, p) in enumerate(work):
        loads[n][0].wait()
        if n + AHEAD < len(work):
            loads.append(fetch(n + AHEAD))
        product = jnp.dot(left[...], held[n], preferred_element_type=f32)
        loads[n][1].wait()
        if which[i] < 2:
            encode(product + got[n], wire.at[n])
            source = wire.at[n]
        else:
            plain[n] = product + got[n]
            source = plain.at[n]
        stores += start_all([source], [outs[i].at[:, pl.ds(p * width, width)]], out_sems, n)
    for store in stores:
        store.wait()


def hop_body(rest, come, _, out_ref, rest_in, come_in, out, sems, out_sems):
    parts = rest_in.shape[0]
    width = rest_in.shape[2]
    loads, stores = [], []
    for p in range(parts):
        columns = pl.ds(p * width, width)
        loads.append(start_all([rest.at[:, columns], come.at[:, columns]], [rest_in.at[p], come_in.at[p]], sems, 2 * p))
    for p in range(parts):
        for load in loads[p]:
            load.wait()
        encode(rest_in[p] + decode(come_in.at[p]), out.at[p])
        stores += start_all([out.at[p]], [out_ref.at[:, pl.ds(p * width, width)]], out_sems, p)
    for store in stores:
        store.wait()


def two(x):
    high = x.astype(bf16)
    return high, (x - high.astype(f32)).astype(bf16)


def newton_step(lows, currents, last):
    def dot(a, b):
        return jnp.dot(a, b, preferred_element_type=f32)

    parts = [two(low) for low in lows]
    next_lows, next_currents = [], []
    if not last:
        for low, (high_part, low_part) in zip(lows, parts):
            mixed = dot(high_part, low_part)
            next_lows.append(2.0 * low - (dot(high_part, high_part) + (mixed + mixed.T)))
    for current, (high_part, low_part) in zip(currents, parts):
        high, rest = two(current)
        product = dot(
            jnp.concatenate([high, rest, high], axis=1),
            jnp.concatenate([high_part, high_part, low_part], axis=0),
        )
        next_currents.append(2.0 * current - product)
    return next_lows, next_currents


def places(extent):
    return (
        lax.broadcasted_iota(jnp.int32, (extent, extent), 0),
        lax.broadcasted_iota(jnp.int32, (extent, extent), 1),
    )


FOLD_ROWS = 16


def fold(matrix, into):
    half = matrix.shape[0] // 2
    row, column = places(half)
    low = matrix[half:, half:]
    both = jnp.where(row <= column, matrix[:half, :half], low)
    coded = fold_rows(half)
    encode(jnp.concatenate([both, matrix[:half, half:]], axis=1), into.at[:coded])
    left = jnp.sum(jnp.where(row == column, low, 0.0), axis=0, keepdims=True)
    line = lax.broadcasted_iota(jnp.int32, (FOLD_ROWS, 2 * half), 0)
    diagonal = jnp.zeros((FOLD_ROWS, 2 * half), f32)
    for part in range(3):
        high = left.astype(bf16).astype(f32)
        diagonal = jnp.where(line == part, jnp.concatenate([high, high], axis=1), diagonal)
        left = left - high
    into[coded:] = diagonal.astype(bf16)


def unfold(packed):
    half = packed.shape[1] // 2
    coded = fold_rows(half)
    row, column = places(half)
    values = decode(packed.at[:coded])
    diagonal = jnp.sum(packed[coded:].astype(f32), axis=0, keepdims=True)[:, :half]
    both, corner = values[:, :half], values[:, half:]
    turned = both.T
    top = jnp.where(row <= column, both, turned)
    low = jnp.where(row == column, diagonal, jnp.where(row > column, both, turned))
    return jnp.concatenate(
        [jnp.concatenate([top, corner], axis=1), jnp.concatenate([corner.T, low], axis=1)], axis=0
    )


def inverses_of(samples, scale):
    row, column = places(FACTOR_BLOCK)
    eye = (row == column).astype(f32)
    lows, currents = [], []
    for rows in samples:
        gram = lax.dot_general(
            rows, rows, (((0,), (0,)), ((), ())), preferred_element_type=f32
        )
        matrix = gram * scale + DAMPING * eye
        bound = jnp.max(jnp.sum(jnp.abs(matrix), axis=1, keepdims=True), axis=0, keepdims=True)
        inverse_bound = 1.0 / bound
        low = matrix * inverse_bound
        lows.append(low)
        currents.append((2.0 * eye - low) * inverse_bound)
    lows = newton_step(lows, [], False)[0]
    for turn in range(1, ITERS):
        lows, currents = newton_step(lows, currents, turn == ITERS - 1)
    return currents


def invert_body(scale, rows_ref, all_ref, own_ref, cot_ref, rows, sems):
    load, copy = start_all([rows_ref.at[:, pl.ds(0, 6)], rows_ref.at[:, 6]], [rows, cot_ref], sems)
    load.wait()
    first, second, own = inverses_of(
        [rows[:, 2 * m : 2 * m + 2].reshape(-1, FACTOR_BLOCK) for m in range(3)], scale
    )
    fold(first, all_ref.at[0])
    fold(second, all_ref.at[1])
    fold(own, all_ref.at[2])
    own_ref[...] = all_ref[2]
    copy.wait()


def group_body(scale, half, other, _, __, out_ref):
    rows = jnp.concatenate([half[...].reshape(-1, FACTOR_BLOCK), other[...].reshape(-1, FACTOR_BLOCK)], axis=0)
    parts = two(inverses_of([rows], scale)[0].T)
    out_ref[...] = jnp.concatenate(parts, axis=0)


def ready_body(own, near, here, beside, _, sum_ref, split):
    odd = lax.axis_index("tensor") % 2
    for k, held in enumerate((here, beside)):
        for p in range(2):
            high, low = two(unfold(held.at[p]))
            at = 2 * (odd if k == 0 else 1 - odd) + p
            split[0, at] = high
            split[1, at] = low
    sum_ref[...] = own[...] + decode(near)


def owned_body(owner, here, beside, two_off, three_off, _, out_ref, done_ref):
    z = lax.axis_index("tensor")
    me = lax.axis_index("dp")
    count = jnp.int32(0)
    for b in range(owner.shape[0]):
        count = count + jnp.where(owner[b] == me, 1, 0)
    for k, held in enumerate((here.at[2], beside.at[2], two_off, three_off)):
        slot = z ^ k
        out_ref[slot] = jnp.where(slot < count, unfold(held), 0.0)
    done_ref[...] = jnp.zeros(done_ref.shape, f32)


def finish_body(split, left, so_far, come, _, step_out, step, out_sems):
    width = FACTOR_BLOCK

    def dot(a, c, dims):
        return lax.dot_general(a, c, (dims, ((), ())), preferred_element_type=f32)

    sum_high, sum_low = two(so_far[...] + decode(come))
    both = dot(left[...], sum_high, ((1,), (0,)))
    right_high, right_low = two(both[:width] + (both[width:] + dot(left[:width], sum_low, ((1,), (0,)))))
    stores = []
    for b in range(split.shape[1]):
        part = slice(b * width, (b + 1) * width)
        both = dot(split[:, b].reshape(2 * width, width), right_high[:, part], ((1,), (1,)))
        step[b] = both[:width] + (both[width:] + dot(split[0, b], right_low[:, part], ((1,), (1,))))
        stores += start_all([step.at[b]], [step_out.at[part, :]], out_sems, b)
    for store in stores:
        store.wait()


def dma(count):
    return pltpu.SemaphoreType.DMA((count,))


def sum_cores(name, which, cotangent, activations, got, own_got, *after):
    tokens, group_w = cotangent.shape
    share = got.shape[2]
    wired = (fold_rows(group_w), share)
    steps, width = len(which) * SUM_PARTS, share // SUM_PARTS
    return call(
        functools.partial(sum_body, which),
        name,
        tuple(shaped(wired, bf16) if i < 2 else shaped((group_w, share)) for i in which),
        [ANY] * (4 + len(after)),
        (ANY,) * len(which),
        [
            pltpu.VMEM(cotangent.shape, bf16),
            pltpu.VMEM((steps, tokens, width), bf16),
            pltpu.VMEM((steps, group_w, width), f32),
            pltpu.VMEM((group_w, tokens), bf16),
            pltpu.VMEM((steps, wired[0], width), bf16),
            pltpu.VMEM((steps, group_w, width), f32),
            dma(1 + steps),
            dma(steps),
            dma(steps),
        ],
        moved=4 * MIB * len(which),
        mib=SUM_MIB,
    )(cotangent, activations, got, own_got, *after)


def invert(rows, scale):
    count, _, samples, _ = rows.shape
    packed = shaped((fold_rows(FACTOR_BLOCK // 2) + FOLD_ROWS, FACTOR_BLOCK), bf16)
    return call(
        functools.partial(invert_body, scale),
        "invert_blocks",
        (shaped((3, *packed.shape), bf16), packed, shaped((count, samples, FACTOR_BLOCK), bf16)),
        [ANY],
        (VMEM, VMEM, ANY),
        [pltpu.VMEM((count, 6, samples, FACTOR_BLOCK), bf16), dma(2)],
        flops=2 * 3 * 4 * 18 * FACTOR_BLOCK**3,
        moved=2 * MIB,
    )(rows)


def invert_group(half, other, after, and_after, scale):
    return call(
        functools.partial(group_body, scale),
        "invert_group",
        shaped((2 * FACTOR_BLOCK, FACTOR_BLOCK), bf16),
        [VMEM, VMEM, ANY, ANY],
        VMEM,
    )(half, other, after, and_after)


def hop(rest, come, after):
    group_w, share = rest.shape
    wired = come.shape
    width = share // HOP_PARTS
    return call(
        hop_body,
        "hop",
        shaped(wired, bf16),
        [ANY] * 3,
        ANY,
        [pltpu.VMEM((HOP_PARTS, group_w, width), f32)]
        + [pltpu.VMEM((HOP_PARTS, wired[0], width), bf16)] * 2
        + [dma(2 * HOP_PARTS), dma(HOP_PARTS)],
    )(rest, come, after)


def ready(own_sum, near, inverses, beside, after):
    square = (4, FACTOR_BLOCK, FACTOR_BLOCK)
    return call(
        ready_body,
        "ready",
        (shaped(own_sum.shape), shaped((2, *square), bf16)),
        [VMEM] * 4 + [ANY],
        (VMEM,) * 2,
    )(own_sum, near, inverses, beside, after)


def owned_blocks(block_owner, inverses, beside, two_off, three_off, after):
    return call(
        owned_body,
        "owned",
        (shaped((4, FACTOR_BLOCK, FACTOR_BLOCK)), shaped((8, 128))),
        [SMEM] + [VMEM] * 4 + [ANY],
        (VMEM,) * 2,
        flops=OWNED_FLOPS,
    )(block_owner, inverses, beside, two_off, three_off, after)


def finish(split, g_parts, so_far, come, after):
    group_w, share = so_far.shape
    blocks = share // FACTOR_BLOCK
    return call(
        finish_body,
        "finish",
        shaped((share, group_w)),
        [VMEM] * 4 + [ANY],
        ANY,
        [pltpu.VMEM((blocks, FACTOR_BLOCK, group_w), f32), dma(blocks)],
        moved=6 * MIB,
    )(split, g_parts, so_far, come, after)


def square_device(activations, cotangent, sampled_rows, block_owner):
    dp_count = lax.axis_size("dp")
    samples = sampled_rows.shape[0]

    def swap(block, bit, axis="dp"):
        count = lax.axis_size(axis)
        return lax.ppermute(block, axis, [(i, i ^ bit) for i in range(count)])

    def travel(block, even, odd):
        return lax.ppermute(block, "dp", [(i, i ^ (odd if i % 2 else even)) for i in range(dp_count)])

    theirs, own_theirs, picked = project(
        block_owner, sampled_rows, cotangent, activations, dp_count
    )
    got = swap(theirs, CORE)
    rows = lax.all_to_all(picked, "dp", split_axis=0, concat_axis=0, tiled=True)
    own_got = swap(own_theirs, CORE)

    (far,) = sum_cores("sum_far", (0,), cotangent, activations, got, got)
    far_come = travel(far, NEAR_X, NEAR_Y)
    near, rest, own_sum = sum_cores("sum_near", (1, 2, 3), cotangent, activations, got, own_got, far)
    near_come = travel(near, NEAR_X, NEAR_Y)

    inverses, own, half = invert(rows, 1.0 / (samples * dp_count))
    beside = swap(inverses, 1, "tensor")
    two_off, three_off = swap(own, 2, "tensor"), swap(own, 3, "tensor")

    hopped = hop(rest, far_come, inverses)
    come_last = travel(hopped, NEAR_Y, NEAR_X)

    other = swap(half, CORE)
    g_parts = invert_group(half, other, near_come, hopped, activations.shape[0] / samples)
    so_far, split = ready(own_sum, near_come, inverses, beside, g_parts)
    owned, done = owned_blocks(block_owner, inverses, beside, two_off, three_off, so_far)
    step = finish(split, g_parts, so_far, come_last, done)
    return step, owned


def solution(mesh):
    def per_device(activations, cotangent, sampled_rows, block_owner):
        block_total = activations.shape[1] // FACTOR_BLOCK
        dp_count, depth = mesh.shape["dp"], mesh.shape["tensor"]
        fits = (
            dp_count == 8
            and depth == 4
            and block_total == dp_count * depth
            and cotangent.shape[1] == FACTOR_BLOCK
            and sampled_rows.shape[0] % 16 == 0
            and activations.shape[0] % 128 == 0
        )
        run = square_device if fits else general_device
        return run(activations, cotangent, sampled_rows, block_owner)

    return jax.shard_map(
        per_device,
        mesh=mesh,
        in_specs=(P("dp", None), P("dp", "tensor"), P("dp"), P()),
        out_specs=(P("dp", "tensor"), P("dp", None, None)),
        check_vma=False,
    )
```
